768 devices in a mesh: wide: 96 (over y, z), narrow: 8 (over x, core).
Axes of the slice: x: 4, y: 8, z: 12, core: 2. Of those that a mesh axis runs over, the one named last changes fastest.
Arguments:
- velocity: float32 [3, 768, 128, 128], P(None, 'wide', 'narrow'), may hold values from -6 to 6
- reaction: float32 [768, 128, 128], P('wide', 'narrow'), may hold values from 1 to 64
Outputs:
- advection: float32 [3, 768, 128, 128], P(None, 'wide', 'narrow')
- pressure: float32 [768, 128, 128], P('wide', 'narrow')
- residual: float32 [768, 128, 128], P('wide', 'narrow')
The draws below stay inside these ranges and needn't reach their ends.
All inputs are finite; a program needn't handle non-finite values.
Results may differ from the reference program's by a relative error of at most 0.00028.
Values sent between devices are 32-bit elements; how exact they have to be, the bound alone decides.
A program may use at most 32 MiB of HBM per device.

```python
import math
import jax
import jax.numpy as jnp
import numpy as np
from jax import lax

ITERS = 3
NXP = 768
NYP = 128
NZP = 128


def level_of(key, extent, shards, smallest, high):
    gain, own = 1.0, jax.random.fold_in(key, 6)
    for dim, parts in shards:
        steps = jnp.exp(jax.random.uniform(jax.random.fold_in(own, dim), (parts,), jnp.float32, smallest / len(shards), high / len(shards)))
        gain = gain * jnp.repeat(steps, extent[dim] // parts).reshape([-1 if axis == dim else 1 for axis in range(len(extent))])
    return gain


def normal_values(rng, dims, width, reach, cuts=(), kind=jnp.bfloat16):
    factor_of = level_of(rng, dims, cuts, -0.22, 0.18) if cuts else 1.0
    result = jax.random.normal(rng, dims, jnp.float32) * width * factor_of
    return jnp.minimum(jnp.maximum(result, -reach), reach).astype(kind)


def setup_inputs(seed: int = 0) -> dict:
    seeds = jax.random.split(jax.random.key(seed), 3)
    return {
        "velocity": normal_values(seeds[0], (3, NXP, NYP, NZP), 1.0, 6.0, ((1, 96), (2, 8)), jnp.float32),
        "reaction": jnp.clip(jnp.exp(math.log(64.0) - 4.158883 * jax.random.uniform(seeds[1], (NXP, NYP, NZP), jnp.float32) ** level_of(seeds[1], (NXP, NYP, NZP), ((0, 96), (1, 8)), -0.2, 0.2)), 1.0, 64.0),
    }


def legendre_pair(order, nodes):
    p_prev = np.ones(nodes.shape)
    p_now = nodes * 1.0
    for k in range(2, order + 1):
        p_next = ((2 * k - 1) * nodes * p_now - (k - 1) * p_prev) / k
        p_prev = p_now
        p_now = p_next
    return p_now, p_prev


def spectral_tables():
    degree = 7
    points = degree + 1
    gll_nodes = np.cos(np.pi * np.arange(points) / degree)
    for sweep in range(100):
        p_now, p_prev = legendre_pair(degree, gll_nodes)
        gll_nodes = gll_nodes - (gll_nodes * p_now - p_prev) / ((degree + 1) * p_now)
    gll_nodes = np.sort(gll_nodes)
    legendre_vals, unused_prev = legendre_pair(degree, gll_nodes)
    gll_weights = 2.0 / (degree * (degree + 1) * legendre_vals ** 2)
    derivative = np.zeros((points, points))
    for row_index in range(points):
        for col_index in range(points):
            if row_index != col_index:
                derivative[row_index, col_index] = legendre_vals[row_index] / (legendre_vals[col_index] * (gll_nodes[row_index] - gll_nodes[col_index]))
    derivative[0, 0] = -degree * (degree + 1) / 4.0
    derivative[-1, -1] = degree * (degree + 1) / 4.0
    gauss_nodes = np.cos(np.pi * (np.arange(12) + 0.75) / 12.5)
    for sweep in range(100):
        p_now, p_prev = legendre_pair(12, gauss_nodes)
        slope = 12 * (gauss_nodes * p_now - p_prev) / (gauss_nodes * gauss_nodes - 1.0)
        gauss_nodes = gauss_nodes - p_now / slope
    gauss_nodes = np.sort(gauss_nodes)
    p_now, p_prev = legendre_pair(12, gauss_nodes)
    slope = 12 * (gauss_nodes * p_now - p_prev) / (gauss_nodes * gauss_nodes - 1.0)
    gauss_weights = 2.0 / ((1.0 - gauss_nodes ** 2) * slope ** 2)
    interpolate = np.ones((12, points))
    for col_index in range(points):
        for other in range(points):
            if other != col_index:
                interpolate[:, col_index] *= (gauss_nodes - gll_nodes[other]) / (gll_nodes[col_index] - gll_nodes[other])
    return gll_weights, derivative, gauss_weights, interpolate


def element_apply(values, mat_x, mat_y, mat_z, counts):
    highest = lax.Precision.HIGHEST
    comps = values.shape[0]
    count_x, count_y, count_z = counts
    blocks = values.reshape(comps, count_x, values.shape[1] // count_x, count_y, values.shape[2] // count_y, count_z, values.shape[3] // count_z)
    blocks = jnp.einsum("naibjgk,pk->naibjgp", blocks, mat_z, precision=highest)
    blocks = jnp.einsum("naibjgk,pj->naibpgk", blocks, mat_y, precision=highest)
    blocks = jnp.einsum("naibjgk,pi->napbjgk", blocks, mat_x, precision=highest)
    return blocks.reshape(comps, count_x * mat_x.shape[0], count_y * mat_y.shape[0], count_z * mat_z.shape[0])


def pair_sum(padded, axis_pos, length):
    self_vals = lax.slice_in_dim(padded, 1, length + 1, axis=axis_pos)
    left_vals = lax.slice_in_dim(padded, 0, length, axis=axis_pos)
    right_vals = lax.slice_in_dim(padded, 2, length + 2, axis=axis_pos)
    dims_shape = [1, 1, 1, 1]
    dims_shape[axis_pos] = length
    position = jnp.arange(length).reshape(dims_shape) % 8
    zero_val = jnp.zeros((), padded.dtype)
    return self_vals + jnp.where(position == 0, left_vals, zero_val) + jnp.where(position == 7, right_vals, zero_val)


def gather_scatter(values):
    summed = values
    for axis_pos in (1, 2, 3):
        pads = [(0, 0), (0, 0), (0, 0), (0, 0)]
        pads[axis_pos] = (1, 1)
        summed = pair_sum(jnp.pad(summed, pads), axis_pos, values.shape[axis_pos])
    return summed


def edge_factor(length):
    position = np.arange(length)
    local_pos = position % 8
    shared = ((local_pos == 0) & (position > 0)) | ((local_pos == 7) & (position < length - 1))
    return np.where(shared, 0.5, 1.0)


def reference(velocity, reaction):
    gll_weights, derivative, gauss_weights, interpolate = spectral_tables()
    dtype_now = velocity.dtype
    width_x, width_y, width_z = reaction.shape
    count_x, count_y, count_z = width_x // 8, width_y // 8, width_z // 8
    interp_t = jnp.asarray(interpolate, dtype=dtype_now)
    back_t = jnp.asarray(interpolate.T, dtype=dtype_now)
    gradint = jnp.asarray(interpolate @ derivative, dtype=dtype_now)
    deriv_t = jnp.asarray(derivative, dtype=dtype_now)
    deriv_back = jnp.asarray(derivative.T, dtype=dtype_now)
    identity = jnp.asarray(np.eye(8), dtype=dtype_now)
    mass_local = jnp.asarray(np.tile(gll_weights, count_x)[:, None, None] * np.tile(gll_weights, count_y)[None, :, None] * np.tile(gll_weights, count_z)[None, None, :], dtype=dtype_now)[None]
    inverse_mult = jnp.asarray(edge_factor(width_x)[:, None, None] * edge_factor(width_y)[None, :, None] * edge_factor(width_z)[None, None, :], dtype=dtype_now)[None]
    block_count = math.gcd(count_x, 32)
    per_block = count_x // block_count
    fine_weights = jnp.asarray(np.tile(gauss_weights, per_block)[:, None, None] * np.tile(gauss_weights, count_y)[None, :, None] * np.tile(gauss_weights, count_z)[None, None, :], dtype=dtype_now)[None]
    counts_block = (per_block, count_y, count_z)

    def convect(piece):
        fine_vel = element_apply(piece, interp_t, interp_t, interp_t, counts_block)
        grad_fx = element_apply(piece, gradint, interp_t, interp_t, counts_block)
        grad_fy = element_apply(piece, interp_t, gradint, interp_t, counts_block)
        grad_fz = element_apply(piece, interp_t, interp_t, gradint, counts_block)
        product = fine_vel[0:1] * grad_fx + fine_vel[1:2] * grad_fy + fine_vel[2:3] * grad_fz
        return element_apply(product * fine_weights, back_t, back_t, back_t, counts_block)

    split = velocity.reshape(3, block_count, per_block * 8, width_y, width_z).transpose(1, 0, 2, 3, 4)
    weak_conv = lax.map(convect, split).transpose(1, 0, 2, 3, 4).reshape(3, width_x, width_y, width_z)
    advection = gather_scatter(weak_conv) / gather_scatter(mass_local)
    counts_all = (count_x, count_y, count_z)
    forward = velocity - 0.05 * advection
    divergence = element_apply(forward[0:1], deriv_t, identity, identity, counts_all)
    divergence = divergence + element_apply(forward[1:2], identity, deriv_t, identity, counts_all)
    divergence = divergence + element_apply(forward[2:3], identity, identity, deriv_t, counts_all)
    rhs = -gather_scatter(mass_local * divergence)

    def operator(values):
        grad_x = element_apply(values, deriv_t, identity, identity, counts_all)
        grad_y = element_apply(values, identity, deriv_t, identity, counts_all)
        grad_z = element_apply(values, identity, identity, deriv_t, counts_all)
        local_sum = element_apply(mass_local * grad_x, deriv_back, identity, identity, counts_all)
        local_sum = local_sum + element_apply(mass_local * grad_y, identity, deriv_back, identity, counts_all)
        local_sum = local_sum + element_apply(mass_local * grad_z, identity, identity, deriv_back, counts_all)
        return gather_scatter(local_sum + mass_local * reaction[None] * values)

    def inner(first, second):
        return jnp.sum(first * second * inverse_mult)

    pressure = jnp.zeros_like(rhs)
    residual = rhs
    direction = rhs
    rr_now = inner(residual, residual)
    for iteration in range(ITERS):
        image_dir = operator(direction)
        step_size = rr_now / inner(direction, image_dir)
        pressure = pressure + step_size * direction
        residual = residual - step_size * image_dir
        rr_next = inner(residual, residual)
        direction = residual + (rr_next / rr_now) * direction
        rr_now = rr_next
    return advection, pressure[0], residual[0]
```

```python
import functools

import jax
import jax.numpy as jnp
import ml_dtypes
import numpy as np
from jax import lax
from jax.experimental import pallas as pl
from jax.experimental.pallas import tpu as pltpu
from jax.sharding import PartitionSpec as P

MESH = pl.DeviceIdType.MESH
SHIFT = 4.0
SIDES = ((1, 0), (-1, 0), (0, 1), (0, -1), (1, 1), (1, -1), (-1, 1), (-1, -1))


def legendre_pair(order, nodes):
    p_prev = np.ones(nodes.shape)
    p_now = nodes * 1.0
    for k in range(2, order + 1):
        p_next = ((2 * k - 1) * nodes * p_now - (k - 1) * p_prev) / k
        p_prev = p_now
        p_now = p_next
    return (p_now, p_prev)


def spectral_tables():
    degree = 7
    points = degree + 1
    gll_nodes = np.cos(np.pi * np.arange(points) / degree)
    for sweep in range(100):
        p_now, p_prev = legendre_pair(degree, gll_nodes)
        gll_nodes = gll_nodes - (gll_nodes * p_now - p_prev) / ((degree + 1) * p_now)
    gll_nodes = np.sort(gll_nodes)
    legendre_vals, unused_prev = legendre_pair(degree, gll_nodes)
    gll_weights = 2.0 / (degree * (degree + 1) * legendre_vals**2)
    derivative = np.zeros((points, points))
    for row_index in range(points):
        for col_index in range(points):
            if row_index != col_index:
                derivative[row_index, col_index] = legendre_vals[row_index] / (
                    legendre_vals[col_index] * (gll_nodes[row_index] - gll_nodes[col_index])
                )
    derivative[0, 0] = -degree * (degree + 1) / 4.0
    derivative[-1, -1] = degree * (degree + 1) / 4.0
    gauss_nodes = np.cos(np.pi * (np.arange(12) + 0.75) / 12.5)
    for sweep in range(100):
        p_now, p_prev = legendre_pair(12, gauss_nodes)
        slope = 12 * (gauss_nodes * p_now - p_prev) / (gauss_nodes * gauss_nodes - 1.0)
        gauss_nodes = gauss_nodes - p_now / slope
    gauss_nodes = np.sort(gauss_nodes)
    p_now, p_prev = legendre_pair(12, gauss_nodes)
    slope = 12 * (gauss_nodes * p_now - p_prev) / (gauss_nodes * gauss_nodes - 1.0)
    gauss_weights = 2.0 / ((1.0 - gauss_nodes**2) * slope**2)
    interpolate = np.ones((12, points))
    for col_index in range(points):
        for other in range(points):
            if other != col_index:
                interpolate[:, col_index] *= (gauss_nodes - gll_nodes[other]) / (
                    gll_nodes[col_index] - gll_nodes[other]
                )
    return (gll_weights, derivative, gauss_weights, interpolate)


def halves(matrix):
    high = matrix.astype(ml_dtypes.bfloat16)
    low = (matrix - high.astype(np.float64)).astype(ml_dtypes.bfloat16)
    return high, low


def left_factor(matrix):
    high, low = halves(matrix)
    return np.concatenate([high, high, low], axis=1)


def right_factor(matrix):
    high, low = halves(matrix)
    return np.concatenate([high, high, low], axis=0)


def tables_for(len_z):
    weights, deriv, fine_weights, interp = spectral_tables()
    els_z = len_z // 8
    gradint = interp @ deriv
    stiff = deriv.T @ np.diag(weights) @ deriv
    eye2, eye_z = np.eye(2), np.eye(els_z)

    def shared(count):
        total = np.eye(8 * count)
        for k in range(count - 1):
            total[8 * k + 7, 8 * k + 8] = total[8 * k + 8, 8 * k + 7] = 1.0
        return total

    sum_y, sum_z = shared(2), shared(els_z)
    w_x, w_y, w_z = weights, np.tile(weights, 2), np.tile(weights, els_z)
    w_y2, w_z2 = sum_y @ w_y, sum_z @ w_z

    fine_z = np.zeros((len_z, 2 * 16 * els_z))
    back_z = np.zeros((16 * els_z, len_z))
    for e in range(els_z):
        fine_z[8 * e : 8 * e + 8, 16 * e : 16 * e + 12] = interp.T
        first = 16 * els_z + 16 * e
        fine_z[8 * e : 8 * e + 8, first : first + 12] = gradint.T
        back_z[16 * e : 16 * e + 12, 8 * e : 8 * e + 8] = fine_weights[:, None] * interp
    back_z = back_z @ sum_z
    fine_xy = np.concatenate(
        [np.kron(interp, interp), np.kron(gradint, interp), np.kron(interp, gradint)], axis=0
    )
    back = interp.T * fine_weights[None, :]
    back_xy = np.kron(back, back)

    op_xy = np.kron(stiff, np.diag(w_y2)) + np.kron(np.diag(w_x), sum_y @ np.kron(eye2, stiff))
    op_z = np.kron(eye_z, stiff).T @ sum_z
    weak = np.diag(weights) @ deriv
    div_xy = np.concatenate(
        [np.kron(weak, np.diag(w_y)), np.kron(np.diag(w_x), np.kron(eye2, weak))], axis=1
    )
    div_xy2 = np.concatenate(
        [np.kron(weak, np.diag(w_y2)), np.kron(np.diag(w_x), sum_y @ np.kron(eye2, weak))], axis=1
    )
    div_z = np.kron(eye_z, weak).T
    div_z2 = div_z @ sum_z

    w_xy, w_xy2 = np.kron(w_x, w_y), np.kron(w_x, w_y2)
    half_y = 1.0 / (sum_y @ np.ones(16))
    half_z = 1.0 / (sum_z @ np.ones(len_z))
    ones_x, ones_z = np.ones(8), np.ones(len_z)
    plain = np.stack(
        [
            np.outer(w_xy, w_z),
            np.outer(w_xy, ones_z),
            np.outer(w_xy2, ones_z),
            1.0 / np.outer(w_xy2, w_z2),
            np.outer(np.kron(ones_x, half_y), half_z),
            np.outer(np.ones(128), w_z),
            np.outer(np.ones(128), w_z2),
        ]
    ).astype(np.float32)
    from_right = np.concatenate(
        [right_factor(back_z), right_factor(op_z), right_factor(div_z), right_factor(div_z2)], axis=0
    )
    from_left = np.concatenate(
        [left_factor(op_xy), left_factor(div_xy), left_factor(div_xy2)], axis=1
    )
    return (
        right_factor(fine_z),
        left_factor(fine_xy),
        from_right,
        from_left,
        left_factor(back_xy),
        plain,
    )


def split(value):
    high = value.astype(jnp.bfloat16)
    low = (value - high.astype(jnp.float32)).astype(jnp.bfloat16)
    return high, low


def stacked(value):
    high, low = split(value)
    return jnp.concatenate([high, low, high], axis=0)


def joined(value):
    high, low = split(value)
    return jnp.concatenate([high, low, high], axis=1)


def mul(first, second):
    return jnp.dot(first, second, preferred_element_type=jnp.float32)


def kernel(
    sizes,
    vel_hbm,
    rea_hbm,
    fine_z_hbm,
    fine_xy_hbm,
    right_hbm,
    left_hbm,
    back_xy_hbm,
    plain_hbm,
    adv_ref,
    pres_ref,
    resid_ref,
    vel_ref,
    rea_ref,
    fine_z_ref,
    fine_xy_ref,
    right_ref,
    left_ref,
    back_xy_ref,
    plain_ref,
    load_sem,
    adv_q,
    ops_q,
    sx3,
    sy3,
    sc3,
    rx3,
    ry3,
    rc3,
    sx1,
    sy1,
    sc1,
    rx1,
    ry1,
    rc1,
    part,
    got,
    send_sem,
    recv_sem,
    tree_send,
    tree_recv,
):
    pairs = (
        (vel_hbm, vel_ref),
        (fine_z_hbm, fine_z_ref),
        (fine_xy_hbm, fine_xy_ref),
        (right_hbm, right_ref),
        (back_xy_hbm, back_xy_ref),
        (plain_hbm, plain_ref),
        (rea_hbm, rea_ref),
        (left_hbm, left_ref),
    )
    loads = [pltpu.make_async_copy(a, b, load_sem.at[k]) for k, (a, b) in enumerate(pairs)]
    for load in loads:
        load.start()

    count_x, count_y, low_count = sizes
    high_count = count_x // low_count
    me_x, me_y = lax.axis_index("wide"), lax.axis_index("narrow")
    me_low, me_high = lax.rem(me_x, low_count), me_x // low_count

    def at_side(side):
        return (
            lax.rem(me_x + (side[0] + count_x), count_x),
            lax.rem(me_y + (side[1] + count_y), count_y),
        )

    stages = (
        [(me_x, lax.rem(me_y + d, count_y)) for d in range(1, count_y)],
        [
            (me_high * low_count + lax.rem(me_low + d, low_count), me_y)
            for d in range(1, low_count)
        ],
        [
            (lax.rem(me_high + d, high_count) * low_count + me_low, me_y)
            for d in range(1, high_count)
        ],
    )
    partners = [at_side(side) for side in SIDES] + [who for stage in stages for who in stage]

    barrier = pltpu.get_barrier_semaphore()
    for who in partners:
        pl.semaphore_signal(barrier, inc=1, device_id=who, device_id_type=MESH)

    for load in loads[:3]:
        load.wait()
    parts = []
    for c in range(3):
        for e in range(2):
            parts.append(vel_ref[c, :, 8 * e : 8 * e + 8, :].reshape(64, 128))
    on_z = mul(joined(jnp.concatenate(parts, axis=0)), fine_z_ref[...])
    width = on_z.shape[1] // 2
    products = {}
    for e in range(2):
        fine = []
        for c in range(3):
            first = 64 * (2 * c + e)
            flat = mul(fine_xy_ref[...], stacked(on_z[first : first + 64, :width]))
            steep = mul(fine_xy_ref[:144, :], stacked(on_z[first : first + 64, width:]))
            fine.append((flat[:144], flat[144:288], flat[288:], steep))
        for c in range(3):
            products[c, e] = (
                fine[0][0] * fine[c][1] + fine[1][0] * fine[c][2] + fine[2][0] * fine[c][3]
            )
    for load in loads[3:5]:
        load.wait()
    row8 = lax.broadcasted_iota(jnp.int32, (8, 8, 128), 1)
    back_rows = 3 * width
    for c in range(3):
        both = []
        for e in range(2):
            both.append(stacked(mul(joined(products[c, e]), right_ref[:back_rows, :])))
        weak = mul(back_xy_ref[...], jnp.concatenate(both, axis=1))
        first = weak[:, :128].reshape(8, 8, 128)
        second = weak[:, 128:].reshape(8, 8, 128)
        first, second = (
            first + jnp.where(row8 == 7, pltpu.roll(second, 7, 1), 0.0),
            second + jnp.where(row8 == 0, pltpu.roll(first, 1, 1), 0.0),
        )
        adv_q[c] = jnp.concatenate([first, second], axis=1).reshape(128, 128)

    pl.semaphore_wait(barrier, len(partners))

    has = {1: (me_x > 0, me_y > 0), -1: (me_x < count_x - 1, me_y < count_y - 1)}

    def exchange(q_ref, slots, bufs, index, comps):
        sx, sy, sc, rx, ry, rc = bufs
        for c in range(comps):
            q = q_ref.at[c]
            sx[0, c] = q[112:128, :]
            sx[1, c] = q[0:16, :]
            sy[0, c] = q[pl.ds(15, 8, stride=16), :]
            sy[1, c] = q[pl.ds(0, 8, stride=16), :]
            for k, row in enumerate((127, 112, 15, 0)):
                sc[k, c : c + 1, :] = q[row : row + 1, :]
        copies = []
        for k, side in enumerate(SIDES):
            if k < 2:
                source, target = sx.at[k], rx.at[k]
            elif k < 4:
                source, target = sy.at[k - 2], ry.at[k - 2]
            else:
                source, target = sc.at[k - 4], rc.at[k - 4]
            copies.append(
                pltpu.make_async_remote_copy(
                    src_ref=source,
                    dst_ref=target,
                    send_sem=send_sem.at[index, k],
                    recv_sem=recv_sem.at[index, k],
                    device_id=at_side(side),
                    device_id_type=MESH,
                )
            )
        for copy in copies:
            copy.start()
        return copies

    row_x = lax.broadcasted_iota(jnp.int32, (8, 128), 0)

    def receive(q_ref, bufs, copies, comps):
        sx, sy, sc, rx, ry, rc = bufs
        for copy in copies:
            copy.wait_recv()
        for c in range(comps):
            q = q_ref.at[c]
            q[0:16, :] = q[0:16, :] + jnp.where(has[1][0], rx[0, c], 0.0)
            q[112:128, :] = q[112:128, :] + jnp.where(has[-1][0], rx[1, c], 0.0)
            for k, step in ((0, 1), (1, -1)):
                line = ry[k, c]
                low = jnp.where(has[1][0], rc[k, c : c + 1, :], 0.0)
                high = jnp.where(has[-1][0], rc[2 + k, c : c + 1, :], 0.0)
                line = line + jnp.where(row_x == 0, low, 0.0) + jnp.where(row_x == 7, high, 0.0)
                rows = pl.ds(0 if step == 1 else 15, 8, stride=16)
                q[rows, :] = q[rows, :] + jnp.where(has[step][1], line, 0.0)

    three = (sx3, sy3, sc3, rx3, ry3, rc3)
    ones = [tuple(buf.at[k] for buf in (sx1, sy1, sc1, rx1, ry1, rc1)) for k in range(4)]
    copies = exchange(adv_q, None, three, 0, 3)
    flights = list(copies)

    for load in loads[5:]:
        load.wait()
    rows = lax.broadcasted_iota(jnp.int32, (128, 128), 0)
    in_x, in_y = rows // 16, lax.rem(rows, 16)
    lane = lax.broadcasted_iota(jnp.int32, (128, 128), 1)
    in_z = lax.rem(lane, 8)
    cross_x = ((in_x == 0) & has[1][0]) | ((in_x == 7) & has[-1][0])
    cross_y = ((in_y == 0) & has[1][1]) | ((in_y == 15) & has[-1][1])
    cross = jnp.where(cross_x, 0.5, 1.0) * jnp.where(cross_y, 0.5, 1.0)
    local_half = plain_ref[4]
    inverse_mult = cross * local_half
    inverse_mass = plain_ref[3] * cross

    def sum_yz(value):
        up = pltpu.roll(value, 1, 1)
        down = pltpu.roll(value, 127, 1)
        value = value + jnp.where((in_z == 0) & (lane > 0), up, 0.0)
        value = value + jnp.where((in_z == 7) & (lane < 127), down, 0.0)
        up = pltpu.roll(value, 1, 0)
        down = pltpu.roll(value, 127, 0)
        return value + jnp.where(in_y == 8, up, 0.0) + jnp.where(in_y == 7, down, 0.0)

    mass_term = sum_yz(plain_ref[0] * rea_ref[...].reshape(128, 128)) - SHIFT * cross
    vel = [vel_ref[c].reshape(128, 128) for c in range(3)]
    op_xy, div_xy, div_xy2 = (slice(0, 384), slice(384, 1152), slice(1152, 1920))
    op_z, div_z, div_z2 = (slice(back_rows + 384 * k, back_rows + 384 * k + 384) for k in range(3))

    def divergence(field, on_xy, on_z, scale_z, scale_xy):
        flat = mul(left_ref[:, on_xy], stacked(jnp.concatenate(field[:2], axis=0)))
        return scale_z * flat + scale_xy * mul(joined(field[2]), right_ref[on_z, :])

    base = sum_yz(divergence(vel, div_xy, div_z, plain_ref[5], plain_ref[1]))

    def operate(value):
        flat = mul(left_ref[:, op_xy], stacked(value))
        along = mul(joined(value), right_ref[op_z, :])
        return plain_ref[6] * flat + plain_ref[2] * along + mass_term * value

    receive(adv_q, three, copies, 3)
    adv = []
    for c in range(3):
        adv.append(adv_q[c] * inverse_mass)
    ops_q[0] = 0.05 * divergence(adv, div_xy2, div_z2, plain_ref[6], plain_ref[2]) - base
    copies = exchange(ops_q.at[pl.ds(0, 1)], None, ones[0], 1, 1)
    flights += copies
    for c in range(3):
        adv_ref[c] = adv[c].reshape(8, 16, 128)
    receive(ops_q.at[pl.ds(0, 1)], ones[0], copies, 1)

    def dot(first, second, scale):
        return jnp.sum(first * second * scale, axis=0, keepdims=True)

    z0 = ops_q[0]
    ops_q[1] = operate(z0)
    copies = exchange(ops_q.at[pl.ds(1, 1)], None, ones[1], 2, 1)
    flights += copies
    part[0, 0:1, :] = dot(z0, z0, inverse_mult)
    part[0, 6:8, :] = jnp.zeros((2, 128), jnp.float32)
    receive(ops_q.at[pl.ds(1, 1)], ones[1], copies, 1)
    z1 = ops_q[1]
    ops_q[2] = operate(z1)
    copies = exchange(ops_q.at[pl.ds(2, 1)], None, ones[2], 3, 1)
    flights += copies
    part[0, 1:2, :] = dot(z0, z1, inverse_mult)
    part[0, 2:3, :] = dot(z1, z1, inverse_mult)
    receive(ops_q.at[pl.ds(2, 1)], ones[2], copies, 1)
    z2 = ops_q[2]
    last = operate(z2)
    part[0, 3:4, :] = dot(z1, z2, inverse_mult)
    part[0, 4:5, :] = dot(z2, z2, inverse_mult)
    part[0, 5:6, :] = dot(z2, last, local_half)

    slot = 0
    for index, stage in enumerate(stages):
        copies_in = []
        for k, who in enumerate(stage):
            copies_in.append(
                pltpu.make_async_remote_copy(
                    src_ref=part.at[index],
                    dst_ref=got.at[slot + k],
                    send_sem=tree_send.at[slot + k],
                    recv_sem=tree_recv.at[slot + k],
                    device_id=who,
                    device_id_type=MESH,
                )
            )
        for copy in copies_in:
            copy.start()
        if index == 0:
            ops_q[3] = last
            copies = exchange(ops_q.at[pl.ds(3, 1)], None, ones[3], 4, 1)
            flights += copies
        for copy in copies_in:
            copy.wait_recv()
        total = part[index]
        for k in range(len(stage)):
            total = total + got[slot + k]
        if index < 2:
            part[index + 1] = total
        flights += copies_in
        slot += len(stage)

    receive(ops_q.at[pl.ds(3, 1)], ones[3], copies, 1)
    sums = jnp.broadcast_to(jnp.sum(total, axis=1, keepdims=True), (8, 128))
    g00, g01, g11, g12, g22, g23 = (sums[k : k + 1, :] for k in range(6))
    h00 = g01 + SHIFT * g00
    h01 = g11 + SHIFT * g01
    h11 = g12 + SHIFT * g11
    h02 = g12 + SHIFT * g11
    h12 = g22 + SHIFT * g12
    h22 = g23 + SHIFT * g22
    over = 1.0 / h00
    l10, l20 = h01 * over, h02 * over
    d1 = h11 - l10 * h01
    e1 = h12 - l10 * h02
    over1 = 1.0 / d1
    l21 = e1 * over1
    d2 = h22 - l20 * h02 - l21 * e1
    b1 = g01 - l10 * g00
    b2 = g11 - l20 * g00 - l21 * b1
    c2 = b2 / d2
    c1 = b1 * over1 - l21 * c2
    c0 = g00 * over - l10 * c1 - l20 * c2
    z3 = ops_q[3]
    pres = c0 * z0 + c1 * z1 + c2 * z2
    pres_ref[...] = pres.reshape(8, 16, 128)
    resid = (
        (1.0 - SHIFT * c0) * z0 - (c0 + SHIFT * c1) * z1 - (c1 + SHIFT * c2) * z2 - c2 * z3
    )
    resid_ref[...] = resid.reshape(8, 16, 128)
    for copy in flights:
        copy.wait_send()


def per_device(sizes, velocity, reaction):
    consts = [jnp.asarray(value) for value in tables_for(reaction.shape[2])]
    operands = [velocity, reaction] + consts
    shape_of = jax.ShapeDtypeStruct
    count_x, count_y, low_count = sizes
    trips = (count_y - 1) + (low_count - 1) + (count_x // low_count - 1)
    vmem, f32, dma = pltpu.VMEM, jnp.float32, pltpu.SemaphoreType.DMA
    return pl.pallas_call(
        functools.partial(kernel, sizes),
        out_shape=(
            shape_of(velocity.shape, f32),
            shape_of(reaction.shape, f32),
            shape_of(reaction.shape, f32),
        ),
        in_specs=[pl.BlockSpec(memory_space=pltpu.HBM)] * 8,
        out_specs=(pl.BlockSpec(memory_space=vmem),) * 3,
        scratch_shapes=[vmem(value.shape, value.dtype) for value in operands]
        + [
            dma((8,)),
            vmem((3, 128, 128), f32),
            vmem((4, 128, 128), f32),
            vmem((2, 3, 16, 128), f32),
            vmem((2, 3, 8, 128), f32),
            vmem((4, 8, 128), f32),
            vmem((2, 3, 16, 128), f32),
            vmem((2, 3, 8, 128), f32),
            vmem((4, 8, 128), f32),
            vmem((4, 2, 1, 16, 128), f32),
            vmem((4, 2, 1, 8, 128), f32),
            vmem((4, 4, 8, 128), f32),
            vmem((4, 2, 1, 16, 128), f32),
            vmem((4, 2, 1, 8, 128), f32),
            vmem((4, 4, 8, 128), f32),
            vmem((3, 8, 128), f32),
            vmem((trips, 8, 128), f32),
            dma((5, 8)),
            dma((5, 8)),
            dma((trips,)),
            dma((trips,)),
        ],
        compiler_params=pltpu.CompilerParams(
            collective_id=0, has_side_effects=True, vmem_limit_bytes=54700 * 1024
        ),
    )(*operands)


def solution(mesh):
    count_x, count_y = mesh.shape["wide"], mesh.shape["narrow"]
    low_count = 12 if count_x % 12 == 0 else 2
    return jax.shard_map(
        functools.partial(per_device, (count_x, count_y, low_count)),
        mesh=mesh,
        in_specs=(P(None, "wide", "narrow", None), P("wide", "narrow", None)),
        out_specs=(
            P(None, "wide", "narrow", None),
            P("wide", "narrow", None),
            P("wide", "narrow", None),
        ),
        check_vma=False,
    )
```

```python
import functools

import jax
import jax.numpy as jnp
import ml_dtypes
import numpy as np
from jax import lax
from jax.experimental import pallas as pl
from jax.experimental.pallas import tpu as pltpu
from jax.sharding import PartitionSpec as P

MESH = pl.DeviceIdType.MESH
SHIFT = 4.0
SIDES = ((1, 0), (-1, 0), (0, 1), (0, -1), (1, 1), (1, -1), (-1, 1), (-1, -1))


def legendre_pair(order, nodes):
    p_prev = np.ones(nodes.shape)
    p_now = nodes * 1.0
    for k in range(2, order + 1):
        p_next = ((2 * k - 1) * nodes * p_now - (k - 1) * p_prev) / k
        p_prev = p_now
        p_now = p_next
    return (p_now, p_prev)


def spectral_tables():
    degree = 7
    points = degree + 1
    gll_nodes = np.cos(np.pi * np.arange(points) / degree)
    for sweep in range(100):
        p_now, p_prev = legendre_pair(degree, gll_nodes)
        gll_nodes = gll_nodes - (gll_nodes * p_now - p_prev) / ((degree + 1) * p_now)
    gll_nodes = np.sort(gll_nodes)
    legendre_vals, unused_prev = legendre_pair(degree, gll_nodes)
    gll_weights = 2.0 / (degree * (degree + 1) * legendre_vals**2)
    derivative = np.zeros((points, points))
    for row_index in range(points):
        for col_index in range(points):
            if row_index != col_index:
                derivative[row_index, col_index] = legendre_vals[row_index] / (
                    legendre_vals[col_index] * (gll_nodes[row_index] - gll_nodes[col_index])
                )
    derivative[0, 0] = -degree * (degree + 1) / 4.0
    derivative[-1, -1] = degree * (degree + 1) / 4.0
    gauss_nodes = np.cos(np.pi * (np.arange(12) + 0.75) / 12.5)
    for sweep in range(100):
        p_now, p_prev = legendre_pair(12, gauss_nodes)
        slope = 12 * (gauss_nodes * p_now - p_prev) / (gauss_nodes * gauss_nodes - 1.0)
        gauss_nodes = gauss_nodes - p_now / slope
    gauss_nodes = np.sort(gauss_nodes)
    p_now, p_prev = legendre_pair(12, gauss_nodes)
    slope = 12 * (gauss_nodes * p_now - p_prev) / (gauss_nodes * gauss_nodes - 1.0)
    gauss_weights = 2.0 / ((1.0 - gauss_nodes**2) * slope**2)
    interpolate = np.ones((12, points))
    for col_index in range(points):
        for other in range(points):
            if other != col_index:
                interpolate[:, col_index] *= (gauss_nodes - gll_nodes[other]) / (
                    gll_nodes[col_index] - gll_nodes[other]
                )
    return (gll_weights, derivative, gauss_weights, interpolate)


def halves(matrix):
    high = matrix.astype(ml_dtypes.bfloat16)
    low = (matrix - high.astype(np.float64)).astype(ml_dtypes.bfloat16)
    return high, low


def left_factor(matrix):
    high, low = halves(matrix)
    return np.concatenate([high, high, low], axis=1)


def right_factor(matrix):
    high, low = halves(matrix)
    return np.concatenate([high, high, low], axis=0)


def tables_for(len_z):
    weights, deriv, fine_weights, interp = spectral_tables()
    els_z = len_z // 8
    gradint = interp @ deriv
    stiff = deriv.T @ np.diag(weights) @ deriv
    eye2, eye_z = np.eye(2), np.eye(els_z)

    def shared(count):
        total = np.eye(8 * count)
        for k in range(count - 1):
            total[8 * k + 7, 8 * k + 8] = total[8 * k + 8, 8 * k + 7] = 1.0
        return total

    sum_y, sum_z = shared(2), shared(els_z)
    w_x, w_y, w_z = weights, np.tile(weights, 2), np.tile(weights, els_z)
    w_y2, w_z2 = sum_y @ w_y, sum_z @ w_z

    fine_z = np.zeros((len_z, 2 * 16 * els_z))
    back_z = np.zeros((16 * els_z, len_z))
    for e in range(els_z):
        fine_z[8 * e : 8 * e + 8, 16 * e : 16 * e + 12] = interp.T
        first = 16 * els_z + 16 * e
        fine_z[8 * e : 8 * e + 8, first : first + 12] = gradint.T
        back_z[16 * e : 16 * e + 12, 8 * e : 8 * e + 8] = fine_weights[:, None] * interp
    back_z = back_z @ sum_z
    fine_xy = np.concatenate(
        [np.kron(interp, interp), np.kron(gradint, interp), np.kron(interp, gradint)], axis=0
    )
    back = interp.T * fine_weights[None, :]
    back_xy = np.kron(back, back)

    op_xy = np.kron(stiff, np.diag(w_y2)) + np.kron(np.diag(w_x), sum_y @ np.kron(eye2, stiff))
    op_z = np.kron(eye_z, stiff).T @ sum_z
    weak = np.diag(weights) @ deriv
    div_xy = np.concatenate(
        [np.kron(weak, np.diag(w_y)), np.kron(np.diag(w_x), np.kron(eye2, weak))], axis=1
    )
    div_xy2 = np.concatenate(
        [np.kron(weak, np.diag(w_y2)), np.kron(np.diag(w_x), sum_y @ np.kron(eye2, weak))], axis=1
    )
    div_z = np.kron(eye_z, weak).T
    div_z2 = div_z @ sum_z

    w_xy, w_xy2 = np.kron(w_x, w_y), np.kron(w_x, w_y2)
    half_y = 1.0 / (sum_y @ np.ones(16))
    half_z = 1.0 / (sum_z @ np.ones(len_z))
    ones_x, ones_z = np.ones(8), np.ones(len_z)
    plain = np.stack(
        [
            np.outer(w_xy, w_z),
            np.outer(w_xy, ones_z),
            np.outer(w_xy2, ones_z),
            1.0 / np.outer(w_xy2, w_z2),
            np.outer(np.kron(ones_x, half_y), half_z),
            np.outer(np.ones(128), w_z),
            np.outer(np.ones(128), w_z2),
        ]
    ).astype(np.float32)
    from_right = np.concatenate(
        [right_factor(back_z), right_factor(op_z), right_factor(div_z), right_factor(div_z2)], axis=0
    )
    from_left = np.concatenate(
        [left_factor(op_xy), left_factor(div_xy), left_factor(div_xy2)], axis=1
    )
    shapes_xy = np.zeros((496, 432), ml_dtypes.bfloat16)
    shapes_xy[:432, :192] = left_factor(fine_xy)
    shapes_xy[432:] = left_factor(back_xy)
    return (
        right_factor(fine_z),
        shapes_xy,
        from_right,
        from_left,
        plain,
    )


def split(value):
    high = value.astype(jnp.bfloat16)
    low = (value - high.astype(jnp.float32)).astype(jnp.bfloat16)
    return high, low


def stacked(value):
    high, low = split(value)
    return jnp.concatenate([high, low, high], axis=0)


def joined(value):
    high, low = split(value)
    return jnp.concatenate([high, low, high], axis=1)


def mul(first, second):
    return jnp.dot(first, second, preferred_element_type=jnp.float32)


def kernel(
    sizes,
    vel_hbm,
    rea_hbm,
    fine_z_hbm,
    fine_xy_hbm,
    right_hbm,
    left_hbm,
    plain_hbm,
    adv_ref,
    pres_ref,
    resid_ref,
    vel_ref,
    rea_ref,
    fine_z_ref,
    fine_xy_ref,
    right_ref,
    left_ref,
    plain_ref,
    load_sem,
    adv_q,
    ops_q,
    sx3,
    sy3,
    sc3,
    rx3,
    ry3,
    rc3,
    sx1,
    sy1,
    sc1,
    rx1,
    ry1,
    rc1,
    part,
    got,
    send_sem,
    recv_sem,
    tree_send,
    tree_recv,
):
    pairs = (
        (vel_hbm, vel_ref),
        (fine_z_hbm, fine_z_ref),
        (fine_xy_hbm, fine_xy_ref),
        (right_hbm, right_ref),
        (plain_hbm, plain_ref),
        (rea_hbm, rea_ref),
        (left_hbm, left_ref),
    )
    loads = [pltpu.make_async_copy(a, b, load_sem.at[k]) for k, (a, b) in enumerate(pairs)]
    for load in loads:
        load.start()

    count_x, count_y, low_count = sizes
    high_count = count_x // low_count
    me_x, me_y = lax.axis_index("wide"), lax.axis_index("narrow")
    me_low, me_high = lax.rem(me_x, low_count), me_x // low_count
    me_pair, me_core = me_y // 2, lax.rem(me_y, 2)

    def turn(place, step, count):
        moved = place + step % count
        return jnp.where(moved >= count, moved - count, moved)

    def at_side(side):
        return turn(me_x, side[0], count_x), turn(me_y, side[1], count_y)

    def far_first(count_a, count_b):
        hops = lambda step, count: min(step, count - step)
        steps = [(i, j) for i in range(count_a) for j in range(count_b) if (i, j) != (0, 0)]
        return sorted(steps, key=lambda s: -hops(s[0], count_a) - hops(s[1], count_b))

    stages = (
        [
            (me_high * low_count + turn(me_low, i, low_count), me_pair * 2 + turn(me_core, j, 2))
            for i, j in far_first(low_count, 2)
        ],
        [
            (
                turn(me_high, i, high_count) * low_count + me_low,
                turn(me_pair, j, count_y // 2) * 2 + me_core,
            )
            for i, j in far_first(high_count, count_y // 2)
        ],
    )
    partners = [at_side(side) for side in SIDES] + [who for stage in stages for who in stage]

    barrier = pltpu.get_barrier_semaphore()
    for who in partners:
        pl.semaphore_signal(barrier, inc=1, device_id=who, device_id_type=MESH)

    for load in loads[:3]:
        load.wait()
    parts = []
    for c in range(3):
        for e in range(2):
            parts.append(vel_ref[c, :, 8 * e : 8 * e + 8, :].reshape(64, 128))
    on_z = mul(joined(jnp.concatenate(parts, axis=0)), fine_z_ref[...])
    width = on_z.shape[1] // 2
    products = {}
    for e in range(2):
        fine = []
        for c in range(3):
            first = 64 * (2 * c + e)
            flat = mul(fine_xy_ref[:432, :192], stacked(on_z[first : first + 64, :width]))
            steep = mul(fine_xy_ref[:144, :192], stacked(on_z[first : first + 64, width:]))
            fine.append((flat[:144], flat[144:288], flat[288:], steep))
        for c in range(3):
            products[c, e] = (
                fine[0][0] * fine[c][1] + fine[1][0] * fine[c][2] + fine[2][0] * fine[c][3]
            )
    for load in loads[3:4]:
        load.wait()
    row8 = lax.broadcasted_iota(jnp.int32, (8, 8, 128), 1)
    back_rows = 3 * width
    for c in range(3):
        both = []
        for e in range(2):
            both.append(stacked(mul(joined(products[c, e]), right_ref[:back_rows, :])))
        weak = mul(fine_xy_ref[432:, :], jnp.concatenate(both, axis=1))
        first = weak[:, :128].reshape(8, 8, 128)
        second = weak[:, 128:].reshape(8, 8, 128)
        first, second = (
            first + jnp.where(row8 == 7, pltpu.roll(second, 7, 1), 0.0),
            second + jnp.where(row8 == 0, pltpu.roll(first, 1, 1), 0.0),
        )
        adv_q[c] = jnp.concatenate([first, second], axis=1).reshape(128, 128)

    pl.semaphore_wait(barrier, len(partners))

    has = {1: (me_x > 0, me_y > 0), -1: (me_x < count_x - 1, me_y < count_y - 1)}

    def exchange(q_ref, slots, bufs, index, comps):
        sx, sy, sc, rx, ry, rc = bufs
        for c in range(comps):
            q = q_ref.at[c]
            sx[0, c] = q[112:128, :]
            sx[1, c] = q[0:16, :]
            sy[0, c] = q[pl.ds(15, 8, stride=16), :]
            sy[1, c] = q[pl.ds(0, 8, stride=16), :]
            for k, row in enumerate((127, 112, 15, 0)):
                sc[k, c : c + 1, :] = q[row : row + 1, :]
        copies = []
        for k, side in enumerate(SIDES):
            if k < 2:
                source, target = sx.at[k], rx.at[k]
            elif k < 4:
                source, target = sy.at[k - 2], ry.at[k - 2]
            else:
                source, target = sc.at[k - 4], rc.at[k - 4]
            copies.append(
                pltpu.make_async_remote_copy(
                    src_ref=source,
                    dst_ref=target,
                    send_sem=send_sem.at[index, k],
                    recv_sem=recv_sem.at[index, k],
                    device_id=at_side(side),
                    device_id_type=MESH,
                )
            )
        for copy in copies[4:] + copies[:4]:
            copy.start()
        return copies

    row_x = lax.broadcasted_iota(jnp.int32, (8, 128), 0)

    def receive(q_ref, bufs, copies, comps):
        sx, sy, sc, rx, ry, rc = bufs
        for copy in copies:
            copy.wait_recv()
        for c in range(comps):
            q = q_ref.at[c]
            q[0:16, :] = q[0:16, :] + jnp.where(has[1][0], rx[0, c], 0.0)
            q[112:128, :] = q[112:128, :] + jnp.where(has[-1][0], rx[1, c], 0.0)
            for k, step in ((0, 1), (1, -1)):
                line = ry[k, c]
                low = jnp.where(has[1][0], rc[k, c : c + 1, :], 0.0)
                high = jnp.where(has[-1][0], rc[2 + k, c : c + 1, :], 0.0)
                line = line + jnp.where(row_x == 0, low, 0.0) + jnp.where(row_x == 7, high, 0.0)
                rows = pl.ds(0 if step == 1 else 15, 8, stride=16)
                q[rows, :] = q[rows, :] + jnp.where(has[step][1], line, 0.0)

    three = (sx3, sy3, sc3, rx3, ry3, rc3)
    ones = [tuple(buf.at[k] for buf in (sx1, sy1, sc1, rx1, ry1, rc1)) for k in range(4)]
    copies = exchange(adv_q, None, three, 0, 3)
    flights = list(copies)

    for load in loads[4:]:
        load.wait()
    rows = lax.broadcasted_iota(jnp.int32, (128, 128), 0)
    in_x, in_y = rows // 16, lax.rem(rows, 16)
    lane = lax.broadcasted_iota(jnp.int32, (128, 128), 1)
    in_z = lax.rem(lane, 8)
    cross_x = ((in_x == 0) & has[1][0]) | ((in_x == 7) & has[-1][0])
    cross_y = ((in_y == 0) & has[1][1]) | ((in_y == 15) & has[-1][1])
    cross = jnp.where(cross_x, 0.5, 1.0) * jnp.where(cross_y, 0.5, 1.0)
    local_half = plain_ref[4]
    inverse_mult = cross * local_half
    inverse_mass = plain_ref[3] * cross

    def sum_yz(value):
        up = pltpu.roll(value, 1, 1)
        down = pltpu.roll(value, 127, 1)
        value = value + jnp.where((in_z == 0) & (lane > 0), up, 0.0)
        value = value + jnp.where((in_z == 7) & (lane < 127), down, 0.0)
        up = pltpu.roll(value, 1, 0)
        down = pltpu.roll(value, 127, 0)
        return value + jnp.where(in_y == 8, up, 0.0) + jnp.where(in_y == 7, down, 0.0)

    mass_term = sum_yz(plain_ref[0] * rea_ref[...].reshape(128, 128)) - SHIFT * cross
    vel = [vel_ref[c].reshape(128, 128) for c in range(3)]
    op_xy, div_xy, div_xy2 = (slice(0, 384), slice(384, 1152), slice(1152, 1920))
    op_z, div_z, div_z2 = (slice(back_rows + 384 * k, back_rows + 384 * k + 384) for k in range(3))

    def divergence(field, on_xy, on_z, scale_z, scale_xy):
        flat = mul(left_ref[:, on_xy], stacked(jnp.concatenate(field[:2], axis=0)))
        return scale_z * flat + scale_xy * mul(joined(field[2]), right_ref[on_z, :])

    base = sum_yz(divergence(vel, div_xy, div_z, plain_ref[5], plain_ref[1]))

    def operate(value):
        flat = mul(left_ref[:, op_xy], stacked(value))
        along = mul(joined(value), right_ref[op_z, :])
        return plain_ref[6] * flat + plain_ref[2] * along + mass_term * value

    receive(adv_q, three, copies, 3)
    adv = []
    for c in range(3):
        adv.append(adv_q[c] * inverse_mass)
    ops_q[0] = 0.05 * divergence(adv, div_xy2, div_z2, plain_ref[6], plain_ref[2]) - base
    copies = exchange(ops_q.at[pl.ds(0, 1)], None, ones[0], 1, 1)
    flights += copies
    for c in range(3):
        adv_ref[c] = adv[c].reshape(8, 16, 128)
    receive(ops_q.at[pl.ds(0, 1)], ones[0], copies, 1)

    def dot(first, second, scale):
        return jnp.sum(first * second * scale, axis=0, keepdims=True)

    z0 = ops_q[0]
    ops_q[1] = operate(z0)
    copies = exchange(ops_q.at[pl.ds(1, 1)], None, ones[1], 2, 1)
    flights += copies
    part[0, 0:1, :] = dot(z0, z0, inverse_mult)
    part[0, 6:8, :] = jnp.zeros((2, 128), jnp.float32)
    receive(ops_q.at[pl.ds(1, 1)], ones[1], copies, 1)
    z1 = ops_q[1]
    ops_q[2] = operate(z1)
    copies = exchange(ops_q.at[pl.ds(2, 1)], None, ones[2], 3, 1)
    flights += copies
    part[0, 1:2, :] = dot(z0, z1, inverse_mult)
    part[0, 2:3, :] = dot(z1, z1, inverse_mult)
    receive(ops_q.at[pl.ds(2, 1)], ones[2], copies, 1)
    z2 = ops_q[2]
    last = operate(z2)
    part[0, 3:4, :] = dot(z1, z2, inverse_mult)
    part[0, 4:5, :] = dot(z2, z2, inverse_mult)
    part[0, 5:6, :] = dot(z2, last, local_half)

    slot = 0
    for index, stage in enumerate(stages):
        copies_in = []
        for k, who in enumerate(stage):
            copies_in.append(
                pltpu.make_async_remote_copy(
                    src_ref=part.at[index],
                    dst_ref=got.at[slot + k],
                    send_sem=tree_send.at[slot + k],
                    recv_sem=tree_recv.at[slot + k],
                    device_id=who,
                    device_id_type=MESH,
                )
            )
        for copy in copies_in:
            copy.start()
        if index == 0:
            ops_q[3] = last
            copies = exchange(ops_q.at[pl.ds(3, 1)], None, ones[3], 4, 1)
            flights += copies
        for copy in copies_in:
            copy.wait_recv()
        total = part[index]
        for k in range(len(stage)):
            total = total + got[slot + k]
        if index < 1:
            part[index + 1] = total
        flights += copies_in
        slot += len(stage)

    receive(ops_q.at[pl.ds(3, 1)], ones[3], copies, 1)
    sums = jnp.broadcast_to(jnp.sum(total, axis=1, keepdims=True), (8, 128))
    g00, g01, g11, g12, g22, g23 = (sums[k : k + 1, :] for k in range(6))
    h00 = g01 + SHIFT * g00
    h01 = g11 + SHIFT * g01
    h11 = g12 + SHIFT * g11
    h02 = g12 + SHIFT * g11
    h12 = g22 + SHIFT * g12
    h22 = g23 + SHIFT * g22
    over = 1.0 / h00
    l10, l20 = h01 * over, h02 * over
    d1 = h11 - l10 * h01
    e1 = h12 - l10 * h02
    over1 = 1.0 / d1
    l21 = e1 * over1
    d2 = h22 - l20 * h02 - l21 * e1
    b1 = g01 - l10 * g00
    b2 = g11 - l20 * g00 - l21 * b1
    c2 = b2 / d2
    c1 = b1 * over1 - l21 * c2
    c0 = g00 * over - l10 * c1 - l20 * c2
    z3 = ops_q[3]
    pres = c0 * z0 + c1 * z1 + c2 * z2
    pres_ref[...] = pres.reshape(8, 16, 128)
    resid = (
        (1.0 - SHIFT * c0) * z0 - (c0 + SHIFT * c1) * z1 - (c1 + SHIFT * c2) * z2 - c2 * z3
    )
    resid_ref[...] = resid.reshape(8, 16, 128)
    for copy in flights:
        copy.wait_send()


def per_device(sizes, velocity, reaction):
    consts = [jnp.asarray(value) for value in tables_for(reaction.shape[2])]
    operands = [velocity, reaction] + consts
    shape_of = jax.ShapeDtypeStruct
    count_x, count_y, low_count = sizes
    trips = (2 * low_count - 1) + (count_x // low_count * count_y // 2 - 1)
    vmem, f32, dma = pltpu.VMEM, jnp.float32, pltpu.SemaphoreType.DMA
    return pl.pallas_call(
        functools.partial(kernel, sizes),
        out_shape=(
            shape_of(velocity.shape, f32),
            shape_of(reaction.shape, f32),
            shape_of(reaction.shape, f32),
        ),
        in_specs=[pl.BlockSpec(memory_space=pltpu.HBM)] * 7,
        out_specs=(pl.BlockSpec(memory_space=vmem),) * 3,
        scratch_shapes=[vmem(value.shape, value.dtype) for value in operands]
        + [
            dma((7,)),
            vmem((3, 128, 128), f32),
            vmem((4, 128, 128), f32),
            vmem((2, 3, 16, 128), f32),
            vmem((2, 3, 8, 128), f32),
            vmem((4, 8, 128), f32),
            vmem((2, 3, 16, 128), f32),
            vmem((2, 3, 8, 128), f32),
            vmem((4, 8, 128), f32),
            vmem((4, 2, 1, 16, 128), f32),
            vmem((4, 2, 1, 8, 128), f32),
            vmem((4, 4, 8, 128), f32),
            vmem((4, 2, 1, 16, 128), f32),
            vmem((4, 2, 1, 8, 128), f32),
            vmem((4, 4, 8, 128), f32),
            vmem((2, 8, 128), f32),
            vmem((trips, 8, 128), f32),
            dma((5, 8)),
            dma((5, 8)),
            dma((trips,)),
            dma((trips,)),
        ],
        compiler_params=pltpu.CompilerParams(
            collective_id=0, has_side_effects=True, vmem_limit_bytes=54700 * 1024
        ),
    )(*operands)


def solution(mesh):
    count_x, count_y = mesh.shape["wide"], mesh.shape["narrow"]
    low_count = 12 if count_x % 12 == 0 else 2
    return jax.shard_map(
        functools.partial(per_device, (count_x, count_y, low_count)),
        mesh=mesh,
        in_specs=(P(None, "wide", "narrow", None), P("wide", "narrow", None)),
        out_specs=(
            P(None, "wide", "narrow", None),
            P("wide", "narrow", None),
            P("wide", "narrow", None),
        ),
        check_vma=False,
    )
```

```python
import functools

import jax
import jax.numpy as jnp
import ml_dtypes
import numpy as np
from jax import lax
from jax.experimental import pallas as pl
from jax.experimental.pallas import tpu as pltpu
from jax.sharding import PartitionSpec as P

MESH = pl.DeviceIdType.MESH
SHIFT = 4.0
SIDES = ((1, 0), (-1, 0), (0, 1), (0, -1), (1, 1), (1, -1), (-1, 1), (-1, -1))


def legendre_pair(order, nodes):
    p_prev = np.ones(nodes.shape)
    p_now = nodes * 1.0
    for k in range(2, order + 1):
        p_next = ((2 * k - 1) * nodes * p_now - (k - 1) * p_prev) / k
        p_prev = p_now
        p_now = p_next
    return (p_now, p_prev)


def spectral_tables():
    degree = 7
    points = degree + 1
    gll_nodes = np.cos(np.pi * np.arange(points) / degree)
    for sweep in range(100):
        p_now, p_prev = legendre_pair(degree, gll_nodes)
        gll_nodes = gll_nodes - (gll_nodes * p_now - p_prev) / ((degree + 1) * p_now)
    gll_nodes = np.sort(gll_nodes)
    legendre_vals, unused_prev = legendre_pair(degree, gll_nodes)
    gll_weights = 2.0 / (degree * (degree + 1) * legendre_vals**2)
    derivative = np.zeros((points, points))
    for row_index in range(points):
        for col_index in range(points):
            if row_index != col_index:
                derivative[row_index, col_index] = legendre_vals[row_index] / (
                    legendre_vals[col_index] * (gll_nodes[row_index] - gll_nodes[col_index])
                )
    derivative[0, 0] = -degree * (degree + 1) / 4.0
    derivative[-1, -1] = degree * (degree + 1) / 4.0
    gauss_nodes = np.cos(np.pi * (np.arange(12) + 0.75) / 12.5)
    for sweep in range(100):
        p_now, p_prev = legendre_pair(12, gauss_nodes)
        slope = 12 * (gauss_nodes * p_now - p_prev) / (gauss_nodes * gauss_nodes - 1.0)
        gauss_nodes = gauss_nodes - p_now / slope
    gauss_nodes = np.sort(gauss_nodes)
    p_now, p_prev = legendre_pair(12, gauss_nodes)
    slope = 12 * (gauss_nodes * p_now - p_prev) / (gauss_nodes * gauss_nodes - 1.0)
    gauss_weights = 2.0 / ((1.0 - gauss_nodes**2) * slope**2)
    interpolate = np.ones((12, points))
    for col_index in range(points):
        for other in range(points):
            if other != col_index:
                interpolate[:, col_index] *= (gauss_nodes - gll_nodes[other]) / (
                    gll_nodes[col_index] - gll_nodes[other]
                )
    return (gll_weights, derivative, gauss_weights, interpolate)


def halves(matrix):
    high = matrix.astype(ml_dtypes.bfloat16)
    low = (matrix - high.astype(np.float64)).astype(ml_dtypes.bfloat16)
    return high, low


def left_factor(matrix):
    high, low = halves(matrix)
    return np.concatenate([high, high, low], axis=1)


def right_factor(matrix):
    high, low = halves(matrix)
    return np.concatenate([high, high, low], axis=0)


def tables_for(len_z):
    weights, deriv, fine_weights, interp = spectral_tables()
    els_z = len_z // 8
    gradint = interp @ deriv
    stiff = deriv.T @ np.diag(weights) @ deriv
    eye2, eye_z = np.eye(2), np.eye(els_z)

    def shared(count):
        total = np.eye(8 * count)
        for k in range(count - 1):
            total[8 * k + 7, 8 * k + 8] = total[8 * k + 8, 8 * k + 7] = 1.0
        return total

    sum_y, sum_z = shared(2), shared(els_z)
    w_x, w_y, w_z = weights, np.tile(weights, 2), np.tile(weights, els_z)
    w_y2, w_z2 = sum_y @ w_y, sum_z @ w_z

    fine_z = np.zeros((len_z, 2 * 16 * els_z))
    back_z = np.zeros((16 * els_z, len_z))
    for e in range(els_z):
        fine_z[8 * e : 8 * e + 8, 16 * e : 16 * e + 12] = interp.T
        first = 16 * els_z + 16 * e
        fine_z[8 * e : 8 * e + 8, first : first + 12] = gradint.T
        back_z[16 * e : 16 * e + 12, 8 * e : 8 * e + 8] = fine_weights[:, None] * interp
    back_z = back_z @ sum_z
    fine_xy = np.concatenate(
        [np.kron(interp, interp), np.kron(gradint, interp), np.kron(interp, gradint)], axis=0
    )
    back = interp.T * fine_weights[None, :]
    back_xy = np.kron(back, back)

    op_xy = np.kron(stiff, np.diag(w_y2)) + np.kron(np.diag(w_x), sum_y @ np.kron(eye2, stiff))
    op_z = np.kron(eye_z, stiff).T @ sum_z
    weak = np.diag(weights) @ deriv
    div_xy = np.concatenate(
        [np.kron(weak, np.diag(w_y)), np.kron(np.diag(w_x), np.kron(eye2, weak))], axis=1
    )
    div_xy2 = np.concatenate(
        [np.kron(weak, np.diag(w_y2)), np.kron(np.diag(w_x), sum_y @ np.kron(eye2, weak))], axis=1
    )
    div_z = np.kron(eye_z, weak).T
    div_z2 = div_z @ sum_z

    w_xy, w_xy2 = np.kron(w_x, w_y), np.kron(w_x, w_y2)
    half_y = 1.0 / (sum_y @ np.ones(16))
    half_z = 1.0 / (sum_z @ np.ones(len_z))
    ones_x, ones_z = np.ones(8), np.ones(len_z)
    plain = np.stack(
        [
            np.outer(w_xy, w_z),
            np.outer(w_xy, ones_z),
            np.outer(w_xy2, ones_z),
            1.0 / np.outer(w_xy2, w_z2),
            np.outer(np.kron(ones_x, half_y), half_z),
            np.outer(np.ones(128), w_z),
            np.outer(np.ones(128), w_z2),
        ]
    ).astype(np.float32)
    from_right = np.concatenate(
        [right_factor(back_z), right_factor(op_z), right_factor(div_z), right_factor(div_z2)], axis=0
    )
    from_left = np.concatenate(
        [left_factor(op_xy), left_factor(div_xy), left_factor(div_xy2)], axis=1
    )
    shapes_xy = np.zeros((496, 432), ml_dtypes.bfloat16)
    shapes_xy[:432, :192] = left_factor(fine_xy)
    shapes_xy[432:] = left_factor(back_xy)
    return (
        right_factor(fine_z),
        shapes_xy,
        from_right,
        from_left,
        plain,
    )


def split(value):
    high = value.astype(jnp.bfloat16)
    low = (value - high.astype(jnp.float32)).astype(jnp.bfloat16)
    return high, low


def stacked(value):
    high, low = split(value)
    return jnp.concatenate([high, low, high], axis=0)


def joined(value):
    high, low = split(value)
    return jnp.concatenate([high, low, high], axis=1)


def mul(first, second):
    return jnp.dot(first, second, preferred_element_type=jnp.float32)


def kernel(
    sizes,
    vel_hbm,
    rea_hbm,
    fine_z_hbm,
    fine_xy_hbm,
    right_hbm,
    left_hbm,
    plain_hbm,
    adv_ref,
    pres_ref,
    resid_ref,
    vel_ref,
    rea_ref,
    fine_z_ref,
    fine_xy_ref,
    right_ref,
    left_ref,
    plain_ref,
    load_sem,
    adv_q,
    ops_q,
    sx3,
    sy3,
    sc3,
    rx3,
    ry3,
    rc3,
    sx1,
    sy1,
    sc1,
    rx1,
    ry1,
    rc1,
    part,
    got,
    send_sem,
    recv_sem,
    tree_send,
    tree_recv,
    word,
):
    pairs = (
        (vel_hbm, vel_ref),
        (fine_z_hbm, fine_z_ref),
        (fine_xy_hbm, fine_xy_ref),
        (right_hbm, right_ref),
        (plain_hbm, plain_ref),
        (rea_hbm, rea_ref),
        (left_hbm, left_ref),
    )
    loads = [pltpu.make_async_copy(a, b, load_sem.at[k]) for k, (a, b) in enumerate(pairs)]
    for load in loads:
        load.start()

    count_x, count_y, low_count = sizes
    high_count = count_x // low_count
    me_x, me_y = lax.axis_index("wide"), lax.axis_index("narrow")
    me_low, me_high = lax.rem(me_x, low_count), me_x // low_count
    me_pair, me_core = me_y // 2, lax.rem(me_y, 2)

    def turn(place, step, count):
        moved = place + step % count
        return jnp.where(moved >= count, moved - count, moved)

    def at_side(side):
        return turn(me_x, side[0], count_x), turn(me_y, side[1], count_y)

    def far_first(count_a, count_b):
        hops = lambda step, count: min(step, count - step)
        steps = [(i, j) for i in range(count_a) for j in range(count_b) if (i, j) != (0, 0)]
        return sorted(steps, key=lambda s: -hops(s[0], count_a) - hops(s[1], count_b))

    stages = (
        [
            (me_high * low_count + turn(me_low, i, low_count), me_pair * 2 + turn(me_core, j, 2))
            for i, j in far_first(low_count, 2)
        ],
        [
            (
                turn(me_high, i, high_count) * low_count + me_low,
                turn(me_pair, j, count_y // 2) * 2 + me_core,
            )
            for i, j in far_first(high_count, count_y // 2)
        ],
    )
    def by_z(step):
        return me_high * low_count + turn(me_low, step, low_count), me_y

    def by_y(step):
        return turn(me_high, step, high_count) * low_count + me_low, me_y

    def by_pair(step):
        return me_x, turn(me_pair, step, count_y // 2) * 2 + me_core

    near = [by_z(1), by_z(-1), by_y(1), by_y(-1), by_pair(1), by_pair(-1)]
    rounds = (
        near[:4],
        [by_z(2), by_z(-2), by_y(2), by_y(-2)],
        [by_z(2), by_z(-2)] + near[4:],
        near[4:] + [(me_x, me_pair * 2 + 1 - me_core)],
    )
    partners = [at_side(side) for side in SIDES] + near

    barrier = pltpu.get_barrier_semaphore()
    for who in partners:
        pl.semaphore_signal(barrier, inc=1, device_id=who, device_id_type=MESH)

    def vouch(index):
        for who in rounds[index]:
            pl.semaphore_signal(word.at[index], inc=1, device_id=who, device_id_type=MESH)

    def hear(index):
        pl.semaphore_wait(word.at[index], len(rounds[index]))

    for load in loads[:3]:
        load.wait()
    parts = []
    for c in range(3):
        for e in range(2):
            parts.append(vel_ref[c, :, 8 * e : 8 * e + 8, :].reshape(64, 128))
    on_z = mul(joined(jnp.concatenate(parts, axis=0)), fine_z_ref[...])
    width = on_z.shape[1] // 2
    products = {}
    for e in range(2):
        fine = []
        for c in range(3):
            first = 64 * (2 * c + e)
            flat = mul(fine_xy_ref[:432, :192], stacked(on_z[first : first + 64, :width]))
            steep = mul(fine_xy_ref[:144, :192], stacked(on_z[first : first + 64, width:]))
            fine.append((flat[:144], flat[144:288], flat[288:], steep))
        for c in range(3):
            products[c, e] = (
                fine[0][0] * fine[c][1] + fine[1][0] * fine[c][2] + fine[2][0] * fine[c][3]
            )
    for load in loads[3:4]:
        load.wait()
    row8 = lax.broadcasted_iota(jnp.int32, (8, 8, 128), 1)
    back_rows = 3 * width
    for c in range(3):
        both = []
        for e in range(2):
            both.append(stacked(mul(joined(products[c, e]), right_ref[:back_rows, :])))
        weak = mul(fine_xy_ref[432:, :], jnp.concatenate(both, axis=1))
        first = weak[:, :128].reshape(8, 8, 128)
        second = weak[:, 128:].reshape(8, 8, 128)
        first, second = (
            first + jnp.where(row8 == 7, pltpu.roll(second, 7, 1), 0.0),
            second + jnp.where(row8 == 0, pltpu.roll(first, 1, 1), 0.0),
        )
        adv_q[c] = jnp.concatenate([first, second], axis=1).reshape(128, 128)

    pl.semaphore_wait(barrier, len(partners))

    has = {1: (me_x > 0, me_y > 0), -1: (me_x < count_x - 1, me_y < count_y - 1)}

    def exchange(q_ref, slots, bufs, index, comps):
        sx, sy, sc, rx, ry, rc = bufs
        for c in range(comps):
            q = q_ref.at[c]
            sx[0, c] = q[112:128, :]
            sx[1, c] = q[0:16, :]
            sy[0, c] = q[pl.ds(15, 8, stride=16), :]
            sy[1, c] = q[pl.ds(0, 8, stride=16), :]
            for k, row in enumerate((127, 112, 15, 0)):
                sc[k, c : c + 1, :] = q[row : row + 1, :]
        copies = []
        for k, side in enumerate(SIDES):
            if k < 2:
                source, target = sx.at[k], rx.at[k]
            elif k < 4:
                source, target = sy.at[k - 2], ry.at[k - 2]
            else:
                source, target = sc.at[k - 4], rc.at[k - 4]
            copies.append(
                pltpu.make_async_remote_copy(
                    src_ref=source,
                    dst_ref=target,
                    send_sem=send_sem.at[index, k],
                    recv_sem=recv_sem.at[index, k],
                    device_id=at_side(side),
                    device_id_type=MESH,
                )
            )
        for copy in copies[4:] + copies[:4]:
            copy.start()
        return copies

    row_x = lax.broadcasted_iota(jnp.int32, (8, 128), 0)

    def receive(q_ref, bufs, copies, comps):
        sx, sy, sc, rx, ry, rc = bufs
        for copy in copies:
            copy.wait_recv()
        for c in range(comps):
            q = q_ref.at[c]
            q[0:16, :] = q[0:16, :] + jnp.where(has[1][0], rx[0, c], 0.0)
            q[112:128, :] = q[112:128, :] + jnp.where(has[-1][0], rx[1, c], 0.0)
            for k, step in ((0, 1), (1, -1)):
                line = ry[k, c]
                low = jnp.where(has[1][0], rc[k, c : c + 1, :], 0.0)
                high = jnp.where(has[-1][0], rc[2 + k, c : c + 1, :], 0.0)
                line = line + jnp.where(row_x == 0, low, 0.0) + jnp.where(row_x == 7, high, 0.0)
                rows = pl.ds(0 if step == 1 else 15, 8, stride=16)
                q[rows, :] = q[rows, :] + jnp.where(has[step][1], line, 0.0)

    three = (sx3, sy3, sc3, rx3, ry3, rc3)
    ones = [tuple(buf.at[k] for buf in (sx1, sy1, sc1, rx1, ry1, rc1)) for k in range(4)]
    copies = exchange(adv_q, None, three, 0, 3)
    vouch(0)
    flights = list(copies)

    for load in loads[4:]:
        load.wait()
    rows = lax.broadcasted_iota(jnp.int32, (128, 128), 0)
    in_x, in_y = rows // 16, lax.rem(rows, 16)
    lane = lax.broadcasted_iota(jnp.int32, (128, 128), 1)
    in_z = lax.rem(lane, 8)
    cross_x = ((in_x == 0) & has[1][0]) | ((in_x == 7) & has[-1][0])
    cross_y = ((in_y == 0) & has[1][1]) | ((in_y == 15) & has[-1][1])
    cross = jnp.where(cross_x, 0.5, 1.0) * jnp.where(cross_y, 0.5, 1.0)
    local_half = plain_ref[4]
    inverse_mult = cross * local_half
    inverse_mass = plain_ref[3] * cross

    def sum_yz(value):
        up = pltpu.roll(value, 1, 1)
        down = pltpu.roll(value, 127, 1)
        value = value + jnp.where((in_z == 0) & (lane > 0), up, 0.0)
        value = value + jnp.where((in_z == 7) & (lane < 127), down, 0.0)
        up = pltpu.roll(value, 1, 0)
        down = pltpu.roll(value, 127, 0)
        return value + jnp.where(in_y == 8, up, 0.0) + jnp.where(in_y == 7, down, 0.0)

    mass_term = sum_yz(plain_ref[0] * rea_ref[...].reshape(128, 128)) - SHIFT * cross
    vel = [vel_ref[c].reshape(128, 128) for c in range(3)]
    op_xy, div_xy, div_xy2 = (slice(0, 384), slice(384, 1152), slice(1152, 1920))
    op_z, div_z, div_z2 = (slice(back_rows + 384 * k, back_rows + 384 * k + 384) for k in range(3))

    def divergence(field, on_xy, on_z, scale_z, scale_xy):
        flat = mul(left_ref[:, on_xy], stacked(jnp.concatenate(field[:2], axis=0)))
        return scale_z * flat + scale_xy * mul(joined(field[2]), right_ref[on_z, :])

    base = sum_yz(divergence(vel, div_xy, div_z, plain_ref[5], plain_ref[1]))

    def operate(value):
        flat = mul(left_ref[:, op_xy], stacked(value))
        along = mul(joined(value), right_ref[op_z, :])
        return plain_ref[6] * flat + plain_ref[2] * along + mass_term * value

    receive(adv_q, three, copies, 3)
    hear(0)
    adv = []
    for c in range(3):
        adv.append(adv_q[c] * inverse_mass)
    ops_q[0] = 0.05 * divergence(adv, div_xy2, div_z2, plain_ref[6], plain_ref[2]) - base
    copies = exchange(ops_q.at[pl.ds(0, 1)], None, ones[0], 1, 1)
    vouch(1)
    flights += copies
    for c in range(3):
        adv_ref[c] = adv[c].reshape(8, 16, 128)
    receive(ops_q.at[pl.ds(0, 1)], ones[0], copies, 1)
    hear(1)

    def dot(first, second, scale):
        return jnp.sum(first * second * scale, axis=0, keepdims=True)

    z0 = ops_q[0]
    ops_q[1] = operate(z0)
    copies = exchange(ops_q.at[pl.ds(1, 1)], None, ones[1], 2, 1)
    vouch(2)
    flights += copies
    part[0, 0:1, :] = dot(z0, z0, inverse_mult)
    part[0, 6:8, :] = jnp.zeros((2, 128), jnp.float32)
    receive(ops_q.at[pl.ds(1, 1)], ones[1], copies, 1)
    hear(2)
    z1 = ops_q[1]
    ops_q[2] = operate(z1)
    copies = exchange(ops_q.at[pl.ds(2, 1)], None, ones[2], 3, 1)
    vouch(3)
    flights += copies
    part[0, 1:2, :] = dot(z0, z1, inverse_mult)
    part[0, 2:3, :] = dot(z1, z1, inverse_mult)
    receive(ops_q.at[pl.ds(2, 1)], ones[2], copies, 1)
    hear(3)
    z2 = ops_q[2]
    last = operate(z2)
    part[0, 3:4, :] = dot(z1, z2, inverse_mult)
    part[0, 4:5, :] = dot(z2, z2, inverse_mult)
    part[0, 5:6, :] = dot(z2, last, local_half)

    slot = 0
    for index, stage in enumerate(stages):
        copies_in = []
        for k, who in enumerate(stage):
            copies_in.append(
                pltpu.make_async_remote_copy(
                    src_ref=part.at[index],
                    dst_ref=got.at[slot + k],
                    send_sem=tree_send.at[slot + k],
                    recv_sem=tree_recv.at[slot + k],
                    device_id=who,
                    device_id_type=MESH,
                )
            )
        for copy in copies_in:
            copy.start()
        if index == 0:
            ops_q[3] = last
            copies = exchange(ops_q.at[pl.ds(3, 1)], None, ones[3], 4, 1)
            flights += copies
        for copy in copies_in:
            copy.wait_recv()
        total = part[index]
        for k in range(len(stage)):
            total = total + got[slot + k]
        if index < 1:
            part[index + 1] = total
        flights += copies_in
        slot += len(stage)

    receive(ops_q.at[pl.ds(3, 1)], ones[3], copies, 1)
    sums = jnp.broadcast_to(jnp.sum(total, axis=1, keepdims=True), (8, 128))
    g00, g01, g11, g12, g22, g23 = (sums[k : k + 1, :] for k in range(6))
    h00 = g01 + SHIFT * g00
    h01 = g11 + SHIFT * g01
    h11 = g12 + SHIFT * g11
    h02 = g12 + SHIFT * g11
    h12 = g22 + SHIFT * g12
    h22 = g23 + SHIFT * g22
    over = 1.0 / h00
    l10, l20 = h01 * over, h02 * over
    d1 = h11 - l10 * h01
    e1 = h12 - l10 * h02
    over1 = 1.0 / d1
    l21 = e1 * over1
    d2 = h22 - l20 * h02 - l21 * e1
    b1 = g01 - l10 * g00
    b2 = g11 - l20 * g00 - l21 * b1
    c2 = b2 / d2
    c1 = b1 * over1 - l21 * c2
    c0 = g00 * over - l10 * c1 - l20 * c2
    z3 = ops_q[3]
    pres = c0 * z0 + c1 * z1 + c2 * z2
    pres_ref[...] = pres.reshape(8, 16, 128)
    resid = (
        (1.0 - SHIFT * c0) * z0 - (c0 + SHIFT * c1) * z1 - (c1 + SHIFT * c2) * z2 - c2 * z3
    )
    resid_ref[...] = resid.reshape(8, 16, 128)
    for copy in flights:
        copy.wait_send()


def store(*refs):
    sources, targets, sems = refs[:3], refs[3:6], refs[6]
    copies = [
        pltpu.make_async_copy(a, b, sems.at[k]) for k, (a, b) in enumerate(zip(sources, targets))
    ]
    for copy in copies:
        copy.start()
    for copy in copies:
        copy.wait()


def per_device(sizes, velocity, reaction):
    consts = [jnp.asarray(value) for value in tables_for(reaction.shape[2])]
    operands = [velocity, reaction] + consts
    shape_of = jax.ShapeDtypeStruct
    count_x, count_y, low_count = sizes
    trips = (2 * low_count - 1) + (count_x // low_count * count_y // 2 - 1)
    vmem, f32, dma = pltpu.VMEM, jnp.float32, pltpu.SemaphoreType.DMA
    results = pl.pallas_call(
        functools.partial(kernel, sizes),
        out_shape=(
            shape_of(velocity.shape, f32),
            shape_of(reaction.shape, f32),
            shape_of(reaction.shape, f32),
        ),
        in_specs=[pl.BlockSpec(memory_space=pltpu.HBM)] * 7,
        out_specs=(pl.BlockSpec(memory_space=vmem),) * 3,
        scratch_shapes=[vmem(value.shape, value.dtype) for value in operands]
        + [
            dma((7,)),
            vmem((3, 128, 128), f32),
            vmem((4, 128, 128), f32),
            vmem((2, 3, 16, 128), f32),
            vmem((2, 3, 8, 128), f32),
            vmem((4, 8, 128), f32),
            vmem((2, 3, 16, 128), f32),
            vmem((2, 3, 8, 128), f32),
            vmem((4, 8, 128), f32),
            vmem((4, 2, 1, 16, 128), f32),
            vmem((4, 2, 1, 8, 128), f32),
            vmem((4, 4, 8, 128), f32),
            vmem((4, 2, 1, 16, 128), f32),
            vmem((4, 2, 1, 8, 128), f32),
            vmem((4, 4, 8, 128), f32),
            vmem((2, 8, 128), f32),
            vmem((trips, 8, 128), f32),
            dma((5, 8)),
            dma((5, 8)),
            dma((trips,)),
            dma((trips,)),
            pltpu.SemaphoreType.REGULAR((4,)),
        ],
        compiler_params=pltpu.CompilerParams(
            collective_id=0, has_side_effects=True, vmem_limit_bytes=54700 * 1024
        ),
    )(*operands)
    return pl.pallas_call(
        store,
        out_shape=tuple(shape_of(value.shape, f32) for value in results),
        in_specs=[pl.BlockSpec(memory_space=vmem)] * 3,
        out_specs=(pl.BlockSpec(memory_space=pltpu.HBM),) * 3,
        scratch_shapes=[dma((3,))],
        compiler_params=pltpu.CompilerParams(vmem_limit_bytes=1024 * 1024),
    )(*results)


def solution(mesh):
    count_x, count_y = mesh.shape["wide"], mesh.shape["narrow"]
    low_count = 12 if count_x % 12 == 0 else 2
    return jax.shard_map(
        functools.partial(per_device, (count_x, count_y, low_count)),
        mesh=mesh,
        in_specs=(P(None, "wide", "narrow", None), P("wide", "narrow", None)),
        out_specs=(
            P(None, "wide", "narrow", None),
            P("wide", "narrow", None),
            P("wide", "narrow", None),
        ),
        check_vma=False,
    )
```

```python
import functools

import jax
import jax.numpy as jnp
import ml_dtypes
import numpy as np
from jax import lax
from jax.experimental import pallas as pl
from jax.experimental.pallas import tpu as pltpu
from jax.sharding import PartitionSpec as P

MESH = pl.DeviceIdType.MESH
SHIFT = 4.0
SIDES = ((1, 0), (-1, 0), (0, 1), (0, -1), (1, 1), (1, -1), (-1, 1), (-1, -1))


def legendre_pair(order, nodes):
    p_prev = np.ones(nodes.shape)
    p_now = nodes * 1.0
    for k in range(2, order + 1):
        p_next = ((2 * k - 1) * nodes * p_now - (k - 1) * p_prev) / k
        p_prev = p_now
        p_now = p_next
    return (p_now, p_prev)


def spectral_tables():
    degree = 7
    points = degree + 1
    gll_nodes = np.cos(np.pi * np.arange(points) / degree)
    for sweep in range(100):
        p_now, p_prev = legendre_pair(degree, gll_nodes)
        gll_nodes = gll_nodes - (gll_nodes * p_now - p_prev) / ((degree + 1) * p_now)
    gll_nodes = np.sort(gll_nodes)
    legendre_vals, unused_prev = legendre_pair(degree, gll_nodes)
    gll_weights = 2.0 / (degree * (degree + 1) * legendre_vals**2)
    derivative = np.zeros((points, points))
    for row_index in range(points):
        for col_index in range(points):
            if row_index != col_index:
                derivative[row_index, col_index] = legendre_vals[row_index] / (
                    legendre_vals[col_index] * (gll_nodes[row_index] - gll_nodes[col_index])
                )
    derivative[0, 0] = -degree * (degree + 1) / 4.0
    derivative[-1, -1] = degree * (degree + 1) / 4.0
    gauss_nodes = np.cos(np.pi * (np.arange(12) + 0.75) / 12.5)
    for sweep in range(100):
        p_now, p_prev = legendre_pair(12, gauss_nodes)
        slope = 12 * (gauss_nodes * p_now - p_prev) / (gauss_nodes * gauss_nodes - 1.0)
        gauss_nodes = gauss_nodes - p_now / slope
    gauss_nodes = np.sort(gauss_nodes)
    p_now, p_prev = legendre_pair(12, gauss_nodes)
    slope = 12 * (gauss_nodes * p_now - p_prev) / (gauss_nodes * gauss_nodes - 1.0)
    gauss_weights = 2.0 / ((1.0 - gauss_nodes**2) * slope**2)
    interpolate = np.ones((12, points))
    for col_index in range(points):
        for other in range(points):
            if other != col_index:
                interpolate[:, col_index] *= (gauss_nodes - gll_nodes[other]) / (
                    gll_nodes[col_index] - gll_nodes[other]
                )
    return (gll_weights, derivative, gauss_weights, interpolate)


def halves(matrix):
    high = matrix.astype(ml_dtypes.bfloat16)
    low = (matrix - high.astype(np.float64)).astype(ml_dtypes.bfloat16)
    return high, low


def left_factor(matrix):
    high, low = halves(matrix)
    return np.concatenate([high, high, low], axis=1)


def right_factor(matrix):
    high, low = halves(matrix)
    return np.concatenate([high, high, low], axis=0)


def tables_for(len_z):
    weights, deriv, fine_weights, interp = spectral_tables()
    els_z = len_z // 8
    gradint = interp @ deriv
    stiff = deriv.T @ np.diag(weights) @ deriv
    eye2, eye_z = np.eye(2), np.eye(els_z)

    def shared(count):
        total = np.eye(8 * count)
        for k in range(count - 1):
            total[8 * k + 7, 8 * k + 8] = total[8 * k + 8, 8 * k + 7] = 1.0
        return total

    sum_y, sum_z = shared(2), shared(els_z)
    w_x, w_y, w_z = weights, np.tile(weights, 2), np.tile(weights, els_z)
    w_y2, w_z2 = sum_y @ w_y, sum_z @ w_z

    fine_z = np.zeros((len_z, 2 * 16 * els_z))
    back_z = np.zeros((16 * els_z, len_z))
    for e in range(els_z):
        fine_z[8 * e : 8 * e + 8, 16 * e : 16 * e + 12] = interp.T
        first = 16 * els_z + 16 * e
        fine_z[8 * e : 8 * e + 8, first : first + 12] = gradint.T
        back_z[16 * e : 16 * e + 12, 8 * e : 8 * e + 8] = fine_weights[:, None] * interp
    back_z = back_z @ sum_z
    fine_xy = np.concatenate(
        [np.kron(interp, interp), np.kron(gradint, interp), np.kron(interp, gradint)], axis=0
    )
    back = interp.T * fine_weights[None, :]
    back_xy = np.kron(back, back)

    op_xy = np.kron(stiff, np.diag(w_y2)) + np.kron(np.diag(w_x), sum_y @ np.kron(eye2, stiff))
    for row in (0, 15):
        pick = np.zeros((1, 16))
        pick[0, row] = weights[0]
        op_xy = np.concatenate([op_xy, np.kron(stiff, pick)], axis=0)
    op_z = np.kron(eye_z, stiff).T @ sum_z
    weak = np.diag(weights) @ deriv
    div_xy = np.concatenate(
        [np.kron(weak, np.diag(w_y)), np.kron(np.diag(w_x), np.kron(eye2, weak))], axis=1
    )
    div_xy2 = np.concatenate(
        [np.kron(weak, np.diag(w_y2)), np.kron(np.diag(w_x), sum_y @ np.kron(eye2, weak))], axis=1
    )
    div_z = np.kron(eye_z, weak).T
    div_z2 = div_z @ sum_z

    w_xy, w_xy2 = np.kron(w_x, w_y), np.kron(w_x, w_y2)
    half_y = 1.0 / (sum_y @ np.ones(16))
    half_z = 1.0 / (sum_z @ np.ones(len_z))
    ones_x, ones_z = np.ones(8), np.ones(len_z)
    plain = np.stack(
        [
            np.outer(w_xy, w_z),
            np.outer(w_xy, ones_z),
            np.outer(w_xy2, ones_z),
            1.0 / np.outer(w_xy2, w_z2),
            np.outer(np.kron(ones_x, half_y), half_z),
            np.outer(np.ones(128), w_z),
            np.outer(np.ones(128), w_z2),
            np.outer(np.tile(np.concatenate([stiff[0], stiff[7]]), 8), ones_z),
            np.outer(np.tile(w_x, 16), w_z2),
        ]
    ).astype(np.float32)
    from_right = np.concatenate(
        [right_factor(back_z), right_factor(op_z), right_factor(div_z), right_factor(div_z2)], axis=0
    )
    from_left = np.zeros((144, 1920), ml_dtypes.bfloat16)
    from_left[:, :384] = left_factor(op_xy)
    from_left[:128, 384:1152] = left_factor(div_xy)
    from_left[:128, 1152:] = left_factor(div_xy2)
    shapes_xy = np.zeros((496, 432), ml_dtypes.bfloat16)
    shapes_xy[:432, :192] = left_factor(fine_xy)
    shapes_xy[432:] = left_factor(back_xy)
    return (
        right_factor(fine_z),
        shapes_xy,
        from_right,
        from_left,
        plain,
    )


def split(value):
    high = value.astype(jnp.bfloat16)
    low = (value - high.astype(jnp.float32)).astype(jnp.bfloat16)
    return high, low


def stacked(value):
    high, low = split(value)
    return jnp.concatenate([high, low, high], axis=0)


def joined(value):
    high, low = split(value)
    return jnp.concatenate([high, low, high], axis=1)


def mul(first, second):
    return jnp.dot(first, second, preferred_element_type=jnp.float32)


def kernel(
    sizes,
    vel_hbm,
    rea_hbm,
    fine_z_hbm,
    fine_xy_hbm,
    right_hbm,
    left_hbm,
    plain_hbm,
    adv_ref,
    pres_ref,
    resid_ref,
    vel_ref,
    rea_ref,
    fine_z_ref,
    fine_xy_ref,
    right_ref,
    left_ref,
    plain_ref,
    load_sem,
    adv_q,
    ops_q,
    sx3,
    sy3,
    sc3,
    rx3,
    ry3,
    rc3,
    sx1,
    sy1,
    sc1,
    rx1,
    ry1,
    rc1,
    part,
    got,
    send_sem,
    recv_sem,
    tree_send,
    tree_recv,
    word,
    mass_q,
    lines_q,
):
    pairs = (
        (vel_hbm, vel_ref),
        (fine_z_hbm, fine_z_ref),
        (fine_xy_hbm, fine_xy_ref),
        (right_hbm, right_ref),
        (plain_hbm, plain_ref),
        (rea_hbm, rea_ref),
        (left_hbm, left_ref),
    )
    loads = [pltpu.make_async_copy(a, b, load_sem.at[k]) for k, (a, b) in enumerate(pairs)]
    for load in loads:
        load.start()

    count_x, count_y, low_count = sizes
    weights, deriv = spectral_tables()[:2]
    corner_stiff = float((deriv.T @ np.diag(weights) @ deriv)[7, 7])
    high_count = count_x // low_count
    me_x, me_y = lax.axis_index("wide"), lax.axis_index("narrow")
    me_low, me_high = lax.rem(me_x, low_count), me_x // low_count
    me_pair, me_core = me_y // 2, lax.rem(me_y, 2)

    def turn(place, step, count):
        moved = place + step % count
        return jnp.where(moved >= count, moved - count, moved)

    def at_side(side):
        return turn(me_x, side[0], count_x), turn(me_y, side[1], count_y)

    def far_first(count_a, count_b):
        hops = lambda step, count: min(step, count - step)
        steps = [(i, j) for i in range(count_a) for j in range(count_b) if (i, j) != (0, 0)]
        return sorted(steps, key=lambda s: -hops(s[0], count_a) - hops(s[1], count_b))

    stages = (
        [
            (me_high * low_count + turn(me_low, i, low_count), me_pair * 2 + turn(me_core, j, 2))
            for i, j in far_first(low_count, 2)
        ],
        [
            (
                turn(me_high, i, high_count) * low_count + me_low,
                turn(me_pair, j, count_y // 2) * 2 + me_core,
            )
            for i, j in far_first(high_count, count_y // 2)
        ],
    )
    def by_z(step):
        return me_high * low_count + turn(me_low, step, low_count), me_y

    def by_y(step):
        return turn(me_high, step, high_count) * low_count + me_low, me_y

    def by_pair(step):
        return me_x, turn(me_pair, step, count_y // 2) * 2 + me_core

    near = [by_z(1), by_z(-1), by_y(1), by_y(-1), by_pair(1), by_pair(-1)]
    rounds = (
        near[:4],
        [by_z(2), by_z(-2), by_y(2), by_y(-2)],
        [by_z(2), by_z(-2)] + near[4:],
        near[4:] + [(me_x, me_pair * 2 + 1 - me_core)],
    )
    partners = [at_side(side) for side in SIDES] + near

    barrier = pltpu.get_barrier_semaphore()
    for who in partners:
        pl.semaphore_signal(barrier, inc=1, device_id=who, device_id_type=MESH)

    def vouch(index):
        for who in rounds[index]:
            pl.semaphore_signal(word.at[index], inc=1, device_id=who, device_id_type=MESH)

    def hear(index):
        pl.semaphore_wait(word.at[index], len(rounds[index]))

    for load in loads[:3]:
        load.wait()
    parts = []
    for c in range(3):
        for e in range(2):
            parts.append(vel_ref[c, :, 8 * e : 8 * e + 8, :].reshape(64, 128))
    on_z = mul(joined(jnp.concatenate(parts, axis=0)), fine_z_ref[...])
    width = on_z.shape[1] // 2
    products = {}
    for e in range(2):
        fine = []
        for c in range(3):
            first = 64 * (2 * c + e)
            flat = mul(fine_xy_ref[:432, :192], stacked(on_z[first : first + 64, :width]))
            steep = mul(fine_xy_ref[:144, :192], stacked(on_z[first : first + 64, width:]))
            fine.append((flat[:144], flat[144:288], flat[288:], steep))
        for c in range(3):
            products[c, e] = (
                fine[0][0] * fine[c][1] + fine[1][0] * fine[c][2] + fine[2][0] * fine[c][3]
            )
    for load in loads[3:4]:
        load.wait()
    row8 = lax.broadcasted_iota(jnp.int32, (8, 8, 128), 1)
    back_rows = 3 * width
    for c in range(3):
        both = []
        for e in range(2):
            both.append(stacked(mul(joined(products[c, e]), right_ref[:back_rows, :])))
        weak = mul(fine_xy_ref[432:, :], jnp.concatenate(both, axis=1))
        first = weak[:, :128].reshape(8, 8, 128)
        second = weak[:, 128:].reshape(8, 8, 128)
        first, second = (
            first + jnp.where(row8 == 7, pltpu.roll(second, 7, 1), 0.0),
            second + jnp.where(row8 == 0, pltpu.roll(first, 1, 1), 0.0),
        )
        adv_q[c] = jnp.concatenate([first, second], axis=1).reshape(128, 128)

    pl.semaphore_wait(barrier, len(partners))

    has = {1: (me_x > 0, me_y > 0), -1: (me_x < count_x - 1, me_y < count_y - 1)}

    def exchange(q_ref, bufs, index, comps, only_x=False, ends=None, corners=0):
        sx, sy, sc, rx, ry, rc = bufs
        for c in range(comps):
            q = q_ref.at[c]
            sx[0, c] = q[112:128, :]
            sx[1, c] = q[0:16, :]
            if only_x:
                continue
            sy[0, c] = q[pl.ds(15, 8, stride=16), :]
            sy[1, c] = q[pl.ds(0, 8, stride=16), :]
            for k, row in enumerate((127, 112, 15, 0)):
                sc[k, c : c + 1, :] = q[row : row + 1, :]
        if ends is not None:
            for k in range(2):
                sy[k, comps] = ends[k]
        for k in range(4 if corners else 0):
            row = 0 if k >= 2 else 7
            sc[k, comps : comps + 1, :] = ends[k % 2][row : row + 1, :]
        copies = []
        for k, side in enumerate(SIDES[:2] if only_x else SIDES):
            if k < 2:
                source, target = sx.at[k], rx.at[k]
            elif k < 4:
                lines = pl.ds(0, comps if ends is None else comps + 1)
                source, target = sy.at[k - 2, lines], ry.at[k - 2, lines]
            else:
                source, target = sc.at[k - 4], rc.at[k - 4]
            copies.append(
                pltpu.make_async_remote_copy(
                    src_ref=source,
                    dst_ref=target,
                    send_sem=send_sem.at[index, k],
                    recv_sem=recv_sem.at[index, k],
                    device_id=at_side(side),
                    device_id_type=MESH,
                )
            )
        copies = copies[:2] if only_x else copies[4:] + copies[:4]
        for copy in copies:
            copy.start()
        return copies

    row_x = lax.broadcasted_iota(jnp.int32, (8, 128), 0)

    def side_line(bufs, k, c):
        ry, rc = bufs[4], bufs[5]
        low = jnp.where(has[1][0], rc[k, c : c + 1, :], 0.0)
        high = jnp.where(has[-1][0], rc[2 + k, c : c + 1, :], 0.0)
        return ry[k, c] + jnp.where(row_x == 0, low, 0.0) + jnp.where(row_x == 7, high, 0.0)

    ends_y = ((pl.ds(0, 8, stride=16), has[1][1]), (pl.ds(15, 8, stride=16), has[-1][1]))

    def receive(q_ref, bufs, copies, comps, only_x=False):
        rx = bufs[3]
        for copy in copies:
            copy.wait_recv()
        for c in range(comps):
            q = q_ref.at[c]
            q[0:16, :] = q[0:16, :] + jnp.where(has[1][0], rx[0, c], 0.0)
            q[112:128, :] = q[112:128, :] + jnp.where(has[-1][0], rx[1, c], 0.0)
            if only_x:
                continue
            for k, (rows, there) in enumerate(ends_y):
                line = side_line(bufs, k, c)
                q[rows, :] = q[rows, :] + jnp.where(there, line, 0.0)

    three = (sx3, sy3, sc3, rx3, ry3, rc3)
    ones = [tuple(buf.at[k] for buf in (sx1, sy1, sc1, rx1, ry1, rc1)) for k in range(4)]
    copies = exchange(adv_q, three, 0, 3)
    vouch(0)
    flights = list(copies)

    for load in loads[4:]:
        load.wait()
    rows = lax.broadcasted_iota(jnp.int32, (128, 128), 0)
    in_x, in_y = rows // 16, lax.rem(rows, 16)
    lane = lax.broadcasted_iota(jnp.int32, (128, 128), 1)
    in_z = lax.rem(lane, 8)
    cross_x = ((in_x == 0) & has[1][0]) | ((in_x == 7) & has[-1][0])
    cross_y = ((in_y == 0) & has[1][1]) | ((in_y == 15) & has[-1][1])
    cross = jnp.where(cross_x, 0.5, 1.0) * jnp.where(cross_y, 0.5, 1.0)
    local_half = plain_ref[4]
    inverse_mult = cross * local_half
    inverse_mass = plain_ref[3] * cross

    def sum_yz(value):
        up = pltpu.roll(value, 1, 1)
        down = pltpu.roll(value, 127, 1)
        value = value + jnp.where((in_z == 0) & (lane > 0), up, 0.0)
        value = value + jnp.where((in_z == 7) & (lane < 127), down, 0.0)
        up = pltpu.roll(value, 1, 0)
        down = pltpu.roll(value, 127, 0)
        return value + jnp.where(in_y == 8, up, 0.0) + jnp.where(in_y == 7, down, 0.0)

    mass_term = sum_yz(plain_ref[0] * rea_ref[...].reshape(128, 128)) - SHIFT * cross
    vel = [vel_ref[c].reshape(128, 128) for c in range(3)]
    op_xy, div_xy, div_xy2 = (slice(0, 384), slice(384, 1152), slice(1152, 1920))
    op_z, div_z, div_z2 = (slice(back_rows + 384 * k, back_rows + 384 * k + 384) for k in range(3))

    def divergence(field, on_xy, on_z, scale_z, scale_xy):
        flat = mul(left_ref[:128, on_xy], stacked(jnp.concatenate(field[:2], axis=0)))
        return scale_z * flat + scale_xy * mul(joined(field[2]), right_ref[on_z, :])

    base = sum_yz(divergence(vel, div_xy, div_z, plain_ref[5], plain_ref[1]))

    def operate(value):
        flat = mul(left_ref[:128, op_xy], stacked(value))
        along = mul(joined(value), right_ref[op_z, :])
        return plain_ref[6] * flat + plain_ref[2] * along + mass_term * value

    receive(adv_q, three, copies, 3)
    hear(0)
    adv = []
    for c in range(3):
        adv.append(adv_q[c] * inverse_mass)
    ops_q[0] = 0.05 * divergence(adv, div_xy2, div_z2, plain_ref[6], plain_ref[2]) - base
    mass_q[...] = mass_term
    copies = exchange(
        ops_q.at[pl.ds(0, 1)],
        ones[0],
        1,
        1,
        ends=(mass_q[pl.ds(15, 8, stride=16), :], mass_q[pl.ds(0, 8, stride=16), :]),
    )
    vouch(1)
    flights += copies
    for c in range(3):
        adv_ref[c] = adv[c].reshape(8, 16, 128)
    receive(ops_q.at[pl.ds(0, 1)], ones[0], copies, 1)
    hear(1)

    def dot(first, second, scale):
        return jnp.sum(first * second * scale, axis=0, keepdims=True)

    z0 = ops_q[0]
    image = operate(z0)
    ops_q[1] = image
    lines_q[...] = jnp.sum((image * plain_ref[7]).reshape(16, 8, 128), axis=1)
    copies = exchange(
        ops_q.at[pl.ds(1, 1)],
        ones[1],
        2,
        1,
        ends=(lines_q[pl.ds(1, 8, stride=2), :], lines_q[pl.ds(0, 8, stride=2), :]),
        corners=1,
    )
    vouch(2)
    flights += copies
    part[0, 0:1, :] = dot(z0, z0, inverse_mult)
    part[0, 6:8, :] = jnp.zeros((2, 128), jnp.float32)
    both = ((in_y == 0) & has[1][1]) | ((in_y == 15) & has[-1][1])
    twice = plain_ref[2] * jnp.where(both, 2.0, 1.0)
    for k, (rows_k, there) in enumerate(ends_y):
        mass_q[rows_k, :] = mass_q[rows_k, :] + jnp.where(there, ones[0][4][k, 1], 0.0)
    receive(ops_q.at[pl.ds(1, 1)], ones[1], copies, 1)
    hear(2)
    z1 = ops_q[1]
    flat = mul(left_ref[:, op_xy], stacked(z1))
    along = mul(joined(z1), right_ref[op_z, :])
    extra = []
    for k, (rows_k, there) in enumerate(ends_y):
        own = ops_q[1, rows_k, :] - side_line(ones[1], k, 0)
        line = side_line(ones[1], k, 1) + corner_stiff * own
        share = plain_ref[6, 0:8, :] * flat[128 + 8 * k : 136 + 8 * k] + plain_ref[8, 0:8, :] * line
        extra.append(jnp.where(there, share, 0.0))
    ops_q[2] = plain_ref[6] * flat[:128] + twice * along + mass_q[...] * z1
    for k, (rows_k, there) in enumerate(ends_y):
        ops_q[2, rows_k, :] = ops_q[2, rows_k, :] + extra[k]
    copies = exchange(ops_q.at[pl.ds(2, 1)], ones[2], 3, 1, only_x=True)
    vouch(3)
    flights += copies
    part[0, 1:2, :] = dot(z0, z1, inverse_mult)
    part[0, 2:3, :] = dot(z1, z1, inverse_mult)
    receive(ops_q.at[pl.ds(2, 1)], ones[2], copies, 1, only_x=True)
    hear(3)
    z2 = ops_q[2]
    last = operate(z2)
    part[0, 3:4, :] = dot(z1, z2, inverse_mult)
    part[0, 4:5, :] = dot(z2, z2, inverse_mult)
    part[0, 5:6, :] = dot(z2, last, local_half)

    slot = 0
    for index, stage in enumerate(stages):
        copies_in = []
        for k, who in enumerate(stage):
            copies_in.append(
                pltpu.make_async_remote_copy(
                    src_ref=part.at[index],
                    dst_ref=got.at[slot + k],
                    send_sem=tree_send.at[slot + k],
                    recv_sem=tree_recv.at[slot + k],
                    device_id=who,
                    device_id_type=MESH,
                )
            )
        for copy in copies_in:
            copy.start()
        if index == 0:
            ops_q[3] = last
            copies = exchange(ops_q.at[pl.ds(3, 1)], ones[3], 4, 1)
            flights += copies
        for copy in copies_in:
            copy.wait_recv()
        total = part[index]
        for k in range(len(stage)):
            total = total + got[slot + k]
        if index < 1:
            part[index + 1] = total
        flights += copies_in
        slot += len(stage)

    receive(ops_q.at[pl.ds(3, 1)], ones[3], copies, 1)
    sums = jnp.broadcast_to(jnp.sum(total, axis=1, keepdims=True), (8, 128))
    g00, g01, g11, g12, g22, g23 = (sums[k : k + 1, :] for k in range(6))
    h00 = g01 + SHIFT * g00
    h01 = g11 + SHIFT * g01
    h11 = g12 + SHIFT * g11
    h02 = g12 + SHIFT * g11
    h12 = g22 + SHIFT * g12
    h22 = g23 + SHIFT * g22
    over = 1.0 / h00
    l10, l20 = h01 * over, h02 * over
    d1 = h11 - l10 * h01
    e1 = h12 - l10 * h02
    over1 = 1.0 / d1
    l21 = e1 * over1
    d2 = h22 - l20 * h02 - l21 * e1
    b1 = g01 - l10 * g00
    b2 = g11 - l20 * g00 - l21 * b1
    c2 = b2 / d2
    c1 = b1 * over1 - l21 * c2
    c0 = g00 * over - l10 * c1 - l20 * c2
    z3 = ops_q[3]
    pres = c0 * z0 + c1 * z1 + c2 * z2
    pres_ref[...] = pres.reshape(8, 16, 128)
    resid = (
        (1.0 - SHIFT * c0) * z0 - (c0 + SHIFT * c1) * z1 - (c1 + SHIFT * c2) * z2 - c2 * z3
    )
    resid_ref[...] = resid.reshape(8, 16, 128)
    for copy in flights:
        copy.wait_send()


def store(*refs):
    sources, targets, sems = refs[:3], refs[3:6], refs[6]
    copies = [
        pltpu.make_async_copy(a, b, sems.at[k]) for k, (a, b) in enumerate(zip(sources, targets))
    ]
    for copy in copies:
        copy.start()
    for copy in copies:
        copy.wait()


def per_device(sizes, velocity, reaction):
    consts = [jnp.asarray(value) for value in tables_for(reaction.shape[2])]
    operands = [velocity, reaction] + consts
    shape_of = jax.ShapeDtypeStruct
    count_x, count_y, low_count = sizes
    trips = (2 * low_count - 1) + (count_x // low_count * count_y // 2 - 1)
    vmem, f32, dma = pltpu.VMEM, jnp.float32, pltpu.SemaphoreType.DMA
    results = pl.pallas_call(
        functools.partial(kernel, sizes),
        out_shape=(
            shape_of(velocity.shape, f32),
            shape_of(reaction.shape, f32),
            shape_of(reaction.shape, f32),
        ),
        in_specs=[pl.BlockSpec(memory_space=pltpu.HBM)] * 7,
        out_specs=(pl.BlockSpec(memory_space=vmem),) * 3,
        scratch_shapes=[vmem(value.shape, value.dtype) for value in operands]
        + [
            dma((7,)),
            vmem((3, 128, 128), f32),
            vmem((4, 128, 128), f32),
            vmem((2, 3, 16, 128), f32),
            vmem((2, 3, 8, 128), f32),
            vmem((4, 8, 128), f32),
            vmem((2, 3, 16, 128), f32),
            vmem((2, 3, 8, 128), f32),
            vmem((4, 8, 128), f32),
            vmem((4, 2, 1, 16, 128), f32),
            vmem((4, 2, 2, 8, 128), f32),
            vmem((4, 4, 8, 128), f32),
            vmem((4, 2, 1, 16, 128), f32),
            vmem((4, 2, 2, 8, 128), f32),
            vmem((4, 4, 8, 128), f32),
            vmem((2, 8, 128), f32),
            vmem((trips, 8, 128), f32),
            dma((5, 8)),
            dma((5, 8)),
            dma((trips,)),
            dma((trips,)),
            pltpu.SemaphoreType.REGULAR((4,)),
            vmem((128, 128), f32),
            vmem((16, 128), f32),
        ],
        compiler_params=pltpu.CompilerParams(
            collective_id=0, has_side_effects=True, vmem_limit_bytes=54700 * 1024
        ),
    )(*operands)
    return pl.pallas_call(
        store,
        out_shape=tuple(shape_of(value.shape, f32) for value in results),
        in_specs=[pl.BlockSpec(memory_space=vmem)] * 3,
        out_specs=(pl.BlockSpec(memory_space=pltpu.HBM),) * 3,
        scratch_shapes=[dma((3,))],
        compiler_params=pltpu.CompilerParams(vmem_limit_bytes=1024 * 1024),
    )(*results)


def solution(mesh):
    count_x, count_y = mesh.shape["wide"], mesh.shape["narrow"]
    low_count = 12 if count_x % 12 == 0 else 2
    return jax.shard_map(
        functools.partial(per_device, (count_x, count_y, low_count)),
        mesh=mesh,
        in_specs=(P(None, "wide", "narrow", None), P("wide", "narrow", None)),
        out_specs=(
            P(None, "wide", "narrow", None),
            P("wide", "narrow", None),
            P("wide", "narrow", None),
        ),
        check_vma=False,
    )
```

```python
import functools

import jax
import jax.numpy as jnp
import ml_dtypes
import numpy as np
from jax import lax
from jax.experimental import pallas as pl
from jax.experimental.pallas import tpu as pltpu
from jax.sharding import PartitionSpec as P

MESH = pl.DeviceIdType.MESH
SHIFT = 4.0
SIDES = ((1, 0), (-1, 0), (0, 1), (0, -1), (1, 1), (1, -1), (-1, 1), (-1, -1))
FAR = ((2, 0), (-2, 0), (2, 1), (2, -1), (-2, 1), (-2, -1))


def legendre_pair(order, nodes):
    p_prev = np.ones(nodes.shape)
    p_now = nodes * 1.0
    for k in range(2, order + 1):
        p_next = ((2 * k - 1) * nodes * p_now - (k - 1) * p_prev) / k
        p_prev = p_now
        p_now = p_next
    return (p_now, p_prev)


def spectral_tables():
    degree = 7
    points = degree + 1
    gll_nodes = np.cos(np.pi * np.arange(points) / degree)
    for sweep in range(100):
        p_now, p_prev = legendre_pair(degree, gll_nodes)
        gll_nodes = gll_nodes - (gll_nodes * p_now - p_prev) / ((degree + 1) * p_now)
    gll_nodes = np.sort(gll_nodes)
    legendre_vals, unused_prev = legendre_pair(degree, gll_nodes)
    gll_weights = 2.0 / (degree * (degree + 1) * legendre_vals**2)
    derivative = np.zeros((points, points))
    for row_index in range(points):
        for col_index in range(points):
            if row_index != col_index:
                derivative[row_index, col_index] = legendre_vals[row_index] / (
                    legendre_vals[col_index] * (gll_nodes[row_index] - gll_nodes[col_index])
                )
    derivative[0, 0] = -degree * (degree + 1) / 4.0
    derivative[-1, -1] = degree * (degree + 1) / 4.0
    gauss_nodes = np.cos(np.pi * (np.arange(12) + 0.75) / 12.5)
    for sweep in range(100):
        p_now, p_prev = legendre_pair(12, gauss_nodes)
        slope = 12 * (gauss_nodes * p_now - p_prev) / (gauss_nodes * gauss_nodes - 1.0)
        gauss_nodes = gauss_nodes - p_now / slope
    gauss_nodes = np.sort(gauss_nodes)
    p_now, p_prev = legendre_pair(12, gauss_nodes)
    slope = 12 * (gauss_nodes * p_now - p_prev) / (gauss_nodes * gauss_nodes - 1.0)
    gauss_weights = 2.0 / ((1.0 - gauss_nodes**2) * slope**2)
    interpolate = np.ones((12, points))
    for col_index in range(points):
        for other in range(points):
            if other != col_index:
                interpolate[:, col_index] *= (gauss_nodes - gll_nodes[other]) / (
                    gll_nodes[col_index] - gll_nodes[other]
                )
    return (gll_weights, derivative, gauss_weights, interpolate)


def halves(matrix):
    high = matrix.astype(ml_dtypes.bfloat16)
    low = (matrix - high.astype(np.float64)).astype(ml_dtypes.bfloat16)
    return high, low


def left_factor(matrix):
    high, low = halves(matrix)
    return np.concatenate([high, high, low], axis=1)


def right_factor(matrix):
    high, low = halves(matrix)
    return np.concatenate([high, high, low], axis=0)


def tables_for(len_z):
    weights, deriv, fine_weights, interp = spectral_tables()
    els_z = len_z // 8
    gradint = interp @ deriv
    stiff = deriv.T @ np.diag(weights) @ deriv
    eye2, eye_z = np.eye(2), np.eye(els_z)

    def shared(count):
        total = np.eye(8 * count)
        for k in range(count - 1):
            total[8 * k + 7, 8 * k + 8] = total[8 * k + 8, 8 * k + 7] = 1.0
        return total

    sum_y, sum_z = shared(2), shared(els_z)
    w_x, w_y, w_z = weights, np.tile(weights, 2), np.tile(weights, els_z)
    w_y2, w_z2 = sum_y @ w_y, sum_z @ w_z

    fine_z = np.zeros((len_z, 2 * 16 * els_z))
    back_z = np.zeros((16 * els_z, len_z))
    for e in range(els_z):
        fine_z[8 * e : 8 * e + 8, 16 * e : 16 * e + 12] = interp.T
        first = 16 * els_z + 16 * e
        fine_z[8 * e : 8 * e + 8, first : first + 12] = gradint.T
        back_z[16 * e : 16 * e + 12, 8 * e : 8 * e + 8] = fine_weights[:, None] * interp
    back_z = back_z @ sum_z
    fine_xy = np.concatenate(
        [np.kron(interp, interp), np.kron(gradint, interp), np.kron(interp, gradint)], axis=0
    )
    back = interp.T * fine_weights[None, :]
    back_xy = np.kron(back, back)

    op_xy = np.kron(stiff, np.diag(w_y2)) + np.kron(np.diag(w_x), sum_y @ np.kron(eye2, stiff))
    op_apart = np.concatenate(
        [np.kron(stiff, np.eye(16)), np.kron(np.eye(8), sum_y @ np.kron(eye2, stiff))], axis=0
    )
    op_z = np.kron(eye_z, stiff).T @ sum_z
    weak = np.diag(weights) @ deriv
    div_xy = np.concatenate(
        [np.kron(weak, np.diag(w_y)), np.kron(np.diag(w_x), np.kron(eye2, weak))], axis=1
    )
    div_xy2 = np.concatenate(
        [np.kron(weak, np.diag(w_y2)), np.kron(np.diag(w_x), sum_y @ np.kron(eye2, weak))], axis=1
    )
    div_z = np.kron(eye_z, weak).T
    div_z2 = div_z @ sum_z

    w_xy, w_xy2 = np.kron(w_x, w_y), np.kron(w_x, w_y2)
    half_y = 1.0 / (sum_y @ np.ones(16))
    half_z = 1.0 / (sum_z @ np.ones(len_z))
    ones_x, ones_z = np.ones(8), np.ones(len_z)
    plain = np.stack(
        [
            np.outer(w_xy, w_z),
            np.outer(w_xy, ones_z),
            np.outer(w_xy2, ones_z),
            1.0 / np.outer(w_xy2, w_z2),
            np.outer(np.kron(ones_x, half_y), half_z),
            np.outer(np.ones(128), w_z),
            np.outer(np.ones(128), w_z2),
            np.outer(np.tile(np.concatenate([stiff[0], stiff[7]]), 8), ones_z),
            np.outer(np.kron(w_x, np.ones(16)), w_z2),
            np.outer(np.kron(ones_x, w_y2), w_z2),
        ]
    ).astype(np.float32)
    from_right = np.concatenate(
        [right_factor(back_z), right_factor(op_z), right_factor(div_z), right_factor(div_z2)], axis=0
    )
    from_left = np.zeros((256, 2304), ml_dtypes.bfloat16)
    from_left[:128, :384] = left_factor(op_xy)
    from_left[:128, 384:1152] = left_factor(div_xy)
    from_left[:128, 1152:1920] = left_factor(div_xy2)
    from_left[:, 1920:] = left_factor(op_apart)
    shapes_xy = np.zeros((496, 432), ml_dtypes.bfloat16)
    shapes_xy[:432, :192] = left_factor(fine_xy)
    shapes_xy[432:] = left_factor(back_xy)
    return (
        right_factor(fine_z),
        shapes_xy,
        from_right,
        from_left,
        plain,
    )


def split(value):
    high = value.astype(jnp.bfloat16)
    low = (value - high.astype(jnp.float32)).astype(jnp.bfloat16)
    return high, low


def stacked(value):
    high, low = split(value)
    return jnp.concatenate([high, low, high], axis=0)


def joined(value):
    high, low = split(value)
    return jnp.concatenate([high, low, high], axis=1)


def mul(first, second):
    return jnp.dot(first, second, preferred_element_type=jnp.float32)


def kernel(
    sizes,
    vel_hbm,
    rea_hbm,
    fine_z_hbm,
    fine_xy_hbm,
    right_hbm,
    left_hbm,
    plain_hbm,
    adv_ref,
    pres_ref,
    resid_ref,
    vel_ref,
    rea_ref,
    fine_z_ref,
    fine_xy_ref,
    right_ref,
    left_ref,
    plain_ref,
    load_sem,
    adv_q,
    ops_q,
    sx3,
    sy3,
    sc3,
    rx3,
    ry3,
    rc3,
    sx1,
    sy1,
    sc1,
    rx1,
    ry1,
    rc1,
    part,
    got,
    send_sem,
    recv_sem,
    tree_send,
    tree_recv,
    word,
    mass_q,
    local_mass,
    lines_q,
    sums_x,
    sums_y,
    far_x,
    far_c,
):
    pairs = (
        (vel_hbm, vel_ref),
        (fine_z_hbm, fine_z_ref),
        (fine_xy_hbm, fine_xy_ref),
        (right_hbm, right_ref),
        (plain_hbm, plain_ref),
        (rea_hbm, rea_ref),
        (left_hbm, left_ref),
    )
    loads = [pltpu.make_async_copy(a, b, load_sem.at[k]) for k, (a, b) in enumerate(pairs)]
    for load in loads:
        load.start()

    count_x, count_y, low_count = sizes
    weights, deriv = spectral_tables()[:2]
    stiff = [[float(v) for v in row] for row in deriv.T @ np.diag(weights) @ deriv]
    high_count = count_x // low_count
    me_x, me_y = lax.axis_index("wide"), lax.axis_index("narrow")
    me_low, me_high = lax.rem(me_x, low_count), me_x // low_count
    me_pair, me_core = me_y // 2, lax.rem(me_y, 2)

    def turn(place, step, count):
        moved = place + step % count
        return jnp.where(moved >= count, moved - count, moved)

    def at_side(side):
        return turn(me_x, side[0], count_x), turn(me_y, side[1], count_y)

    def far_first(count_a, count_b):
        hops = lambda step, count: min(step, count - step)
        steps = [(i, j) for i in range(count_a) for j in range(count_b) if (i, j) != (0, 0)]
        return sorted(steps, key=lambda s: -hops(s[0], count_a) - hops(s[1], count_b))

    stages = (
        [
            (me_high * low_count + turn(me_low, i, low_count), me_pair * 2 + turn(me_core, j, 2))
            for i, j in far_first(low_count, 2)
        ],
        [
            (
                turn(me_high, i, high_count) * low_count + me_low,
                turn(me_pair, j, count_y // 2) * 2 + me_core,
            )
            for i, j in far_first(high_count, count_y // 2)
        ],
    )
    def by_z(step):
        return me_high * low_count + turn(me_low, step, low_count), me_y

    def by_y(step):
        return turn(me_high, step, high_count) * low_count + me_low, me_y

    def by_pair(step):
        return me_x, turn(me_pair, step, count_y // 2) * 2 + me_core

    near = [by_z(1), by_z(-1), by_y(1), by_y(-1), by_pair(1), by_pair(-1)]
    rounds = (
        near[:4],
        [by_z(2), by_z(-2), by_y(2), by_y(-2)],
        [by_z(2), by_z(-2)] + near[4:],
        near[4:] + [(me_x, me_pair * 2 + 1 - me_core)],
    )
    partners = [at_side(side) for side in SIDES] + near

    barrier = pltpu.get_barrier_semaphore()
    for who in partners:
        pl.semaphore_signal(barrier, inc=1, device_id=who, device_id_type=MESH)

    def vouch(index):
        for who in rounds[index]:
            pl.semaphore_signal(word.at[index], inc=1, device_id=who, device_id_type=MESH)

    def hear(index):
        pl.semaphore_wait(word.at[index], len(rounds[index]))

    for load in loads[:3]:
        load.wait()
    parts = []
    for c in range(3):
        for e in range(2):
            parts.append(vel_ref[c, :, 8 * e : 8 * e + 8, :].reshape(64, 128))
    on_z = mul(joined(jnp.concatenate(parts, axis=0)), fine_z_ref[...])
    width = on_z.shape[1] // 2
    products = {}
    for e in range(2):
        fine = []
        for c in range(3):
            first = 64 * (2 * c + e)
            flat = mul(fine_xy_ref[:432, :192], stacked(on_z[first : first + 64, :width]))
            steep = mul(fine_xy_ref[:144, :192], stacked(on_z[first : first + 64, width:]))
            fine.append((flat[:144], flat[144:288], flat[288:], steep))
        for c in range(3):
            products[c, e] = (
                fine[0][0] * fine[c][1] + fine[1][0] * fine[c][2] + fine[2][0] * fine[c][3]
            )
    for load in loads[3:4]:
        load.wait()
    row8 = lax.broadcasted_iota(jnp.int32, (8, 8, 128), 1)
    back_rows = 3 * width
    for c in range(3):
        both = []
        for e in range(2):
            both.append(stacked(mul(joined(products[c, e]), right_ref[:back_rows, :])))
        weak = mul(fine_xy_ref[432:, :], jnp.concatenate(both, axis=1))
        first = weak[:, :128].reshape(8, 8, 128)
        second = weak[:, 128:].reshape(8, 8, 128)
        first, second = (
            first + jnp.where(row8 == 7, pltpu.roll(second, 7, 1), 0.0),
            second + jnp.where(row8 == 0, pltpu.roll(first, 1, 1), 0.0),
        )
        adv_q[c] = jnp.concatenate([first, second], axis=1).reshape(128, 128)

    pl.semaphore_wait(barrier, len(partners))

    has = {1: (me_x > 0, me_y > 0), -1: (me_x < count_x - 1, me_y < count_y - 1)}

    def pack(q, bufs, c):
        sx, sy, sc = bufs[:3]
        sx[0, c] = q[112:128, :]
        sx[1, c] = q[0:16, :]
        sy[0, c] = q[pl.ds(15, 8, stride=16), :]
        sy[1, c] = q[pl.ds(0, 8, stride=16), :]
        for k, row in enumerate((127, 112, 15, 0)):
            sc[k, c : c + 1, :] = q[row : row + 1, :]

    def launch(bufs, index, comps, far=False):
        sx, sy, sc, rx, ry, rc = bufs
        used = pl.ds(0, comps)
        moves = []
        for k in range(4):
            moves.append((SIDES[4 + k], sc.at[k], rc.at[k]))
        if far:
            for k in range(4):
                moves.append((FAR[2 + k], sc.at[k], far_c.at[k]))
            for k in range(2):
                moves.append((FAR[k], sx.at[k, 0], far_x.at[k]))
        for k in range(2):
            moves.append((SIDES[k], sx.at[k, used], rx.at[k, used]))
        for k in range(2):
            moves.append((SIDES[2 + k], sy.at[k, used], ry.at[k, used]))
        copies = []
        for k, (side, source, target) in enumerate(moves):
            copy = pltpu.make_async_remote_copy(
                src_ref=source,
                dst_ref=target,
                send_sem=send_sem.at[index, k],
                recv_sem=recv_sem.at[index, k],
                device_id=at_side(side),
                device_id_type=MESH,
            )
            copy.start()
            copies.append(copy)
        return copies

    row_x = lax.broadcasted_iota(jnp.int32, (8, 128), 0)

    def side_line(bufs, k, c):
        ry, rc = bufs[4], bufs[5]
        low = jnp.where(has[1][0], rc[k, c : c + 1, :], 0.0)
        high = jnp.where(has[-1][0], rc[2 + k, c : c + 1, :], 0.0)
        return ry[k, c] + jnp.where(row_x == 0, low, 0.0) + jnp.where(row_x == 7, high, 0.0)

    ends_y = ((pl.ds(0, 8, stride=16), has[1][1]), (pl.ds(15, 8, stride=16), has[-1][1]))

    row_y = lax.broadcasted_iota(jnp.int32, (16, 128), 0)

    def side_face(face, corner, k, row):
        low = jnp.where(has[1][1], corner[2 * k, row : row + 1, :], 0.0)
        high = jnp.where(has[-1][1], corner[2 * k + 1, row : row + 1, :], 0.0)
        return face + jnp.where(row_y == 0, low, 0.0) + jnp.where(row_y == 15, high, 0.0)

    ends_x = ((slice(0, 16), has[1][0]), (slice(112, 128), has[-1][0]))

    def receive(fields, bufs, copies):
        rx = bufs[3]
        for copy in copies:
            copy.wait_recv()
        for c, q in enumerate(fields):
            for k, (rows, there) in enumerate(ends_x):
                q[rows, :] = q[rows, :] + jnp.where(there, rx[k, c], 0.0)
            for k, (rows, there) in enumerate(ends_y):
                q[rows, :] = q[rows, :] + jnp.where(there, side_line(bufs, k, c), 0.0)

    three = (sx3, sy3, sc3, rx3, ry3, rc3)
    ones = [tuple(buf.at[k] for buf in (sx1, sy1, sc1, rx1, ry1, rc1)) for k in range(3)]
    for c in range(3):
        pack(adv_q.at[c], three, c)
    copies = launch(three, 0, 3)
    vouch(0)
    flights = list(copies)

    for load in loads[4:]:
        load.wait()
    rows = lax.broadcasted_iota(jnp.int32, (128, 128), 0)
    in_x, in_y = rows // 16, lax.rem(rows, 16)
    lane = lax.broadcasted_iota(jnp.int32, (128, 128), 1)
    in_z = lax.rem(lane, 8)
    cross_x = ((in_x == 0) & has[1][0]) | ((in_x == 7) & has[-1][0])
    cross_y = ((in_y == 0) & has[1][1]) | ((in_y == 15) & has[-1][1])
    cross = jnp.where(cross_x, 0.5, 1.0) * jnp.where(cross_y, 0.5, 1.0)
    twice_x, twice_y = jnp.where(cross_x, 2.0, 1.0), jnp.where(cross_y, 2.0, 1.0)
    scale_y = plain_ref[8] * twice_x
    scale_x = plain_ref[9] * twice_y
    scale_z = plain_ref[2] * twice_x * twice_y
    local_half = plain_ref[4]
    inverse_mult = cross * local_half
    inverse_mass = plain_ref[3] * cross

    def sum_yz(value):
        up = pltpu.roll(value, 1, 1)
        down = pltpu.roll(value, 127, 1)
        value = value + jnp.where((in_z == 0) & (lane > 0), up, 0.0)
        value = value + jnp.where((in_z == 7) & (lane < 127), down, 0.0)
        up = pltpu.roll(value, 1, 0)
        down = pltpu.roll(value, 127, 0)
        return value + jnp.where(in_y == 8, up, 0.0) + jnp.where(in_y == 7, down, 0.0)

    mass_q[...] = sum_yz(plain_ref[0] * rea_ref[...].reshape(128, 128)) - SHIFT * cross
    vel = [vel_ref[c].reshape(128, 128) for c in range(3)]
    local_mass[...] = mass_q[...]
    op_xy, div_xy, div_xy2 = (slice(0, 384), slice(384, 1152), slice(1152, 1920))
    op_apart = slice(1920, 2304)
    op_z, div_z, div_z2 = (slice(back_rows + 384 * k, back_rows + 384 * k + 384) for k in range(3))

    def divergence(field, on_xy, on_z, scale_z, scale_xy):
        flat = mul(left_ref[:128, on_xy], stacked(jnp.concatenate(field[:2], axis=0)))
        return scale_z * flat + scale_xy * mul(joined(field[2]), right_ref[on_z, :])

    base = sum_yz(divergence(vel, div_xy, div_z, plain_ref[5], plain_ref[1]))

    def operate(value):
        flat = mul(left_ref[:128, op_xy], stacked(value))
        along = mul(joined(value), right_ref[op_z, :])
        return plain_ref[6] * flat + plain_ref[2] * along + local_mass[...] * value

    hear(0)
    vouch(1)
    receive([adv_q.at[c] for c in range(3)], three, copies)
    adv = []
    for c in range(3):
        adv.append(adv_q[c] * inverse_mass)
    ops_q[0] = 0.05 * divergence(adv, div_xy2, div_z2, plain_ref[6], plain_ref[2]) - base
    pack(ops_q.at[0], ones[0], 0)
    pack(mass_q, ones[0], 1)
    copies = launch(ones[0], 1, 2)
    flights += copies
    hear(1)
    vouch(2)
    for c in range(3):
        adv_ref[c] = adv[c].reshape(8, 16, 128)
    receive([ops_q.at[0], mass_q], ones[0], copies)
    hear(2)

    def dot(first, second, scale):
        return jnp.sum(first * second * scale, axis=0, keepdims=True)

    z0 = ops_q[0]
    image = operate(z0)
    ops_q[1] = image
    pack(ops_q.at[1], ones[1], 0)
    sx, sy, sc = ones[1][:3]
    lines_q[...] = jnp.sum((image * plain_ref[7]).reshape(16, 8, 128), axis=1)
    for k, end in ((0, 7), (1, 0)):
        face = stiff[end][0] * image[0:16]
        for i in range(1, 8):
            face = face + stiff[end][i] * image[16 * i : 16 * i + 16]
        sx[k, 1] = face
        sc[2 * k, 2:3, :] = face[15:16]
        sc[2 * k + 1, 2:3, :] = face[0:1]
        line = lines_q[pl.ds(1 - k, 8, stride=2), :]
        sy[k, 1] = line
        sc[k, 1:2, :] = line[7:8]
        sc[2 + k, 1:2, :] = line[0:1]
    copies = launch(ones[1], 2, 2, far=True)
    flights += copies
    vouch(3)
    part[0, 0:1, :] = dot(z0, z0, inverse_mult)
    part[0, 6:8, :] = jnp.zeros((2, 128), jnp.float32)
    receive([ops_q.at[1]], ones[1], copies)
    hear(3)
    z1 = ops_q[1]
    rx, ry, rc = ones[1][3:]
    apart = mul(left_ref[:, op_apart], stacked(z1))
    along = mul(joined(z1), right_ref[op_z, :])
    sums_x[...] = apart[:128]
    sums_y[...] = apart[128:]
    two = (me_x > 1, me_x < count_x - 2)
    for k, (rows_k, there) in enumerate(ends_x):
        mine = ops_q[1, rows_k, :] - side_face(rx[k, 0], rc, k, 0)
        other = jnp.where(two[k], side_face(far_x[k], far_c, k, 0), 0.0)
        face = side_face(rx[k, 1], rc, k, 2) + stiff[7][7] * mine + stiff[7][0] * other
        sums_x[rows_k, :] = sums_x[rows_k, :] + jnp.where(there, face, 0.0)
    for k, (rows_k, there) in enumerate(ends_y):
        mine = ops_q[1, rows_k, :] - side_line(ones[1], k, 0)
        line = side_line(ones[1], k, 1) + stiff[7][7] * mine
        sums_y[rows_k, :] = sums_y[rows_k, :] + jnp.where(there, line, 0.0)
    z2 = scale_x * sums_x[...] + scale_y * sums_y[...] + scale_z * along + mass_q[...] * z1
    ops_q[2] = z2
    part[0, 1:2, :] = dot(z0, z1, inverse_mult)
    part[0, 2:3, :] = dot(z1, z1, inverse_mult)
    last = operate(z2)
    part[0, 3:4, :] = dot(z1, z2, inverse_mult)
    part[0, 4:5, :] = dot(z2, z2, inverse_mult)
    part[0, 5:6, :] = dot(z2, last, local_half)

    slot = 0
    for index, stage in enumerate(stages):
        copies_in = []
        for k, who in enumerate(stage):
            copies_in.append(
                pltpu.make_async_remote_copy(
                    src_ref=part.at[index],
                    dst_ref=got.at[slot + k],
                    send_sem=tree_send.at[slot + k],
                    recv_sem=tree_recv.at[slot + k],
                    device_id=who,
                    device_id_type=MESH,
                )
            )
        for copy in copies_in:
            copy.start()
        if index == 0:
            ops_q[3] = last
            pack(ops_q.at[3], ones[2], 0)
            copies = launch(ones[2], 3, 1)
            flights += copies
        for copy in copies_in:
            copy.wait_recv()
        total = part[index]
        for k in range(len(stage)):
            total = total + got[slot + k]
        if index < 1:
            part[index + 1] = total
        flights += copies_in
        slot += len(stage)

    receive([ops_q.at[3]], ones[2], copies)
    sums = jnp.broadcast_to(jnp.sum(total, axis=1, keepdims=True), (8, 128))
    g00, g01, g11, g12, g22, g23 = (sums[k : k + 1, :] for k in range(6))
    h00 = g01 + SHIFT * g00
    h01 = g11 + SHIFT * g01
    h11 = g12 + SHIFT * g11
    h02 = g12 + SHIFT * g11
    h12 = g22 + SHIFT * g12
    h22 = g23 + SHIFT * g22
    over = 1.0 / h00
    l10, l20 = h01 * over, h02 * over
    d1 = h11 - l10 * h01
    e1 = h12 - l10 * h02
    over1 = 1.0 / d1
    l21 = e1 * over1
    d2 = h22 - l20 * h02 - l21 * e1
    b1 = g01 - l10 * g00
    b2 = g11 - l20 * g00 - l21 * b1
    c2 = b2 / d2
    c1 = b1 * over1 - l21 * c2
    c0 = g00 * over - l10 * c1 - l20 * c2
    z3 = ops_q[3]
    pres = c0 * z0 + c1 * z1 + c2 * z2
    pres_ref[...] = pres.reshape(8, 16, 128)
    resid = (
        (1.0 - SHIFT * c0) * z0 - (c0 + SHIFT * c1) * z1 - (c1 + SHIFT * c2) * z2 - c2 * z3
    )
    resid_ref[...] = resid.reshape(8, 16, 128)
    for copy in flights:
        copy.wait_send()


def store(*refs):
    sources, targets, sems = refs[:3], refs[3:6], refs[6]
    copies = [
        pltpu.make_async_copy(a, b, sems.at[k]) for k, (a, b) in enumerate(zip(sources, targets))
    ]
    for copy in copies:
        copy.start()
    for copy in copies:
        copy.wait()


def per_device(sizes, velocity, reaction):
    consts = [jnp.asarray(value) for value in tables_for(reaction.shape[2])]
    operands = [velocity, reaction] + consts
    shape_of = jax.ShapeDtypeStruct
    count_x, count_y, low_count = sizes
    trips = (2 * low_count - 1) + (count_x // low_count * count_y // 2 - 1)
    vmem, f32, dma = pltpu.VMEM, jnp.float32, pltpu.SemaphoreType.DMA
    results = pl.pallas_call(
        functools.partial(kernel, sizes),
        out_shape=(
            shape_of(velocity.shape, f32),
            shape_of(reaction.shape, f32),
            shape_of(reaction.shape, f32),
        ),
        in_specs=[pl.BlockSpec(memory_space=pltpu.HBM)] * 7,
        out_specs=(pl.BlockSpec(memory_space=vmem),) * 3,
        scratch_shapes=[vmem(value.shape, value.dtype) for value in operands]
        + [
            dma((7,)),
            vmem((3, 128, 128), f32),
            vmem((4, 128, 128), f32),
            vmem((2, 3, 16, 128), f32),
            vmem((2, 3, 8, 128), f32),
            vmem((4, 8, 128), f32),
            vmem((2, 3, 16, 128), f32),
            vmem((2, 3, 8, 128), f32),
            vmem((4, 8, 128), f32),
            vmem((3, 2, 2, 16, 128), f32),
            vmem((3, 2, 2, 8, 128), f32),
            vmem((3, 4, 8, 128), f32),
            vmem((3, 2, 2, 16, 128), f32),
            vmem((3, 2, 2, 8, 128), f32),
            vmem((3, 4, 8, 128), f32),
            vmem((2, 8, 128), f32),
            vmem((trips, 8, 128), f32),
            dma((4, 14)),
            dma((4, 14)),
            dma((trips,)),
            dma((trips,)),
            pltpu.SemaphoreType.REGULAR((4,)),
            vmem((128, 128), f32),
            vmem((128, 128), f32),
            vmem((16, 128), f32),
            vmem((128, 128), f32),
            vmem((128, 128), f32),
            vmem((2, 16, 128), f32),
            vmem((4, 8, 128), f32),
        ],
        compiler_params=pltpu.CompilerParams(
            collective_id=0, has_side_effects=True, vmem_limit_bytes=54700 * 1024
        ),
    )(*operands)
    return pl.pallas_call(
        store,
        out_shape=tuple(shape_of(value.shape, f32) for value in results),
        in_specs=[pl.BlockSpec(memory_space=vmem)] * 3,
        out_specs=(pl.BlockSpec(memory_space=pltpu.HBM),) * 3,
        scratch_shapes=[dma((3,))],
        compiler_params=pltpu.CompilerParams(vmem_limit_bytes=1024 * 1024),
    )(*results)


def solution(mesh):
    count_x, count_y = mesh.shape["wide"], mesh.shape["narrow"]
    low_count = 12 if count_x % 12 == 0 else 2
    return jax.shard_map(
        functools.partial(per_device, (count_x, count_y, low_count)),
        mesh=mesh,
        in_specs=(P(None, "wide", "narrow", None), P("wide", "narrow", None)),
        out_specs=(
            P(None, "wide", "narrow", None),
            P("wide", "narrow", None),
            P("wide", "narrow", None),
        ),
        check_vma=False,
    )
```

```python
import functools

import jax
import jax.numpy as jnp
import ml_dtypes
import numpy as np
from jax import lax
from jax.experimental import pallas as pl
from jax.experimental.pallas import tpu as pltpu
from jax.sharding import PartitionSpec as P

MESH = pl.DeviceIdType.MESH
SHIFT = 4.0
SIDES = ((1, 0), (-1, 0), (0, 1), (0, -1), (1, 1), (1, -1), (-1, 1), (-1, -1))
FAR = ((2, 0), (-2, 0), (2, 1), (2, -1), (-2, 1), (-2, -1))


def legendre_pair(order, nodes):
    p_prev = np.ones(nodes.shape)
    p_now = nodes * 1.0
    for k in range(2, order + 1):
        p_next = ((2 * k - 1) * nodes * p_now - (k - 1) * p_prev) / k
        p_prev = p_now
        p_now = p_next
    return (p_now, p_prev)


def spectral_tables():
    degree = 7
    points = degree + 1
    gll_nodes = np.cos(np.pi * np.arange(points) / degree)
    for sweep in range(100):
        p_now, p_prev = legendre_pair(degree, gll_nodes)
        gll_nodes = gll_nodes - (gll_nodes * p_now - p_prev) / ((degree + 1) * p_now)
    gll_nodes = np.sort(gll_nodes)
    legendre_vals, unused_prev = legendre_pair(degree, gll_nodes)
    gll_weights = 2.0 / (degree * (degree + 1) * legendre_vals**2)
    derivative = np.zeros((points, points))
    for row_index in range(points):
        for col_index in range(points):
            if row_index != col_index:
                derivative[row_index, col_index] = legendre_vals[row_index] / (
                    legendre_vals[col_index] * (gll_nodes[row_index] - gll_nodes[col_index])
                )
    derivative[0, 0] = -degree * (degree + 1) / 4.0
    derivative[-1, -1] = degree * (degree + 1) / 4.0
    gauss_nodes = np.cos(np.pi * (np.arange(12) + 0.75) / 12.5)
    for sweep in range(100):
        p_now, p_prev = legendre_pair(12, gauss_nodes)
        slope = 12 * (gauss_nodes * p_now - p_prev) / (gauss_nodes * gauss_nodes - 1.0)
        gauss_nodes = gauss_nodes - p_now / slope
    gauss_nodes = np.sort(gauss_nodes)
    p_now, p_prev = legendre_pair(12, gauss_nodes)
    slope = 12 * (gauss_nodes * p_now - p_prev) / (gauss_nodes * gauss_nodes - 1.0)
    gauss_weights = 2.0 / ((1.0 - gauss_nodes**2) * slope**2)
    interpolate = np.ones((12, points))
    for col_index in range(points):
        for other in range(points):
            if other != col_index:
                interpolate[:, col_index] *= (gauss_nodes - gll_nodes[other]) / (
                    gll_nodes[col_index] - gll_nodes[other]
                )
    return (gll_weights, derivative, gauss_weights, interpolate)


def halves(matrix):
    high = matrix.astype(ml_dtypes.bfloat16)
    low = (matrix - high.astype(np.float64)).astype(ml_dtypes.bfloat16)
    return high, low


def left_factor(matrix):
    high, low = halves(matrix)
    return np.concatenate([high, high, low], axis=1)


def right_factor(matrix):
    high, low = halves(matrix)
    return np.concatenate([high, high, low], axis=0)


def tables_for(len_z):
    weights, deriv, fine_weights, interp = spectral_tables()
    els_z = len_z // 8
    gradint = interp @ deriv
    stiff = deriv.T @ np.diag(weights) @ deriv
    eye2, eye_z = np.eye(2), np.eye(els_z)

    def shared(count):
        total = np.eye(8 * count)
        for k in range(count - 1):
            total[8 * k + 7, 8 * k + 8] = total[8 * k + 8, 8 * k + 7] = 1.0
        return total

    sum_y, sum_z = shared(2), shared(els_z)
    w_x, w_y, w_z = weights, np.tile(weights, 2), np.tile(weights, els_z)
    w_y2, w_z2 = sum_y @ w_y, sum_z @ w_z

    fine_z = np.zeros((len_z, 2 * 16 * els_z))
    back_z = np.zeros((16 * els_z, len_z))
    for e in range(els_z):
        fine_z[8 * e : 8 * e + 8, 16 * e : 16 * e + 12] = interp.T
        first = 16 * els_z + 16 * e
        fine_z[8 * e : 8 * e + 8, first : first + 12] = gradint.T
        back_z[16 * e : 16 * e + 12, 8 * e : 8 * e + 8] = fine_weights[:, None] * interp
    back_z = back_z @ sum_z
    fine_xy = np.concatenate(
        [np.kron(interp, interp), np.kron(gradint, interp), np.kron(interp, gradint)], axis=0
    )
    back = interp.T * fine_weights[None, :]
    back_xy = np.kron(back, back)

    op_xy = np.kron(stiff, np.diag(w_y2)) + np.kron(np.diag(w_x), sum_y @ np.kron(eye2, stiff))
    op_apart = np.concatenate(
        [np.kron(stiff, np.eye(16)), np.kron(np.eye(8), sum_y @ np.kron(eye2, stiff))], axis=0
    )
    op_z = np.kron(eye_z, stiff).T @ sum_z
    weak = np.diag(weights) @ deriv
    div_xy = np.concatenate(
        [np.kron(weak, np.diag(w_y)), np.kron(np.diag(w_x), np.kron(eye2, weak))], axis=1
    )
    div_x = np.kron(weak, np.eye(16))
    div_y = np.kron(np.eye(8), sum_y @ np.kron(eye2, weak))
    div_z = np.kron(eye_z, weak).T
    div_z2 = div_z @ sum_z

    w_xy, w_xy2 = np.kron(w_x, w_y), np.kron(w_x, w_y2)
    half_y = 1.0 / (sum_y @ np.ones(16))
    half_z = 1.0 / (sum_z @ np.ones(len_z))
    ones_x, ones_z = np.ones(8), np.ones(len_z)
    plain = np.stack(
        [
            np.outer(w_xy, w_z),
            np.outer(w_xy, ones_z),
            np.outer(w_xy2, ones_z),
            1.0 / np.outer(w_xy2, w_z2),
            np.outer(np.kron(ones_x, half_y), half_z),
            np.outer(np.ones(128), w_z),
            np.outer(np.ones(128), w_z2),
            np.outer(np.tile(np.concatenate([stiff[0], stiff[7]]), 8), ones_z),
            np.outer(np.kron(w_x, np.ones(16)), w_z2),
            np.outer(np.kron(ones_x, w_y2), w_z2),
            np.outer(np.tile(np.concatenate([weak[0], weak[7]]), 8) / np.kron(ones_x, w_y2), ones_z),
        ]
    ).astype(np.float32)
    from_right = np.concatenate(
        [right_factor(back_z), right_factor(op_z), right_factor(div_z), right_factor(div_z2)], axis=0
    )
    from_left = np.zeros((256, 2304), ml_dtypes.bfloat16)
    from_left[:128, :384] = left_factor(op_xy)
    from_left[:128, 384:1152] = left_factor(div_xy)
    from_left[:128, 1152:1536] = left_factor(div_x)
    from_left[:128, 1536:1920] = left_factor(div_y)
    from_left[:, 1920:] = left_factor(op_apart)
    shapes_xy = np.zeros((496, 432), ml_dtypes.bfloat16)
    shapes_xy[:432, :192] = left_factor(fine_xy)
    shapes_xy[432:] = left_factor(back_xy)
    return (
        right_factor(fine_z),
        shapes_xy,
        from_right,
        from_left,
        plain,
    )


def split(value):
    high = value.astype(jnp.bfloat16)
    low = (value - high.astype(jnp.float32)).astype(jnp.bfloat16)
    return high, low


def stacked(value):
    high, low = split(value)
    return jnp.concatenate([high, low, high], axis=0)


def joined(value):
    high, low = split(value)
    return jnp.concatenate([high, low, high], axis=1)


def mul(first, second):
    return jnp.dot(first, second, preferred_element_type=jnp.float32)


def kernel(
    sizes,
    vel_hbm,
    rea_hbm,
    fine_z_hbm,
    fine_xy_hbm,
    right_hbm,
    left_hbm,
    plain_hbm,
    adv_ref,
    pres_ref,
    resid_ref,
    vel_ref,
    rea_ref,
    fine_z_ref,
    fine_xy_ref,
    right_ref,
    left_ref,
    plain_ref,
    load_sem,
    adv_q,
    ops_q,
    sx3,
    sy3,
    sc3,
    rx3,
    ry3,
    rc3,
    sx1,
    sy1,
    sc1,
    rx1,
    ry1,
    rc1,
    part,
    got,
    send_sem,
    recv_sem,
    tree_send,
    tree_recv,
    word,
    mass_q,
    local_mass,
    lines_q,
    sums_x,
    sums_y,
    far_x,
    far_c,
    inverse_q,
):
    pairs = (
        (vel_hbm, vel_ref),
        (fine_z_hbm, fine_z_ref),
        (fine_xy_hbm, fine_xy_ref),
        (right_hbm, right_ref),
        (plain_hbm, plain_ref),
        (rea_hbm, rea_ref),
        (left_hbm, left_ref),
    )
    loads = [pltpu.make_async_copy(a, b, load_sem.at[k]) for k, (a, b) in enumerate(pairs)]
    for load in loads:
        load.start()

    count_x, count_y, low_count = sizes
    weights, deriv = spectral_tables()[:2]
    stiff = [[float(v) for v in row] for row in deriv.T @ np.diag(weights) @ deriv]
    slope = [[float(v) for v in row] for row in np.diag(weights) @ deriv @ np.diag(1.0 / weights)]
    thick = float(2.0 * weights[0])
    high_count = count_x // low_count
    me_x, me_y = lax.axis_index("wide"), lax.axis_index("narrow")
    me_low, me_high = lax.rem(me_x, low_count), me_x // low_count
    me_pair, me_core = me_y // 2, lax.rem(me_y, 2)

    def turn(place, step, count):
        moved = place + step % count
        return jnp.where(moved >= count, moved - count, moved)

    def at_side(side):
        return turn(me_x, side[0], count_x), turn(me_y, side[1], count_y)

    def far_first(count_a, count_b):
        hops = lambda step, count: min(step, count - step)
        steps = [(i, j) for i in range(count_a) for j in range(count_b) if (i, j) != (0, 0)]
        return sorted(steps, key=lambda s: -hops(s[0], count_a) - hops(s[1], count_b))

    stages = (
        [
            (me_high * low_count + turn(me_low, i, low_count), me_pair * 2 + turn(me_core, j, 2))
            for i, j in far_first(low_count, 2)
        ],
        [
            (
                turn(me_high, i, high_count) * low_count + me_low,
                turn(me_pair, j, count_y // 2) * 2 + me_core,
            )
            for i, j in far_first(high_count, count_y // 2)
        ],
    )
    def by_z(step):
        return me_high * low_count + turn(me_low, step, low_count), me_y

    def by_y(step):
        return turn(me_high, step, high_count) * low_count + me_low, me_y

    def by_pair(step):
        return me_x, turn(me_pair, step, count_y // 2) * 2 + me_core

    near = [by_z(1), by_z(-1), by_y(1), by_y(-1), by_pair(1), by_pair(-1)]
    rounds = (
        near[:4],
        [by_z(2), by_z(-2), by_y(2), by_y(-2)],
        [by_z(2), by_z(-2)] + near[4:],
        near[4:] + [(me_x, me_pair * 2 + 1 - me_core)],
    )
    partners = [at_side(side) for side in SIDES + FAR] + near

    barrier = pltpu.get_barrier_semaphore()
    for who in partners:
        pl.semaphore_signal(barrier, inc=1, device_id=who, device_id_type=MESH)

    def vouch(index):
        for who in rounds[index]:
            pl.semaphore_signal(word.at[index], inc=1, device_id=who, device_id_type=MESH)

    def hear(index):
        pl.semaphore_wait(word.at[index], len(rounds[index]))

    for load in loads[:3]:
        load.wait()
    parts = []
    for c in range(3):
        for e in range(2):
            parts.append(vel_ref[c, :, 8 * e : 8 * e + 8, :].reshape(64, 128))
    on_z = mul(joined(jnp.concatenate(parts, axis=0)), fine_z_ref[...])
    width = on_z.shape[1] // 2
    products = {}
    for e in range(2):
        fine = []
        for c in range(3):
            first = 64 * (2 * c + e)
            flat = mul(fine_xy_ref[:432, :192], stacked(on_z[first : first + 64, :width]))
            steep = mul(fine_xy_ref[:144, :192], stacked(on_z[first : first + 64, width:]))
            fine.append((flat[:144], flat[144:288], flat[288:], steep))
        for c in range(3):
            products[c, e] = (
                fine[0][0] * fine[c][1] + fine[1][0] * fine[c][2] + fine[2][0] * fine[c][3]
            )
    for load in loads[3:4]:
        load.wait()
    row8 = lax.broadcasted_iota(jnp.int32, (8, 8, 128), 1)
    back_rows = 3 * width
    for c in range(3):
        both = []
        for e in range(2):
            both.append(stacked(mul(joined(products[c, e]), right_ref[:back_rows, :])))
        weak = mul(fine_xy_ref[432:, :], jnp.concatenate(both, axis=1))
        first = weak[:, :128].reshape(8, 8, 128)
        second = weak[:, 128:].reshape(8, 8, 128)
        first, second = (
            first + jnp.where(row8 == 7, pltpu.roll(second, 7, 1), 0.0),
            second + jnp.where(row8 == 0, pltpu.roll(first, 1, 1), 0.0),
        )
        adv_q[c] = jnp.concatenate([first, second], axis=1).reshape(128, 128)

    pl.semaphore_wait(barrier, len(partners))

    has = {1: (me_x > 0, me_y > 0), -1: (me_x < count_x - 1, me_y < count_y - 1)}
    for load in loads[4:]:
        load.wait()

    rows = lax.broadcasted_iota(jnp.int32, (128, 128), 0)
    in_x, in_y = rows // 16, lax.rem(rows, 16)
    lane = lax.broadcasted_iota(jnp.int32, (128, 128), 1)
    in_z = lax.rem(lane, 8)
    cross_x = ((in_x == 0) & has[1][0]) | ((in_x == 7) & has[-1][0])
    cross_y = ((in_y == 0) & has[1][1]) | ((in_y == 15) & has[-1][1])
    cross = jnp.where(cross_x, 0.5, 1.0) * jnp.where(cross_y, 0.5, 1.0)
    twice_x, twice_y = jnp.where(cross_x, 2.0, 1.0), jnp.where(cross_y, 2.0, 1.0)
    scale_y = plain_ref[8] * twice_x
    scale_x = plain_ref[9] * twice_y
    scale_z = plain_ref[2] * twice_x * twice_y

    def pack(q, bufs, c):
        sx, sy, sc = bufs[:3]
        sx[0, c] = q[112:128, :]
        sx[1, c] = q[0:16, :]
        sy[0, c] = q[pl.ds(15, 8, stride=16), :]
        sy[1, c] = q[pl.ds(0, 8, stride=16), :]
        for k, row in enumerate((127, 112, 15, 0)):
            sc[k, c : c + 1, :] = q[row : row + 1, :]

    def attach(bufs, c, k, face):
        sx, sy, sc = bufs[:3]
        sx[k, c] = face
        sc[2 * k, c + 1 : c + 2, :] = face[15:16]
        sc[2 * k + 1, c + 1 : c + 2, :] = face[0:1]
        line = lines_q[pl.ds(1 - k, 8, stride=2), :]
        sy[k, c] = line
        sc[k, c : c + 1, :] = line[7:8]
        sc[2 + k, c : c + 1, :] = line[0:1]

    def launch(bufs, index, comps, far=None):
        sx, sy, sc, rx, ry, rc = bufs
        used = pl.ds(0, comps)
        moves = []
        for k in range(4):
            moves.append((SIDES[4 + k], sc.at[k], rc.at[k]))
        if far is not None:
            for k in range(4):
                moves.append((FAR[2 + k], sc.at[k], far_c.at[far, k]))
            for k in range(2):
                moves.append((FAR[k], sx.at[k, 0], far_x.at[far, k]))
        for k in range(2):
            moves.append((SIDES[k], sx.at[k, used], rx.at[k, used]))
        for k in range(2):
            moves.append((SIDES[2 + k], sy.at[k, used], ry.at[k, used]))
        copies = []
        for k, (side, source, target) in enumerate(moves):
            copy = pltpu.make_async_remote_copy(
                src_ref=source,
                dst_ref=target,
                send_sem=send_sem.at[index, k],
                recv_sem=recv_sem.at[index, k],
                device_id=at_side(side),
                device_id_type=MESH,
            )
            copy.start()
            copies.append(copy)
        return copies

    row_x = lax.broadcasted_iota(jnp.int32, (8, 128), 0)

    def side_line(bufs, k, c):
        ry, rc = bufs[4], bufs[5]
        low = jnp.where(has[1][0], rc[k, c : c + 1, :], 0.0)
        high = jnp.where(has[-1][0], rc[2 + k, c : c + 1, :], 0.0)
        return ry[k, c] + jnp.where(row_x == 0, low, 0.0) + jnp.where(row_x == 7, high, 0.0)

    ends_y = ((pl.ds(0, 8, stride=16), has[1][1]), (pl.ds(15, 8, stride=16), has[-1][1]))

    row_y = lax.broadcasted_iota(jnp.int32, (16, 128), 0)

    def side_face(face, corner, k, row):
        low = jnp.where(has[1][1], corner[2 * k, row : row + 1, :], 0.0)
        high = jnp.where(has[-1][1], corner[2 * k + 1, row : row + 1, :], 0.0)
        return face + jnp.where(row_y == 0, low, 0.0) + jnp.where(row_y == 15, high, 0.0)

    ends_x = ((slice(0, 16), has[1][0]), (slice(112, 128), has[-1][0]))

    def receive(fields, bufs, copies):
        rx = bufs[3]
        for copy in copies:
            copy.wait_recv()
        for c, q in enumerate(fields):
            for k, (rows, there) in enumerate(ends_x):
                q[rows, :] = q[rows, :] + jnp.where(there, rx[k, c], 0.0)
            for k, (rows, there) in enumerate(ends_y):
                q[rows, :] = q[rows, :] + jnp.where(there, side_line(bufs, k, c), 0.0)

    three = (sx3, sy3, sc3, rx3, ry3, rc3)
    ones = [tuple(buf.at[k] for buf in (sx1, sy1, sc1, rx1, ry1, rc1)) for k in range(3)]
    for c in range(3):
        pack(adv_q.at[c], three, c)
    lines_q[...] = jnp.sum(
        (adv_q[1] * plain_ref[10] * jnp.where(cross_y, 0.5, 1.0)).reshape(16, 8, 128), axis=1
    )
    outer = (jnp.where(has[1][0], 0.5, 1.0), jnp.where(has[-1][0], 0.5, 1.0))
    for k, end in ((0, 7), (1, 0)):
        face = (slope[end][0] * outer[0]) * adv_q[0, 0:16, :]
        face = face + (slope[end][7] * outer[1]) * adv_q[0, 112:128, :]
        for i in range(1, 7):
            face = face + slope[end][i] * adv_q[0, 16 * i : 16 * i + 16, :]
        attach(three, 3, k, face)
    copies = launch(three, 0, 4, far=0)
    vouch(0)
    flights = list(copies)

    local_half = plain_ref[4]
    inverse_mult = cross * local_half
    inverse_mass = plain_ref[3] * cross

    def sum_yz(value):
        up = pltpu.roll(value, 1, 1)
        down = pltpu.roll(value, 127, 1)
        value = value + jnp.where((in_z == 0) & (lane > 0), up, 0.0)
        value = value + jnp.where((in_z == 7) & (lane < 127), down, 0.0)
        up = pltpu.roll(value, 1, 0)
        down = pltpu.roll(value, 127, 0)
        return value + jnp.where(in_y == 8, up, 0.0) + jnp.where(in_y == 7, down, 0.0)

    mass_q[...] = sum_yz(plain_ref[0] * rea_ref[...].reshape(128, 128)) - SHIFT * cross
    vel = [vel_ref[c].reshape(128, 128) for c in range(3)]
    local_mass[...] = mass_q[...]
    op_xy, div_xy = slice(0, 384), slice(384, 1152)
    div_x, div_y = slice(1152, 1536), slice(1536, 1920)
    op_apart = slice(1920, 2304)
    op_z, div_z, div_z2 = (slice(back_rows + 384 * k, back_rows + 384 * k + 384) for k in range(3))

    def divergence(field, on_xy, on_z, scale_z, scale_xy):
        flat = mul(left_ref[:128, on_xy], stacked(jnp.concatenate(field[:2], axis=0)))
        return scale_z * flat + scale_xy * mul(joined(field[2]), right_ref[on_z, :])

    base = sum_yz(divergence(vel, div_xy, div_z, plain_ref[5], plain_ref[1]))

    def operate(value):
        flat = mul(left_ref[:128, op_xy], stacked(value))
        along = mul(joined(value), right_ref[op_z, :])
        return plain_ref[6] * flat + plain_ref[2] * along + local_mass[...] * value

    ops_q[0] = base
    pack(ops_q.at[0], ones[0], 0)
    pack(mass_q, ones[0], 1)
    later = launch(ones[0], 1, 2)
    flights += later
    hear(0)
    vouch(1)
    inverse_q[...] = inverse_mass
    two = (me_x > 1, me_x < count_x - 2)
    receive([adv_q.at[c] for c in range(3)], three, copies)
    adv = []
    for c in range(3):
        adv.append(adv_q[c] * inverse_mass)
    sums_x[...] = mul(left_ref[:128, div_x], stacked(adv[0]))
    sums_y[...] = mul(left_ref[:128, div_y], stacked(adv[1]))
    along = mul(joined(adv[2]), right_ref[div_z2, :])
    rx, ry, rc = three[3:]
    for k, (rows_k, there) in enumerate(ends_x):
        near_end, far_end = 7 - 7 * k, 7 * k
        mine = adv_q[0, rows_k, :] - side_face(rx[k, 0], rc, k, 0)
        other = jnp.where(two[k], side_face(far_x[0, k], far_c[0], k, 0), 0.0)
        face = side_face(rx[k, 3], rc, k, 4)
        face = face + (0.5 * slope[near_end][near_end]) * mine
        face = face + (0.5 * slope[near_end][far_end]) * other
        face = face * (thick * inverse_q[rows_k, :])
        sums_x[rows_k, :] = sums_x[rows_k, :] + jnp.where(there, face, 0.0)
    for k, (rows_k, there) in enumerate(ends_y):
        near_end = 7 - 7 * k
        mine = adv_q[1, rows_k, :] - side_line(three, k, 1)
        line = side_line(three, k, 3) + (0.5 * slope[near_end][near_end]) * mine
        line = line * (thick * inverse_q[rows_k, :])
        sums_y[rows_k, :] = sums_y[rows_k, :] + jnp.where(there, line, 0.0)
    receive([ops_q.at[0], mass_q], ones[0], later)
    hear(1)
    vouch(2)
    z0 = 0.05 * (scale_x * sums_x[...] + scale_y * sums_y[...] + scale_z * along) - ops_q[0]

    def dot(first, second, scale):
        return jnp.sum(first * second * scale, axis=0, keepdims=True)

    image = operate(z0)
    ops_q[1] = image
    pack(ops_q.at[1], ones[1], 0)
    lines_q[...] = jnp.sum((image * plain_ref[7]).reshape(16, 8, 128), axis=1)
    for k, end in ((0, 7), (1, 0)):
        face = stiff[end][0] * image[0:16]
        for i in range(1, 8):
            face = face + stiff[end][i] * image[16 * i : 16 * i + 16]
        attach(ones[1], 1, k, face)
    copies = launch(ones[1], 2, 2, far=1)
    flights += copies
    hear(2)
    vouch(3)
    for c in range(3):
        adv_ref[c] = adv[c].reshape(8, 16, 128)
    part[0, 0:1, :] = dot(z0, z0, inverse_mult)
    part[0, 6:8, :] = jnp.zeros((2, 128), jnp.float32)
    receive([ops_q.at[1]], ones[1], copies)
    hear(3)
    z1 = ops_q[1]
    rx, ry, rc = ones[1][3:]
    apart = mul(left_ref[:, op_apart], stacked(z1))
    along = mul(joined(z1), right_ref[op_z, :])
    sums_x[...] = apart[:128]
    sums_y[...] = apart[128:]
    for k, (rows_k, there) in enumerate(ends_x):
        mine = ops_q[1, rows_k, :] - side_face(rx[k, 0], rc, k, 0)
        other = jnp.where(two[k], side_face(far_x[1, k], far_c[1], k, 0), 0.0)
        face = side_face(rx[k, 1], rc, k, 2) + stiff[7][7] * mine + stiff[7][0] * other
        sums_x[rows_k, :] = sums_x[rows_k, :] + jnp.where(there, face, 0.0)
    for k, (rows_k, there) in enumerate(ends_y):
        mine = ops_q[1, rows_k, :] - side_line(ones[1], k, 0)
        line = side_line(ones[1], k, 1) + stiff[7][7] * mine
        sums_y[rows_k, :] = sums_y[rows_k, :] + jnp.where(there, line, 0.0)
    z2 = scale_x * sums_x[...] + scale_y * sums_y[...] + scale_z * along + mass_q[...] * z1
    ops_q[2] = z2
    part[0, 1:2, :] = dot(z0, z1, inverse_mult)
    part[0, 2:3, :] = dot(z1, z1, inverse_mult)
    last = operate(z2)
    part[0, 3:4, :] = dot(z1, z2, inverse_mult)
    part[0, 4:5, :] = dot(z2, z2, inverse_mult)
    part[0, 5:6, :] = dot(z2, last, local_half)

    slot = 0
    for index, stage in enumerate(stages):
        copies_in = []
        for k, who in enumerate(stage):
            copies_in.append(
                pltpu.make_async_remote_copy(
                    src_ref=part.at[index],
                    dst_ref=got.at[slot + k],
                    send_sem=tree_send.at[slot + k],
                    recv_sem=tree_recv.at[slot + k],
                    device_id=who,
                    device_id_type=MESH,
                )
            )
        for copy in copies_in:
            copy.start()
        if index == 0:
            ops_q[3] = last
            pack(ops_q.at[3], ones[2], 0)
            copies = launch(ones[2], 3, 1)
            flights += copies
        for copy in copies_in:
            copy.wait_recv()
        total = part[index]
        for k in range(len(stage)):
            total = total + got[slot + k]
        if index < 1:
            part[index + 1] = total
        flights += copies_in
        slot += len(stage)

    receive([ops_q.at[3]], ones[2], copies)
    sums = jnp.broadcast_to(jnp.sum(total, axis=1, keepdims=True), (8, 128))
    g00, g01, g11, g12, g22, g23 = (sums[k : k + 1, :] for k in range(6))
    h00 = g01 + SHIFT * g00
    h01 = g11 + SHIFT * g01
    h11 = g12 + SHIFT * g11
    h02 = g12 + SHIFT * g11
    h12 = g22 + SHIFT * g12
    h22 = g23 + SHIFT * g22
    over = 1.0 / h00
    l10, l20 = h01 * over, h02 * over
    d1 = h11 - l10 * h01
    e1 = h12 - l10 * h02
    over1 = 1.0 / d1
    l21 = e1 * over1
    d2 = h22 - l20 * h02 - l21 * e1
    b1 = g01 - l10 * g00
    b2 = g11 - l20 * g00 - l21 * b1
    c2 = b2 / d2
    c1 = b1 * over1 - l21 * c2
    c0 = g00 * over - l10 * c1 - l20 * c2
    z3 = ops_q[3]
    pres = c0 * z0 + c1 * z1 + c2 * z2
    pres_ref[...] = pres.reshape(8, 16, 128)
    resid = (
        (1.0 - SHIFT * c0) * z0 - (c0 + SHIFT * c1) * z1 - (c1 + SHIFT * c2) * z2 - c2 * z3
    )
    resid_ref[...] = resid.reshape(8, 16, 128)
    for copy in flights:
        copy.wait_send()


def store(*refs):
    sources, targets, sems = refs[:3], refs[3:6], refs[6]
    copies = [
        pltpu.make_async_copy(a, b, sems.at[k]) for k, (a, b) in enumerate(zip(sources, targets))
    ]
    for copy in copies:
        copy.start()
    for copy in copies:
        copy.wait()


def per_device(sizes, velocity, reaction):
    consts = [jnp.asarray(value) for value in tables_for(reaction.shape[2])]
    operands = [velocity, reaction] + consts
    shape_of = jax.ShapeDtypeStruct
    count_x, count_y, low_count = sizes
    trips = (2 * low_count - 1) + (count_x // low_count * count_y // 2 - 1)
    vmem, f32, dma = pltpu.VMEM, jnp.float32, pltpu.SemaphoreType.DMA
    results = pl.pallas_call(
        functools.partial(kernel, sizes),
        out_shape=(
            shape_of(velocity.shape, f32),
            shape_of(reaction.shape, f32),
            shape_of(reaction.shape, f32),
        ),
        in_specs=[pl.BlockSpec(memory_space=pltpu.HBM)] * 7,
        out_specs=(pl.BlockSpec(memory_space=vmem),) * 3,
        scratch_shapes=[vmem(value.shape, value.dtype) for value in operands]
        + [
            dma((7,)),
            vmem((3, 128, 128), f32),
            vmem((4, 128, 128), f32),
            vmem((2, 4, 16, 128), f32),
            vmem((2, 4, 8, 128), f32),
            vmem((4, 8, 128), f32),
            vmem((2, 4, 16, 128), f32),
            vmem((2, 4, 8, 128), f32),
            vmem((4, 8, 128), f32),
            vmem((3, 2, 2, 16, 128), f32),
            vmem((3, 2, 2, 8, 128), f32),
            vmem((3, 4, 8, 128), f32),
            vmem((3, 2, 2, 16, 128), f32),
            vmem((3, 2, 2, 8, 128), f32),
            vmem((3, 4, 8, 128), f32),
            vmem((2, 8, 128), f32),
            vmem((trips, 8, 128), f32),
            dma((4, 14)),
            dma((4, 14)),
            dma((trips,)),
            dma((trips,)),
            pltpu.SemaphoreType.REGULAR((4,)),
            vmem((128, 128), f32),
            vmem((128, 128), f32),
            vmem((16, 128), f32),
            vmem((128, 128), f32),
            vmem((128, 128), f32),
            vmem((2, 2, 16, 128), f32),
            vmem((2, 4, 8, 128), f32),
            vmem((128, 128), f32),
        ],
        compiler_params=pltpu.CompilerParams(
            collective_id=0, has_side_effects=True, vmem_limit_bytes=54700 * 1024
        ),
    )(*operands)
    return pl.pallas_call(
        store,
        out_shape=tuple(shape_of(value.shape, f32) for value in results),
        in_specs=[pl.BlockSpec(memory_space=vmem)] * 3,
        out_specs=(pl.BlockSpec(memory_space=pltpu.HBM),) * 3,
        scratch_shapes=[dma((3,))],
        compiler_params=pltpu.CompilerParams(vmem_limit_bytes=1024 * 1024),
    )(*results)


def solution(mesh):
    count_x, count_y = mesh.shape["wide"], mesh.shape["narrow"]
    low_count = 12 if count_x % 12 == 0 else 2
    return jax.shard_map(
        functools.partial(per_device, (count_x, count_y, low_count)),
        mesh=mesh,
        in_specs=(P(None, "wide", "narrow", None), P("wide", "narrow", None)),
        out_specs=(
            P(None, "wide", "narrow", None),
            P("wide", "narrow", None),
            P("wide", "narrow", None),
        ),
        check_vma=False,
    )
```

```python
import functools

import jax
import jax.numpy as jnp
import ml_dtypes
import numpy as np
from jax import lax
from jax.experimental import pallas as pl
from jax.experimental.pallas import tpu as pltpu
from jax.sharding import PartitionSpec as P

MESH = pl.DeviceIdType.MESH
SHIFT = 4.0
SIDES = ((1, 0), (-1, 0), (0, 1), (0, -1), (1, 1), (1, -1), (-1, 1), (-1, -1))
FAR = ((2, 0), (-2, 0), (2, 1), (2, -1), (-2, 1), (-2, -1))


def legendre_pair(order, nodes):
    p_prev = np.ones(nodes.shape)
    p_now = nodes * 1.0
    for k in range(2, order + 1):
        p_next = ((2 * k - 1) * nodes * p_now - (k - 1) * p_prev) / k
        p_prev = p_now
        p_now = p_next
    return (p_now, p_prev)


def spectral_tables():
    degree = 7
    points = degree + 1
    gll_nodes = np.cos(np.pi * np.arange(points) / degree)
    for sweep in range(100):
        p_now, p_prev = legendre_pair(degree, gll_nodes)
        gll_nodes = gll_nodes - (gll_nodes * p_now - p_prev) / ((degree + 1) * p_now)
    gll_nodes = np.sort(gll_nodes)
    legendre_vals, unused_prev = legendre_pair(degree, gll_nodes)
    gll_weights = 2.0 / (degree * (degree + 1) * legendre_vals**2)
    derivative = np.zeros((points, points))
    for row_index in range(points):
        for col_index in range(points):
            if row_index != col_index:
                derivative[row_index, col_index] = legendre_vals[row_index] / (
                    legendre_vals[col_index] * (gll_nodes[row_index] - gll_nodes[col_index])
                )
    derivative[0, 0] = -degree * (degree + 1) / 4.0
    derivative[-1, -1] = degree * (degree + 1) / 4.0
    gauss_nodes = np.cos(np.pi * (np.arange(12) + 0.75) / 12.5)
    for sweep in range(100):
        p_now, p_prev = legendre_pair(12, gauss_nodes)
        slope = 12 * (gauss_nodes * p_now - p_prev) / (gauss_nodes * gauss_nodes - 1.0)
        gauss_nodes = gauss_nodes - p_now / slope
    gauss_nodes = np.sort(gauss_nodes)
    p_now, p_prev = legendre_pair(12, gauss_nodes)
    slope = 12 * (gauss_nodes * p_now - p_prev) / (gauss_nodes * gauss_nodes - 1.0)
    gauss_weights = 2.0 / ((1.0 - gauss_nodes**2) * slope**2)
    interpolate = np.ones((12, points))
    for col_index in range(points):
        for other in range(points):
            if other != col_index:
                interpolate[:, col_index] *= (gauss_nodes - gll_nodes[other]) / (
                    gll_nodes[col_index] - gll_nodes[other]
                )
    return (gll_weights, derivative, gauss_weights, interpolate)


def halves(matrix):
    high = matrix.astype(ml_dtypes.bfloat16)
    low = (matrix - high.astype(np.float64)).astype(ml_dtypes.bfloat16)
    return high, low


def left_factor(matrix):
    high, low = halves(matrix)
    return np.concatenate([high, high, low], axis=1)


def right_factor(matrix):
    high, low = halves(matrix)
    return np.concatenate([high, high, low], axis=0)


def tables_for(len_z):
    weights, deriv, fine_weights, interp = spectral_tables()
    els_z = len_z // 8
    gradint = interp @ deriv
    stiff = deriv.T @ np.diag(weights) @ deriv
    eye2, eye_z = np.eye(2), np.eye(els_z)

    def shared(count):
        total = np.eye(8 * count)
        for k in range(count - 1):
            total[8 * k + 7, 8 * k + 8] = total[8 * k + 8, 8 * k + 7] = 1.0
        return total

    sum_y, sum_z = shared(2), shared(els_z)
    w_x, w_y, w_z = weights, np.tile(weights, 2), np.tile(weights, els_z)
    w_y2, w_z2 = sum_y @ w_y, sum_z @ w_z

    fine_z = np.zeros((len_z, 2 * 16 * els_z))
    back_z = np.zeros((16 * els_z, len_z))
    for e in range(els_z):
        fine_z[8 * e : 8 * e + 8, 16 * e : 16 * e + 12] = interp.T
        first = 16 * els_z + 16 * e
        fine_z[8 * e : 8 * e + 8, first : first + 12] = gradint.T
        back_z[16 * e : 16 * e + 12, 8 * e : 8 * e + 8] = fine_weights[:, None] * interp
    back_z = back_z @ sum_z
    fine_xy = np.concatenate(
        [np.kron(interp, interp), np.kron(gradint, interp), np.kron(interp, gradint)], axis=0
    )
    back = interp.T * fine_weights[None, :]
    back_xy = np.kron(back, back)

    op_xy = np.kron(stiff, np.diag(w_y2)) + np.kron(np.diag(w_x), sum_y @ np.kron(eye2, stiff))
    op_apart = np.concatenate(
        [np.kron(stiff, np.eye(16)), np.kron(np.eye(8), sum_y @ np.kron(eye2, stiff))], axis=0
    )
    op_z = np.kron(eye_z, stiff).T @ sum_z
    weak = np.diag(weights) @ deriv
    div_xy = np.concatenate(
        [np.kron(weak, np.diag(w_y)), np.kron(np.diag(w_x), np.kron(eye2, weak))], axis=1
    )
    div_x = np.kron(weak, np.eye(16))
    div_y = np.kron(np.eye(8), sum_y @ np.kron(eye2, weak))
    div_z = np.kron(eye_z, weak).T
    div_z2 = div_z @ sum_z

    w_xy, w_xy2 = np.kron(w_x, w_y), np.kron(w_x, w_y2)
    half_y = 1.0 / (sum_y @ np.ones(16))
    half_z = 1.0 / (sum_z @ np.ones(len_z))
    ones_x, ones_z = np.ones(8), np.ones(len_z)
    plain = np.stack(
        [
            np.outer(w_xy, w_z),
            np.outer(w_xy, ones_z),
            np.outer(w_xy2, ones_z),
            1.0 / np.outer(w_xy2, w_z2),
            np.outer(np.kron(ones_x, half_y), half_z),
            np.outer(np.ones(128), w_z),
            np.outer(np.ones(128), w_z2),
            np.outer(np.tile(np.concatenate([stiff[0], stiff[7]]), 8), ones_z),
            np.outer(np.kron(w_x, np.ones(16)), w_z2),
            np.outer(np.kron(ones_x, w_y2), w_z2),
            np.outer(np.tile(np.concatenate([weak[0], weak[7]]), 8) / np.kron(ones_x, w_y2), ones_z),
        ]
    ).astype(np.float32)
    from_right = np.concatenate(
        [right_factor(back_z), right_factor(op_z), right_factor(div_z), right_factor(div_z2)], axis=0
    )
    from_left = np.zeros((256, 2304), ml_dtypes.bfloat16)
    from_left[:128, :384] = left_factor(op_xy)
    from_left[:128, 384:1152] = left_factor(div_xy)
    from_left[:128, 1152:1536] = left_factor(div_x)
    from_left[:128, 1536:1920] = left_factor(div_y)
    from_left[:, 1920:] = left_factor(op_apart)
    shapes_xy = np.zeros((496, 432), ml_dtypes.bfloat16)
    shapes_xy[:432, :192] = left_factor(fine_xy)
    shapes_xy[432:] = left_factor(back_xy)
    return (
        right_factor(fine_z),
        shapes_xy,
        from_right,
        from_left,
        plain,
    )


def split(value):
    high = value.astype(jnp.bfloat16)
    low = (value - high.astype(jnp.float32)).astype(jnp.bfloat16)
    return high, low


def stacked(value):
    high, low = split(value)
    return jnp.concatenate([high, low, high], axis=0)


def joined(value):
    high, low = split(value)
    return jnp.concatenate([high, low, high], axis=1)


def mul(first, second):
    return jnp.dot(first, second, preferred_element_type=jnp.float32)


def kernel(
    sizes,
    vel_hbm,
    rea_hbm,
    fine_z_hbm,
    fine_xy_hbm,
    right_hbm,
    left_hbm,
    plain_hbm,
    adv_ref,
    pres_ref,
    resid_ref,
    vel_ref,
    rea_ref,
    fine_z_ref,
    fine_xy_ref,
    right_ref,
    left_ref,
    plain_ref,
    load_sem,
    adv_q,
    ops_q,
    sx3,
    sy3,
    sc3,
    rx3,
    ry3,
    rc3,
    sx1,
    sy1,
    sc1,
    rx1,
    ry1,
    rc1,
    part,
    got,
    send_sem,
    recv_sem,
    tree_send,
    tree_recv,
    word,
    mass_q,
    local_mass,
    lines_q,
    sums_x,
    sums_y,
    far_x,
    far_c,
    inverse_q,
):
    pairs = (
        (vel_hbm, vel_ref),
        (fine_z_hbm, fine_z_ref),
        (fine_xy_hbm, fine_xy_ref),
        (right_hbm, right_ref),
        (plain_hbm, plain_ref),
        (rea_hbm, rea_ref),
        (left_hbm, left_ref),
    )
    loads = [pltpu.make_async_copy(a, b, load_sem.at[k]) for k, (a, b) in enumerate(pairs)]
    for load in loads:
        load.start()

    count_x, count_y, low_count = sizes
    weights, deriv = spectral_tables()[:2]
    stiff = [[float(v) for v in row] for row in deriv.T @ np.diag(weights) @ deriv]
    slope = [[float(v) for v in row] for row in np.diag(weights) @ deriv @ np.diag(1.0 / weights)]
    thick = float(2.0 * weights[0])
    high_count = count_x // low_count
    me_x, me_y = lax.axis_index("wide"), lax.axis_index("narrow")
    me_low, me_high = lax.rem(me_x, low_count), me_x // low_count
    me_pair, me_core = me_y // 2, lax.rem(me_y, 2)

    def turn(place, step, count):
        moved = place + step % count
        return jnp.where(moved >= count, moved - count, moved)

    def at_side(side):
        return turn(me_x, side[0], count_x), turn(me_y, side[1], count_y)

    def far_first(count_a, count_b):
        hops = lambda step, count: min(step, count - step)
        steps = [(i, j) for i in range(count_a) for j in range(count_b) if (i, j) != (0, 0)]
        return sorted(steps, key=lambda s: -hops(s[0], count_a) - hops(s[1], count_b))

    stages = (
        [
            (me_high * low_count + turn(me_low, i, low_count), me_pair * 2 + turn(me_core, j, 2))
            for i, j in far_first(low_count, 2)
        ],
        [
            (
                turn(me_high, i, high_count) * low_count + me_low,
                turn(me_pair, j, count_y // 2) * 2 + me_core,
            )
            for i, j in far_first(high_count, count_y // 2)
        ],
    )
    def by_z(step):
        return me_high * low_count + turn(me_low, step, low_count), me_y

    def by_y(step):
        return turn(me_high, step, high_count) * low_count + me_low, me_y

    def by_pair(step):
        return me_x, turn(me_pair, step, count_y // 2) * 2 + me_core

    near = [by_z(1), by_z(-1), by_y(1), by_y(-1), by_pair(1), by_pair(-1)]
    rounds = (
        near[:4],
        [by_z(2), by_z(-2), by_y(2), by_y(-2)],
        [by_z(2), by_z(-2)] + near[4:],
        near[4:] + [(me_x, me_pair * 2 + 1 - me_core)],
    )
    partners = [at_side(side) for side in FAR + SIDES] + near

    barrier = pltpu.get_barrier_semaphore()
    for who in partners:
        pl.semaphore_signal(barrier, inc=1, device_id=who, device_id_type=MESH)

    def vouch(index):
        for who in rounds[index]:
            pl.semaphore_signal(word.at[index], inc=1, device_id=who, device_id_type=MESH)

    def hear(index):
        pl.semaphore_wait(word.at[index], len(rounds[index]))

    for load in loads[:3]:
        load.wait()
    parts = []
    for c in range(3):
        for e in range(2):
            parts.append(vel_ref[c, :, 8 * e : 8 * e + 8, :].reshape(64, 128))
    on_z = mul(joined(jnp.concatenate(parts, axis=0)), fine_z_ref[...])
    width = on_z.shape[1] // 2
    products = {}
    for e in range(2):
        fine = []
        for c in range(3):
            first = 64 * (2 * c + e)
            flat = mul(fine_xy_ref[:432, :192], stacked(on_z[first : first + 64, :width]))
            steep = mul(fine_xy_ref[:144, :192], stacked(on_z[first : first + 64, width:]))
            fine.append((flat[:144], flat[144:288], flat[288:], steep))
        for c in range(3):
            products[c, e] = (
                fine[0][0] * fine[c][1] + fine[1][0] * fine[c][2] + fine[2][0] * fine[c][3]
            )
    for load in loads[3:4]:
        load.wait()
    row8 = lax.broadcasted_iota(jnp.int32, (8, 8, 128), 1)
    back_rows = 3 * width
    for c in range(3):
        both = []
        for e in range(2):
            both.append(stacked(mul(joined(products[c, e]), right_ref[:back_rows, :])))
        weak = mul(fine_xy_ref[432:, :], jnp.concatenate(both, axis=1))
        first = weak[:, :128].reshape(8, 8, 128)
        second = weak[:, 128:].reshape(8, 8, 128)
        first, second = (
            first + jnp.where(row8 == 7, pltpu.roll(second, 7, 1), 0.0),
            second + jnp.where(row8 == 0, pltpu.roll(first, 1, 1), 0.0),
        )
        adv_q[c] = jnp.concatenate([first, second], axis=1).reshape(128, 128)

    pl.semaphore_wait(barrier, len(partners))

    has = {1: (me_x > 0, me_y > 0), -1: (me_x < count_x - 1, me_y < count_y - 1)}
    for load in loads[4:]:
        load.wait()

    rows = lax.broadcasted_iota(jnp.int32, (128, 128), 0)
    in_x, in_y = rows // 16, lax.rem(rows, 16)
    lane = lax.broadcasted_iota(jnp.int32, (128, 128), 1)
    in_z = lax.rem(lane, 8)
    cross_x = ((in_x == 0) & has[1][0]) | ((in_x == 7) & has[-1][0])
    cross_y = ((in_y == 0) & has[1][1]) | ((in_y == 15) & has[-1][1])
    cross = jnp.where(cross_x, 0.5, 1.0) * jnp.where(cross_y, 0.5, 1.0)
    twice_x, twice_y = jnp.where(cross_x, 2.0, 1.0), jnp.where(cross_y, 2.0, 1.0)
    scale_y = plain_ref[8] * twice_x
    scale_x = plain_ref[9] * twice_y
    scale_z = plain_ref[2] * twice_x * twice_y

    def pack(q, bufs, c):
        sx, sy, sc = bufs[:3]
        sx[0, c] = q[112:128, :]
        sx[1, c] = q[0:16, :]
        sy[0, c] = q[pl.ds(15, 8, stride=16), :]
        sy[1, c] = q[pl.ds(0, 8, stride=16), :]
        for k, row in enumerate((127, 112, 15, 0)):
            sc[k, c : c + 1, :] = q[row : row + 1, :]

    def attach(bufs, c, k, face):
        sx, sy, sc = bufs[:3]
        sx[k, c] = face
        sc[2 * k, c + 1 : c + 2, :] = face[15:16]
        sc[2 * k + 1, c + 1 : c + 2, :] = face[0:1]
        line = lines_q[pl.ds(1 - k, 8, stride=2), :]
        sy[k, c] = line
        sc[k, c : c + 1, :] = line[7:8]
        sc[2 + k, c : c + 1, :] = line[0:1]

    def launch(bufs, index, comps, far=None):
        sx, sy, sc, rx, ry, rc = bufs
        used = pl.ds(0, comps)
        moves = []
        if far is not None:
            for k in range(4):
                moves.append((FAR[2 + k], sc.at[k], far_c.at[far, k]))
        for k in range(4):
            moves.append((SIDES[4 + k], sc.at[k], rc.at[k]))
        if far is not None:
            for k in range(2):
                moves.append((FAR[k], sx.at[k, 0], far_x.at[far, k]))
        for k in range(2):
            moves.append((SIDES[k], sx.at[k, used], rx.at[k, used]))
        for k in range(2):
            moves.append((SIDES[2 + k], sy.at[k, used], ry.at[k, used]))
        copies = []
        for k, (side, source, target) in enumerate(moves):
            copy = pltpu.make_async_remote_copy(
                src_ref=source,
                dst_ref=target,
                send_sem=send_sem.at[index, k],
                recv_sem=recv_sem.at[index, k],
                device_id=at_side(side),
                device_id_type=MESH,
            )
            copy.start()
            copies.append(copy)
        return copies

    row_x = lax.broadcasted_iota(jnp.int32, (8, 128), 0)

    def side_line(bufs, k, c):
        ry, rc = bufs[4], bufs[5]
        low = jnp.where(has[1][0], rc[k, c : c + 1, :], 0.0)
        high = jnp.where(has[-1][0], rc[2 + k, c : c + 1, :], 0.0)
        return ry[k, c] + jnp.where(row_x == 0, low, 0.0) + jnp.where(row_x == 7, high, 0.0)

    ends_y = ((pl.ds(0, 8, stride=16), has[1][1]), (pl.ds(15, 8, stride=16), has[-1][1]))

    row_y = lax.broadcasted_iota(jnp.int32, (16, 128), 0)

    def side_face(face, corner, k, row):
        low = jnp.where(has[1][1], corner[2 * k, row : row + 1, :], 0.0)
        high = jnp.where(has[-1][1], corner[2 * k + 1, row : row + 1, :], 0.0)
        return face + jnp.where(row_y == 0, low, 0.0) + jnp.where(row_y == 15, high, 0.0)

    ends_x = ((slice(0, 16), has[1][0]), (slice(112, 128), has[-1][0]))

    def receive(fields, bufs, copies):
        rx = bufs[3]
        for copy in copies:
            copy.wait_recv()
        for c, q in enumerate(fields):
            for k, (rows, there) in enumerate(ends_x):
                q[rows, :] = q[rows, :] + jnp.where(there, rx[k, c], 0.0)
            for k, (rows, there) in enumerate(ends_y):
                q[rows, :] = q[rows, :] + jnp.where(there, side_line(bufs, k, c), 0.0)

    three = (sx3, sy3, sc3, rx3, ry3, rc3)
    ones = [tuple(buf.at[k] for buf in (sx1, sy1, sc1, rx1, ry1, rc1)) for k in range(3)]
    for c in range(3):
        pack(adv_q.at[c], three, c)
    lines_q[...] = jnp.sum(
        (adv_q[1] * plain_ref[10] * jnp.where(cross_y, 0.5, 1.0)).reshape(16, 8, 128), axis=1
    )
    outer = (jnp.where(has[1][0], 0.5, 1.0), jnp.where(has[-1][0], 0.5, 1.0))
    for k, end in ((0, 7), (1, 0)):
        face = (slope[end][0] * outer[0]) * adv_q[0, 0:16, :]
        face = face + (slope[end][7] * outer[1]) * adv_q[0, 112:128, :]
        for i in range(1, 7):
            face = face + slope[end][i] * adv_q[0, 16 * i : 16 * i + 16, :]
        attach(three, 3, k, face)
    copies = launch(three, 0, 4, far=0)
    vouch(0)
    flights = list(copies)

    local_half = plain_ref[4]
    inverse_mult = cross * local_half
    inverse_mass = plain_ref[3] * cross

    def sum_yz(value):
        up = pltpu.roll(value, 1, 1)
        down = pltpu.roll(value, 127, 1)
        value = value + jnp.where((in_z == 0) & (lane > 0), up, 0.0)
        value = value + jnp.where((in_z == 7) & (lane < 127), down, 0.0)
        up = pltpu.roll(value, 1, 0)
        down = pltpu.roll(value, 127, 0)
        return value + jnp.where(in_y == 8, up, 0.0) + jnp.where(in_y == 7, down, 0.0)

    mass_q[...] = sum_yz(plain_ref[0] * rea_ref[...].reshape(128, 128)) - SHIFT * cross
    vel = [vel_ref[c].reshape(128, 128) for c in range(3)]
    local_mass[...] = mass_q[...]
    op_xy, div_xy = slice(0, 384), slice(384, 1152)
    div_x, div_y = slice(1152, 1536), slice(1536, 1920)
    op_apart = slice(1920, 2304)
    op_z, div_z, div_z2 = (slice(back_rows + 384 * k, back_rows + 384 * k + 384) for k in range(3))

    def divergence(field, on_xy, on_z, scale_z, scale_xy):
        flat = mul(left_ref[:128, on_xy], stacked(jnp.concatenate(field[:2], axis=0)))
        return scale_z * flat + scale_xy * mul(joined(field[2]), right_ref[on_z, :])

    base = sum_yz(divergence(vel, div_xy, div_z, plain_ref[5], plain_ref[1]))

    def operate(value):
        flat = mul(left_ref[:128, op_xy], stacked(value))
        along = mul(joined(value), right_ref[op_z, :])
        return plain_ref[6] * flat + plain_ref[2] * along + local_mass[...] * value

    ops_q[0] = base
    pack(ops_q.at[0], ones[0], 0)
    pack(mass_q, ones[0], 1)
    later = launch(ones[0], 1, 2)
    flights += later
    hear(0)
    vouch(1)
    inverse_q[...] = inverse_mass
    two = (me_x > 1, me_x < count_x - 2)
    receive([adv_q.at[c] for c in range(3)], three, copies)
    adv = []
    for c in range(3):
        adv.append(adv_q[c] * inverse_mass)
    sums_x[...] = mul(left_ref[:128, div_x], stacked(adv[0]))
    sums_y[...] = mul(left_ref[:128, div_y], stacked(adv[1]))
    along = mul(joined(adv[2]), right_ref[div_z2, :])
    rx, ry, rc = three[3:]
    for k, (rows_k, there) in enumerate(ends_x):
        near_end, far_end = 7 - 7 * k, 7 * k
        mine = adv_q[0, rows_k, :] - side_face(rx[k, 0], rc, k, 0)
        other = jnp.where(two[k], side_face(far_x[0, k], far_c[0], k, 0), 0.0)
        face = side_face(rx[k, 3], rc, k, 4)
        face = face + (0.5 * slope[near_end][near_end]) * mine
        face = face + (0.5 * slope[near_end][far_end]) * other
        face = face * (thick * inverse_q[rows_k, :])
        sums_x[rows_k, :] = sums_x[rows_k, :] + jnp.where(there, face, 0.0)
    for k, (rows_k, there) in enumerate(ends_y):
        near_end = 7 - 7 * k
        mine = adv_q[1, rows_k, :] - side_line(three, k, 1)
        line = side_line(three, k, 3) + (0.5 * slope[near_end][near_end]) * mine
        line = line * (thick * inverse_q[rows_k, :])
        sums_y[rows_k, :] = sums_y[rows_k, :] + jnp.where(there, line, 0.0)
    receive([ops_q.at[0], mass_q], ones[0], later)
    hear(1)
    vouch(2)
    z0 = 0.05 * (scale_x * sums_x[...] + scale_y * sums_y[...] + scale_z * along) - ops_q[0]

    def dot(first, second, scale):
        return jnp.sum(first * second * scale, axis=0, keepdims=True)

    image = operate(z0)
    ops_q[1] = image
    pack(ops_q.at[1], ones[1], 0)
    lines_q[...] = jnp.sum((image * plain_ref[7]).reshape(16, 8, 128), axis=1)
    for k, end in ((0, 7), (1, 0)):
        face = stiff[end][0] * image[0:16]
        for i in range(1, 8):
            face = face + stiff[end][i] * image[16 * i : 16 * i + 16]
        attach(ones[1], 1, k, face)
    copies = launch(ones[1], 2, 2, far=1)
    flights += copies
    hear(2)
    vouch(3)
    for c in range(3):
        adv_ref[c] = adv[c].reshape(8, 16, 128)
    part[0, 0:1, :] = dot(z0, z0, inverse_mult)
    part[0, 6:8, :] = jnp.zeros((2, 128), jnp.float32)
    receive([ops_q.at[1]], ones[1], copies)
    hear(3)
    z1 = ops_q[1]
    rx, ry, rc = ones[1][3:]
    apart = mul(left_ref[:, op_apart], stacked(z1))
    along = mul(joined(z1), right_ref[op_z, :])
    sums_x[...] = apart[:128]
    sums_y[...] = apart[128:]
    for k, (rows_k, there) in enumerate(ends_x):
        mine = ops_q[1, rows_k, :] - side_face(rx[k, 0], rc, k, 0)
        other = jnp.where(two[k], side_face(far_x[1, k], far_c[1], k, 0), 0.0)
        face = side_face(rx[k, 1], rc, k, 2) + stiff[7][7] * mine + stiff[7][0] * other
        sums_x[rows_k, :] = sums_x[rows_k, :] + jnp.where(there, face, 0.0)
    for k, (rows_k, there) in enumerate(ends_y):
        mine = ops_q[1, rows_k, :] - side_line(ones[1], k, 0)
        line = side_line(ones[1], k, 1) + stiff[7][7] * mine
        sums_y[rows_k, :] = sums_y[rows_k, :] + jnp.where(there, line, 0.0)
    z2 = scale_x * sums_x[...] + scale_y * sums_y[...] + scale_z * along + mass_q[...] * z1
    ops_q[2] = z2
    part[0, 1:2, :] = dot(z0, z1, inverse_mult)
    part[0, 2:3, :] = dot(z1, z1, inverse_mult)
    last = operate(z2)
    part[0, 3:4, :] = dot(z1, z2, inverse_mult)
    part[0, 4:5, :] = dot(z2, z2, inverse_mult)
    part[0, 5:6, :] = dot(z2, last, local_half)

    slot = 0
    for index, stage in enumerate(stages):
        copies_in = []
        for k, who in enumerate(stage):
            copies_in.append(
                pltpu.make_async_remote_copy(
                    src_ref=part.at[index],
                    dst_ref=got.at[slot + k],
                    send_sem=tree_send.at[slot + k],
                    recv_sem=tree_recv.at[slot + k],
                    device_id=who,
                    device_id_type=MESH,
                )
            )
        for copy in copies_in:
            copy.start()
        if index == 0:
            ops_q[3] = last
            pack(ops_q.at[3], ones[2], 0)
            copies = launch(ones[2], 3, 1)
            flights += copies
        for copy in copies_in:
            copy.wait_recv()
        total = part[index]
        for k in range(len(stage)):
            total = total + got[slot + k]
        if index < 1:
            part[index + 1] = total
        flights += copies_in
        slot += len(stage)

    receive([ops_q.at[3]], ones[2], copies)
    sums = jnp.broadcast_to(jnp.sum(total, axis=1, keepdims=True), (8, 128))
    g00, g01, g11, g12, g22, g23 = (sums[k : k + 1, :] for k in range(6))
    h00 = g01 + SHIFT * g00
    h01 = g11 + SHIFT * g01
    h11 = g12 + SHIFT * g11
    h02 = g12 + SHIFT * g11
    h12 = g22 + SHIFT * g12
    h22 = g23 + SHIFT * g22
    over = 1.0 / h00
    l10, l20 = h01 * over, h02 * over
    d1 = h11 - l10 * h01
    e1 = h12 - l10 * h02
    over1 = 1.0 / d1
    l21 = e1 * over1
    d2 = h22 - l20 * h02 - l21 * e1
    b1 = g01 - l10 * g00
    b2 = g11 - l20 * g00 - l21 * b1
    c2 = b2 / d2
    c1 = b1 * over1 - l21 * c2
    c0 = g00 * over - l10 * c1 - l20 * c2
    z3 = ops_q[3]
    pres = c0 * z0 + c1 * z1 + c2 * z2
    pres_ref[...] = pres.reshape(8, 16, 128)
    resid = (
        (1.0 - SHIFT * c0) * z0 - (c0 + SHIFT * c1) * z1 - (c1 + SHIFT * c2) * z2 - c2 * z3
    )
    resid_ref[...] = resid.reshape(8, 16, 128)
    for copy in flights:
        copy.wait_send()


def store(*refs):
    sources, targets, sems = refs[:3], refs[3:6], refs[6]
    copies = [
        pltpu.make_async_copy(a, b, sems.at[k]) for k, (a, b) in enumerate(zip(sources, targets))
    ]
    for copy in copies:
        copy.start()
    for copy in copies:
        copy.wait()


def per_device(sizes, velocity, reaction):
    consts = [jnp.asarray(value) for value in tables_for(reaction.shape[2])]
    operands = [velocity, reaction] + consts
    shape_of = jax.ShapeDtypeStruct
    count_x, count_y, low_count = sizes
    trips = (2 * low_count - 1) + (count_x // low_count * count_y // 2 - 1)
    vmem, f32, dma = pltpu.VMEM, jnp.float32, pltpu.SemaphoreType.DMA
    results = pl.pallas_call(
        functools.partial(kernel, sizes),
        out_shape=(
            shape_of(velocity.shape, f32),
            shape_of(reaction.shape, f32),
            shape_of(reaction.shape, f32),
        ),
        in_specs=[pl.BlockSpec(memory_space=pltpu.HBM)] * 7,
        out_specs=(pl.BlockSpec(memory_space=vmem),) * 3,
        scratch_shapes=[vmem(value.shape, value.dtype) for value in operands]
        + [
            dma((7,)),
            vmem((3, 128, 128), f32),
            vmem((4, 128, 128), f32),
            vmem((2, 4, 16, 128), f32),
            vmem((2, 4, 8, 128), f32),
            vmem((4, 8, 128), f32),
            vmem((2, 4, 16, 128), f32),
            vmem((2, 4, 8, 128), f32),
            vmem((4, 8, 128), f32),
            vmem((3, 2, 2, 16, 128), f32),
            vmem((3, 2, 2, 8, 128), f32),
            vmem((3, 4, 8, 128), f32),
            vmem((3, 2, 2, 16, 128), f32),
            vmem((3, 2, 2, 8, 128), f32),
            vmem((3, 4, 8, 128), f32),
            vmem((2, 8, 128), f32),
            vmem((trips, 8, 128), f32),
            dma((4, 14)),
            dma((4, 14)),
            dma((trips,)),
            dma((trips,)),
            pltpu.SemaphoreType.REGULAR((4,)),
            vmem((128, 128), f32),
            vmem((128, 128), f32),
            vmem((16, 128), f32),
            vmem((128, 128), f32),
            vmem((128, 128), f32),
            vmem((2, 2, 16, 128), f32),
            vmem((2, 4, 8, 128), f32),
            vmem((128, 128), f32),
        ],
        compiler_params=pltpu.CompilerParams(
            collective_id=0, has_side_effects=True, vmem_limit_bytes=54700 * 1024
        ),
    )(*operands)
    return pl.pallas_call(
        store,
        out_shape=tuple(shape_of(value.shape, f32) for value in results),
        in_specs=[pl.BlockSpec(memory_space=vmem)] * 3,
        out_specs=(pl.BlockSpec(memory_space=pltpu.HBM),) * 3,
        scratch_shapes=[dma((3,))],
        compiler_params=pltpu.CompilerParams(vmem_limit_bytes=1024 * 1024),
    )(*results)


def solution(mesh):
    count_x, count_y = mesh.shape["wide"], mesh.shape["narrow"]
    low_count = 12 if count_x % 12 == 0 else 2
    return jax.shard_map(
        functools.partial(per_device, (count_x, count_y, low_count)),
        mesh=mesh,
        in_specs=(P(None, "wide", "narrow", None), P("wide", "narrow", None)),
        out_specs=(
            P(None, "wide", "narrow", None),
            P("wide", "narrow", None),
            P("wide", "narrow", None),
        ),
        check_vma=False,
    )
```

```python
import functools

import jax
import jax.numpy as jnp
import ml_dtypes
import numpy as np
from jax import lax
from jax.experimental import pallas as pl
from jax.experimental.pallas import tpu as pltpu
from jax.sharding import PartitionSpec as P

MESH = pl.DeviceIdType.MESH
SHIFT = 4.0
SIDES = ((1, 0), (-1, 0), (0, 1), (0, -1), (1, 1), (1, -1), (-1, 1), (-1, -1))
FAR = ((2, 0), (-2, 0), (2, 1), (2, -1), (-2, 1), (-2, -1))


def legendre_pair(order, nodes):
    p_prev = np.ones(nodes.shape)
    p_now = nodes * 1.0
    for k in range(2, order + 1):
        p_next = ((2 * k - 1) * nodes * p_now - (k - 1) * p_prev) / k
        p_prev = p_now
        p_now = p_next
    return (p_now, p_prev)


def spectral_tables():
    degree = 7
    points = degree + 1
    gll_nodes = np.cos(np.pi * np.arange(points) / degree)
    for sweep in range(100):
        p_now, p_prev = legendre_pair(degree, gll_nodes)
        gll_nodes = gll_nodes - (gll_nodes * p_now - p_prev) / ((degree + 1) * p_now)
    gll_nodes = np.sort(gll_nodes)
    legendre_vals, unused_prev = legendre_pair(degree, gll_nodes)
    gll_weights = 2.0 / (degree * (degree + 1) * legendre_vals**2)
    derivative = np.zeros((points, points))
    for row_index in range(points):
        for col_index in range(points):
            if row_index != col_index:
                derivative[row_index, col_index] = legendre_vals[row_index] / (
                    legendre_vals[col_index] * (gll_nodes[row_index] - gll_nodes[col_index])
                )
    derivative[0, 0] = -degree * (degree + 1) / 4.0
    derivative[-1, -1] = degree * (degree + 1) / 4.0
    gauss_nodes = np.cos(np.pi * (np.arange(12) + 0.75) / 12.5)
    for sweep in range(100):
        p_now, p_prev = legendre_pair(12, gauss_nodes)
        slope = 12 * (gauss_nodes * p_now - p_prev) / (gauss_nodes * gauss_nodes - 1.0)
        gauss_nodes = gauss_nodes - p_now / slope
    gauss_nodes = np.sort(gauss_nodes)
    p_now, p_prev = legendre_pair(12, gauss_nodes)
    slope = 12 * (gauss_nodes * p_now - p_prev) / (gauss_nodes * gauss_nodes - 1.0)
    gauss_weights = 2.0 / ((1.0 - gauss_nodes**2) * slope**2)
    interpolate = np.ones((12, points))
    for col_index in range(points):
        for other in range(points):
            if other != col_index:
                interpolate[:, col_index] *= (gauss_nodes - gll_nodes[other]) / (
                    gll_nodes[col_index] - gll_nodes[other]
                )
    return (gll_weights, derivative, gauss_weights, interpolate)


def halves(matrix):
    high = matrix.astype(ml_dtypes.bfloat16)
    low = (matrix - high.astype(np.float64)).astype(ml_dtypes.bfloat16)
    return high, low


def left_factor(matrix):
    high, low = halves(matrix)
    return np.concatenate([high, high, low], axis=1)


def right_factor(matrix):
    high, low = halves(matrix)
    return np.concatenate([high, high, low], axis=0)


def tables_for(len_z):
    weights, deriv, fine_weights, interp = spectral_tables()
    els_z = len_z // 8
    gradint = interp @ deriv
    stiff = deriv.T @ np.diag(weights) @ deriv
    eye2, eye_z = np.eye(2), np.eye(els_z)

    def shared(count):
        total = np.eye(8 * count)
        for k in range(count - 1):
            total[8 * k + 7, 8 * k + 8] = total[8 * k + 8, 8 * k + 7] = 1.0
        return total

    sum_y, sum_z = shared(2), shared(els_z)
    w_x, w_y, w_z = weights, np.tile(weights, 2), np.tile(weights, els_z)
    w_y2, w_z2 = sum_y @ w_y, sum_z @ w_z

    fine_z = np.zeros((len_z, 2 * 16 * els_z))
    back_z = np.zeros((16 * els_z, len_z))
    for e in range(els_z):
        fine_z[8 * e : 8 * e + 8, 16 * e : 16 * e + 12] = interp.T
        first = 16 * els_z + 16 * e
        fine_z[8 * e : 8 * e + 8, first : first + 12] = gradint.T
        back_z[16 * e : 16 * e + 12, 8 * e : 8 * e + 8] = fine_weights[:, None] * interp
    back_z = back_z @ sum_z
    fine_xy = np.concatenate(
        [np.kron(interp, interp), np.kron(gradint, interp), np.kron(interp, gradint)], axis=0
    )
    back = interp.T * fine_weights[None, :]
    back_xy = np.kron(back, back)

    op_xy = np.kron(stiff, np.diag(w_y2)) + np.kron(np.diag(w_x), sum_y @ np.kron(eye2, stiff))
    op_apart = np.concatenate(
        [np.kron(stiff, np.eye(16)), np.kron(np.eye(8), sum_y @ np.kron(eye2, stiff))], axis=0
    )
    op_z = np.kron(eye_z, stiff).T @ sum_z
    weak = np.diag(weights) @ deriv
    div_xy = np.concatenate(
        [np.kron(weak, np.diag(w_y)), np.kron(np.diag(w_x), np.kron(eye2, weak))], axis=1
    )
    div_x = np.kron(weak, np.eye(16))
    div_y = np.kron(np.eye(8), sum_y @ np.kron(eye2, weak))
    div_z = np.kron(eye_z, weak).T
    div_z2 = div_z @ sum_z

    w_xy, w_xy2 = np.kron(w_x, w_y), np.kron(w_x, w_y2)
    half_y = 1.0 / (sum_y @ np.ones(16))
    half_z = 1.0 / (sum_z @ np.ones(len_z))
    ones_x, ones_z = np.ones(8), np.ones(len_z)
    plain = np.stack(
        [
            np.outer(w_xy, w_z),
            np.outer(w_xy, ones_z),
            np.outer(w_xy2, ones_z),
            1.0 / np.outer(w_xy2, w_z2),
            np.outer(np.kron(ones_x, half_y), half_z),
            np.outer(np.ones(128), w_z),
            np.outer(np.ones(128), w_z2),
            np.outer(np.tile(np.concatenate([stiff[0], stiff[7]]), 8), ones_z),
            np.outer(np.kron(w_x, np.ones(16)), w_z2),
            np.outer(np.kron(ones_x, w_y2), w_z2),
            np.outer(np.tile(np.concatenate([weak[0], weak[7]]), 8) / np.kron(ones_x, w_y2), ones_z),
        ]
    ).astype(np.float32)
    from_right = np.concatenate(
        [right_factor(back_z), right_factor(op_z), right_factor(div_z), right_factor(div_z2)], axis=0
    )
    from_left = np.zeros((256, 2304), ml_dtypes.bfloat16)
    from_left[:128, :384] = left_factor(op_xy)
    from_left[:128, 384:1152] = left_factor(div_xy)
    from_left[:128, 1152:1536] = left_factor(div_x)
    from_left[:128, 1536:1920] = left_factor(div_y)
    from_left[:, 1920:] = left_factor(op_apart)
    shapes_xy = np.zeros((496, 432), ml_dtypes.bfloat16)
    shapes_xy[:432, :192] = left_factor(fine_xy)
    shapes_xy[432:] = left_factor(back_xy)
    return (
        right_factor(fine_z),
        shapes_xy,
        from_right,
        from_left,
        plain,
    )


def split(value):
    high = value.astype(jnp.bfloat16)
    low = (value - high.astype(jnp.float32)).astype(jnp.bfloat16)
    return high, low


def stacked(value):
    high, low = split(value)
    return jnp.concatenate([high, low, high], axis=0)


def joined(value):
    high, low = split(value)
    return jnp.concatenate([high, low, high], axis=1)


def mul(first, second):
    return jnp.dot(first, second, preferred_element_type=jnp.float32)


def kernel(
    sizes,
    vel_hbm,
    rea_hbm,
    fine_z_hbm,
    fine_xy_hbm,
    right_hbm,
    left_hbm,
    plain_hbm,
    adv_ref,
    pres_ref,
    resid_ref,
    vel_ref,
    rea_ref,
    fine_z_ref,
    fine_xy_ref,
    right_ref,
    left_ref,
    plain_ref,
    load_sem,
    adv_q,
    ops_q,
    sx3,
    sy3,
    sc3,
    rx3,
    ry3,
    rc3,
    sx1,
    sy1,
    sc1,
    rx1,
    ry1,
    rc1,
    part,
    got,
    send_sem,
    recv_sem,
    tree_send,
    tree_recv,
    word,
    mass_q,
    local_mass,
    lines_q,
    sums_x,
    sums_y,
    far_x,
    far_c,
    inverse_q,
):
    pairs = (
        (vel_hbm, vel_ref),
        (fine_z_hbm, fine_z_ref),
        (fine_xy_hbm, fine_xy_ref),
        (right_hbm, right_ref),
        (plain_hbm, plain_ref),
        (rea_hbm, rea_ref),
        (left_hbm, left_ref),
    )
    loads = [pltpu.make_async_copy(a, b, load_sem.at[k]) for k, (a, b) in enumerate(pairs)]
    for load in loads:
        load.start()

    count_x, count_y, low_count = sizes
    weights, deriv = spectral_tables()[:2]
    stiff = [[float(v) for v in row] for row in deriv.T @ np.diag(weights) @ deriv]
    slope = [[float(v) for v in row] for row in np.diag(weights) @ deriv @ np.diag(1.0 / weights)]
    thick = float(2.0 * weights[0])
    high_count = count_x // low_count
    me_x, me_y = lax.axis_index("wide"), lax.axis_index("narrow")
    me_low, me_high = lax.rem(me_x, low_count), me_x // low_count
    me_pair, me_core = me_y // 2, lax.rem(me_y, 2)

    def turn(place, step, count):
        moved = place + step % count
        return jnp.where(moved >= count, moved - count, moved)

    def at_side(side):
        return turn(me_x, side[0], count_x), turn(me_y, side[1], count_y)

    def far_first(count_a, count_b):
        hops = lambda step, count: min(step, count - step)
        steps = [(i, j) for i in range(count_a) for j in range(count_b) if (i, j) != (0, 0)]
        return sorted(steps, key=lambda s: -hops(s[0], count_a) - hops(s[1], count_b))

    stages = (
        [
            (me_high * low_count + turn(me_low, i, low_count), me_pair * 2 + turn(me_core, j, 2))
            for i, j in far_first(low_count, 2)
        ],
        [
            (
                turn(me_high, i, high_count) * low_count + me_low,
                turn(me_pair, j, count_y // 2) * 2 + me_core,
            )
            for i, j in far_first(high_count, count_y // 2)
        ],
    )
    def by_z(step):
        return me_high * low_count + turn(me_low, step, low_count), me_y

    def by_y(step):
        return turn(me_high, step, high_count) * low_count + me_low, me_y

    def by_pair(step):
        return me_x, turn(me_pair, step, count_y // 2) * 2 + me_core

    near = [by_z(1), by_z(-1), by_y(1), by_y(-1), by_pair(1), by_pair(-1)]
    rounds = (
        near[:4],
        [by_z(2), by_z(-2), by_y(2), by_y(-2)],
        [by_z(2), by_z(-2)] + near[4:],
        near[4:] + [(me_x, me_pair * 2 + 1 - me_core)],
    )
    partners = [at_side(side) for side in FAR + SIDES] + near

    barrier = pltpu.get_barrier_semaphore()
    for who in partners:
        pl.semaphore_signal(barrier, inc=1, device_id=who, device_id_type=MESH)

    def vouch(index):
        for who in rounds[index]:
            pl.semaphore_signal(word.at[index], inc=1, device_id=who, device_id_type=MESH)

    def hear(index):
        pl.semaphore_wait(word.at[index], len(rounds[index]))

    for load in loads[:3]:
        load.wait()
    parts = []
    for c in range(3):
        for e in range(2):
            parts.append(vel_ref[c, :, 8 * e : 8 * e + 8, :].reshape(64, 128))
    on_z = mul(joined(jnp.concatenate(parts, axis=0)), fine_z_ref[...])
    width = on_z.shape[1] // 2
    products = {}
    for e in range(2):
        fine = []
        for c in range(3):
            first = 64 * (2 * c + e)
            flat = mul(fine_xy_ref[:432, :192], stacked(on_z[first : first + 64, :width]))
            steep = mul(fine_xy_ref[:144, :192], stacked(on_z[first : first + 64, width:]))
            fine.append((flat[:144], flat[144:288], flat[288:], steep))
        for c in range(3):
            products[c, e] = (
                fine[0][0] * fine[c][1] + fine[1][0] * fine[c][2] + fine[2][0] * fine[c][3]
            )
    for load in loads[3:4]:
        load.wait()
    row8 = lax.broadcasted_iota(jnp.int32, (8, 8, 128), 1)
    back_rows = 3 * width
    for c in range(3):
        both = []
        for e in range(2):
            both.append(stacked(mul(joined(products[c, e]), right_ref[:back_rows, :])))
        weak = mul(fine_xy_ref[432:, :], jnp.concatenate(both, axis=1))
        first = weak[:, :128].reshape(8, 8, 128)
        second = weak[:, 128:].reshape(8, 8, 128)
        first, second = (
            first + jnp.where(row8 == 7, pltpu.roll(second, 7, 1), 0.0),
            second + jnp.where(row8 == 0, pltpu.roll(first, 1, 1), 0.0),
        )
        adv_q[c] = jnp.concatenate([first, second], axis=1).reshape(128, 128)

    pl.semaphore_wait(barrier, len(partners))

    has = {1: (me_x > 0, me_y > 0), -1: (me_x < count_x - 1, me_y < count_y - 1)}
    for load in loads[4:]:
        load.wait()

    rows = lax.broadcasted_iota(jnp.int32, (128, 128), 0)
    in_x, in_y = rows // 16, lax.rem(rows, 16)
    lane = lax.broadcasted_iota(jnp.int32, (128, 128), 1)
    in_z = lax.rem(lane, 8)
    cross_x = ((in_x == 0) & has[1][0]) | ((in_x == 7) & has[-1][0])
    cross_y = ((in_y == 0) & has[1][1]) | ((in_y == 15) & has[-1][1])
    cross = jnp.where(cross_x, 0.5, 1.0) * jnp.where(cross_y, 0.5, 1.0)
    twice_x, twice_y = jnp.where(cross_x, 2.0, 1.0), jnp.where(cross_y, 2.0, 1.0)
    scale_y = plain_ref[8] * twice_x
    scale_x = plain_ref[9] * twice_y
    scale_z = plain_ref[2] * twice_x * twice_y

    def pack(q, bufs, c):
        sx, sy, sc = bufs[:3]
        sx[0, c] = q[112:128, :]
        sx[1, c] = q[0:16, :]
        sy[0, c] = q[pl.ds(15, 8, stride=16), :]
        sy[1, c] = q[pl.ds(0, 8, stride=16), :]
        for k, row in enumerate((127, 112, 15, 0)):
            sc[k, c : c + 1, :] = q[row : row + 1, :]

    def attach(bufs, c, k, face):
        sx, sy, sc = bufs[:3]
        sx[k, c] = face
        sc[2 * k, c + 1 : c + 2, :] = face[15:16]
        sc[2 * k + 1, c + 1 : c + 2, :] = face[0:1]
        line = lines_q[pl.ds(1 - k, 8, stride=2), :]
        sy[k, c] = line
        sc[k, c : c + 1, :] = line[7:8]
        sc[2 + k, c : c + 1, :] = line[0:1]

    def launch(bufs, index, comps, far=None):
        sx, sy, sc, rx, ry, rc = bufs
        used = pl.ds(0, comps)
        moves = []
        if far is not None:
            for k in range(4):
                moves.append((FAR[2 + k], sc.at[k], far_c.at[far, k]))
        for k in range(4):
            moves.append((SIDES[4 + k], sc.at[k], rc.at[k]))
        if far is not None:
            for k in range(2):
                moves.append((FAR[k], sx.at[k, 0], far_x.at[far, k]))
        for k in range(2):
            moves.append((SIDES[k], sx.at[k, used], rx.at[k, used]))
        for k in range(2):
            moves.append((SIDES[2 + k], sy.at[k, used], ry.at[k, used]))
        copies = []
        for k, (side, source, target) in enumerate(moves):
            copy = pltpu.make_async_remote_copy(
                src_ref=source,
                dst_ref=target,
                send_sem=send_sem.at[index, k],
                recv_sem=recv_sem.at[index, k],
                device_id=at_side(side),
                device_id_type=MESH,
            )
            copy.start()
            copies.append(copy)
        return copies

    row_x = lax.broadcasted_iota(jnp.int32, (8, 128), 0)

    def side_line(bufs, k, c):
        ry, rc = bufs[4], bufs[5]
        low = jnp.where(has[1][0], rc[k, c : c + 1, :], 0.0)
        high = jnp.where(has[-1][0], rc[2 + k, c : c + 1, :], 0.0)
        return ry[k, c] + jnp.where(row_x == 0, low, 0.0) + jnp.where(row_x == 7, high, 0.0)

    ends_y = ((pl.ds(0, 8, stride=16), has[1][1]), (pl.ds(15, 8, stride=16), has[-1][1]))

    row_y = lax.broadcasted_iota(jnp.int32, (16, 128), 0)

    def side_face(face, corner, k, row):
        low = jnp.where(has[1][1], corner[2 * k, row : row + 1, :], 0.0)
        high = jnp.where(has[-1][1], corner[2 * k + 1, row : row + 1, :], 0.0)
        return face + jnp.where(row_y == 0, low, 0.0) + jnp.where(row_y == 15, high, 0.0)

    ends_x = ((slice(0, 16), has[1][0]), (slice(112, 128), has[-1][0]))

    def receive(fields, bufs, copies):
        rx = bufs[3]
        for copy in copies:
            copy.wait_recv()
        for c, q in enumerate(fields):
            for k, (rows, there) in enumerate(ends_x):
                q[rows, :] = q[rows, :] + jnp.where(there, rx[k, c], 0.0)
            for k, (rows, there) in enumerate(ends_y):
                q[rows, :] = q[rows, :] + jnp.where(there, side_line(bufs, k, c), 0.0)

    three = (sx3, sy3, sc3, rx3, ry3, rc3)
    ones = [tuple(buf.at[k] for buf in (sx1, sy1, sc1, rx1, ry1, rc1)) for k in range(3)]
    for c in range(3):
        pack(adv_q.at[c], three, c)
    lines_q[...] = jnp.sum(
        (adv_q[1] * plain_ref[10] * jnp.where(cross_y, 0.5, 1.0)).reshape(16, 8, 128), axis=1
    )
    outer = (jnp.where(has[1][0], 0.5, 1.0), jnp.where(has[-1][0], 0.5, 1.0))
    for k, end in ((0, 7), (1, 0)):
        face = (slope[end][0] * outer[0]) * adv_q[0, 0:16, :]
        face = face + (slope[end][7] * outer[1]) * adv_q[0, 112:128, :]
        for i in range(1, 7):
            face = face + slope[end][i] * adv_q[0, 16 * i : 16 * i + 16, :]
        attach(three, 3, k, face)
    copies = launch(three, 0, 4, far=0)
    vouch(0)
    flights = list(copies)

    local_half = plain_ref[4]
    inverse_mult = cross * local_half
    inverse_mass = plain_ref[3] * cross

    def sum_yz(value):
        up = pltpu.roll(value, 1, 1)
        down = pltpu.roll(value, 127, 1)
        value = value + jnp.where((in_z == 0) & (lane > 0), up, 0.0)
        value = value + jnp.where((in_z == 7) & (lane < 127), down, 0.0)
        up = pltpu.roll(value, 1, 0)
        down = pltpu.roll(value, 127, 0)
        return value + jnp.where(in_y == 8, up, 0.0) + jnp.where(in_y == 7, down, 0.0)

    mass_q[...] = sum_yz(plain_ref[0] * rea_ref[...].reshape(128, 128)) - SHIFT * cross
    vel = [vel_ref[c].reshape(128, 128) for c in range(3)]
    local_mass[...] = mass_q[...]
    op_xy, div_xy = slice(0, 384), slice(384, 1152)
    div_x, div_y = slice(1152, 1536), slice(1536, 1920)
    op_apart = slice(1920, 2304)
    op_z, div_z, div_z2 = (slice(back_rows + 384 * k, back_rows + 384 * k + 384) for k in range(3))

    def divergence(field, on_xy, on_z, scale_z, scale_xy):
        flat = mul(left_ref[:128, on_xy], stacked(jnp.concatenate(field[:2], axis=0)))
        return scale_z * flat + scale_xy * mul(joined(field[2]), right_ref[on_z, :])

    base = sum_yz(divergence(vel, div_xy, div_z, plain_ref[5], plain_ref[1]))

    def operate(value):
        flat = mul(left_ref[:128, op_xy], stacked(value))
        along = mul(joined(value), right_ref[op_z, :])
        return plain_ref[6] * flat + plain_ref[2] * along + local_mass[...] * value

    ops_q[0] = base
    pack(ops_q.at[0], ones[0], 0)
    pack(mass_q, ones[0], 1)
    later = launch(ones[0], 1, 2)
    flights += later
    hear(0)
    vouch(1)
    inverse_q[...] = inverse_mass
    two = (me_x > 1, me_x < count_x - 2)
    receive([adv_q.at[c] for c in range(3)], three, copies)
    adv = []
    for c in range(3):
        adv.append(adv_q[c] * inverse_mass)
    sums_x[...] = mul(left_ref[:128, div_x], stacked(adv[0]))
    sums_y[...] = mul(left_ref[:128, div_y], stacked(adv[1]))
    along = mul(joined(adv[2]), right_ref[div_z2, :])
    rx, ry, rc = three[3:]
    for k, (rows_k, there) in enumerate(ends_x):
        near_end, far_end = 7 - 7 * k, 7 * k
        mine = adv_q[0, rows_k, :] - side_face(rx[k, 0], rc, k, 0)
        other = jnp.where(two[k], side_face(far_x[0, k], far_c[0], k, 0), 0.0)
        face = side_face(rx[k, 3], rc, k, 4)
        face = face + (0.5 * slope[near_end][near_end]) * mine
        face = face + (0.5 * slope[near_end][far_end]) * other
        face = face * (thick * inverse_q[rows_k, :])
        sums_x[rows_k, :] = sums_x[rows_k, :] + jnp.where(there, face, 0.0)
    for k, (rows_k, there) in enumerate(ends_y):
        near_end = 7 - 7 * k
        mine = adv_q[1, rows_k, :] - side_line(three, k, 1)
        line = side_line(three, k, 3) + (0.5 * slope[near_end][near_end]) * mine
        line = line * (thick * inverse_q[rows_k, :])
        sums_y[rows_k, :] = sums_y[rows_k, :] + jnp.where(there, line, 0.0)
    receive([ops_q.at[0], mass_q], ones[0], later)
    hear(1)
    vouch(2)
    z0 = 0.05 * (scale_x * sums_x[...] + scale_y * sums_y[...] + scale_z * along) - ops_q[0]

    def dot(first, second, scale):
        return jnp.sum(first * second * scale, axis=0, keepdims=True)

    image = operate(z0)
    ops_q[1] = image
    pack(ops_q.at[1], ones[1], 0)
    lines_q[...] = jnp.sum((image * plain_ref[7]).reshape(16, 8, 128), axis=1)
    for k, end in ((0, 7), (1, 0)):
        face = stiff[end][0] * image[0:16]
        for i in range(1, 8):
            face = face + stiff[end][i] * image[16 * i : 16 * i + 16]
        attach(ones[1], 1, k, face)
    copies = launch(ones[1], 2, 2, far=1)
    for copy in flights:
        copy.wait_send()
    flights = list(copies)
    hear(2)
    vouch(3)
    for c in range(3):
        adv_ref[c] = adv[c].reshape(8, 16, 128)
    part[0, 0:1, :] = dot(z0, z0, inverse_mult)
    part[0, 6:8, :] = jnp.zeros((2, 128), jnp.float32)
    receive([ops_q.at[1]], ones[1], copies)
    hear(3)
    z1 = ops_q[1]
    rx, ry, rc = ones[1][3:]
    apart = mul(left_ref[:, op_apart], stacked(z1))
    along = mul(joined(z1), right_ref[op_z, :])
    sums_x[...] = apart[:128]
    sums_y[...] = apart[128:]
    for k, (rows_k, there) in enumerate(ends_x):
        mine = ops_q[1, rows_k, :] - side_face(rx[k, 0], rc, k, 0)
        other = jnp.where(two[k], side_face(far_x[1, k], far_c[1], k, 0), 0.0)
        face = side_face(rx[k, 1], rc, k, 2) + stiff[7][7] * mine + stiff[7][0] * other
        sums_x[rows_k, :] = sums_x[rows_k, :] + jnp.where(there, face, 0.0)
    for k, (rows_k, there) in enumerate(ends_y):
        mine = ops_q[1, rows_k, :] - side_line(ones[1], k, 0)
        line = side_line(ones[1], k, 1) + stiff[7][7] * mine
        sums_y[rows_k, :] = sums_y[rows_k, :] + jnp.where(there, line, 0.0)
    z2 = scale_x * sums_x[...] + scale_y * sums_y[...] + scale_z * along + mass_q[...] * z1
    ops_q[2] = z2
    part[0, 1:2, :] = dot(z0, z1, inverse_mult)
    part[0, 2:3, :] = dot(z1, z1, inverse_mult)
    last = operate(z2)
    part[0, 3:4, :] = dot(z1, z2, inverse_mult)
    part[0, 4:5, :] = dot(z2, z2, inverse_mult)
    part[0, 5:6, :] = dot(z2, last, local_half)

    slot = 0
    for index, stage in enumerate(stages):
        copies_in = []
        for k, who in enumerate(stage):
            copies_in.append(
                pltpu.make_async_remote_copy(
                    src_ref=part.at[index],
                    dst_ref=got.at[slot + k],
                    send_sem=tree_send.at[slot + k],
                    recv_sem=tree_recv.at[slot + k],
                    device_id=who,
                    device_id_type=MESH,
                )
            )
        for copy in copies_in:
            copy.start()
        if index == 0:
            ops_q[3] = last
            pack(ops_q.at[3], ones[2], 0)
            copies = launch(ones[2], 3, 1)
        for copy in flights:
            copy.wait_send()
        flights = copies_in
        for copy in copies_in:
            copy.wait_recv()
        total = part[index]
        for k in range(len(stage)):
            total = total + got[slot + k]
        if index < 1:
            part[index + 1] = total
        slot += len(stage)

    flights = flights + copies
    receive([ops_q.at[3]], ones[2], copies)
    sums = jnp.broadcast_to(jnp.sum(total, axis=1, keepdims=True), (8, 128))
    g00, g01, g11, g12, g22, g23 = (sums[k : k + 1, :] for k in range(6))
    h00 = g01 + SHIFT * g00
    h01 = g11 + SHIFT * g01
    h11 = g12 + SHIFT * g11
    h02 = g12 + SHIFT * g11
    h12 = g22 + SHIFT * g12
    h22 = g23 + SHIFT * g22
    over = 1.0 / h00
    l10, l20 = h01 * over, h02 * over
    d1 = h11 - l10 * h01
    e1 = h12 - l10 * h02
    over1 = 1.0 / d1
    l21 = e1 * over1
    d2 = h22 - l20 * h02 - l21 * e1
    b1 = g01 - l10 * g00
    b2 = g11 - l20 * g00 - l21 * b1
    c2 = b2 / d2
    c1 = b1 * over1 - l21 * c2
    c0 = g00 * over - l10 * c1 - l20 * c2
    z3 = ops_q[3]
    pres = c0 * z0 + c1 * z1 + c2 * z2
    pres_ref[...] = pres.reshape(8, 16, 128)
    resid = (
        (1.0 - SHIFT * c0) * z0 - (c0 + SHIFT * c1) * z1 - (c1 + SHIFT * c2) * z2 - c2 * z3
    )
    resid_ref[...] = resid.reshape(8, 16, 128)
    for copy in flights:
        copy.wait_send()


def store(*refs):
    sources, targets, sems = refs[:3], refs[3:6], refs[6]
    copies = [
        pltpu.make_async_copy(a, b, sems.at[k]) for k, (a, b) in enumerate(zip(sources, targets))
    ]
    for copy in copies:
        copy.start()
    for copy in copies:
        copy.wait()


def per_device(sizes, velocity, reaction):
    consts = [jnp.asarray(value) for value in tables_for(reaction.shape[2])]
    operands = [velocity, reaction] + consts
    shape_of = jax.ShapeDtypeStruct
    count_x, count_y, low_count = sizes
    trips = (2 * low_count - 1) + (count_x // low_count * count_y // 2 - 1)
    vmem, f32, dma = pltpu.VMEM, jnp.float32, pltpu.SemaphoreType.DMA
    results = pl.pallas_call(
        functools.partial(kernel, sizes),
        out_shape=(
            shape_of(velocity.shape, f32),
            shape_of(reaction.shape, f32),
            shape_of(reaction.shape, f32),
        ),
        in_specs=[pl.BlockSpec(memory_space=pltpu.HBM)] * 7,
        out_specs=(pl.BlockSpec(memory_space=vmem),) * 3,
        scratch_shapes=[vmem(value.shape, value.dtype) for value in operands]
        + [
            dma((7,)),
            vmem((3, 128, 128), f32),
            vmem((4, 128, 128), f32),
            vmem((2, 4, 16, 128), f32),
            vmem((2, 4, 8, 128), f32),
            vmem((4, 8, 128), f32),
            vmem((2, 4, 16, 128), f32),
            vmem((2, 4, 8, 128), f32),
            vmem((4, 8, 128), f32),
            vmem((3, 2, 2, 16, 128), f32),
            vmem((3, 2, 2, 8, 128), f32),
            vmem((3, 4, 8, 128), f32),
            vmem((3, 2, 2, 16, 128), f32),
            vmem((3, 2, 2, 8, 128), f32),
            vmem((3, 4, 8, 128), f32),
            vmem((2, 8, 128), f32),
            vmem((trips, 8, 128), f32),
            dma((4, 14)),
            dma((4, 14)),
            dma((trips,)),
            dma((trips,)),
            pltpu.SemaphoreType.REGULAR((4,)),
            vmem((128, 128), f32),
            vmem((128, 128), f32),
            vmem((16, 128), f32),
            vmem((128, 128), f32),
            vmem((128, 128), f32),
            vmem((2, 2, 16, 128), f32),
            vmem((2, 4, 8, 128), f32),
            vmem((128, 128), f32),
        ],
        compiler_params=pltpu.CompilerParams(
            collective_id=0, has_side_effects=True, vmem_limit_bytes=54700 * 1024
        ),
    )(*operands)
    return pl.pallas_call(
        store,
        out_shape=tuple(shape_of(value.shape, f32) for value in results),
        in_specs=[pl.BlockSpec(memory_space=vmem)] * 3,
        out_specs=(pl.BlockSpec(memory_space=pltpu.HBM),) * 3,
        scratch_shapes=[dma((3,))],
        compiler_params=pltpu.CompilerParams(vmem_limit_bytes=1024 * 1024),
    )(*results)


def solution(mesh):
    count_x, count_y = mesh.shape["wide"], mesh.shape["narrow"]
    low_count = 12 if count_x % 12 == 0 else 2
    return jax.shard_map(
        functools.partial(per_device, (count_x, count_y, low_count)),
        mesh=mesh,
        in_specs=(P(None, "wide", "narrow", None), P("wide", "narrow", None)),
        out_specs=(
            P(None, "wide", "narrow", None),
            P("wide", "narrow", None),
            P("wide", "narrow", None),
        ),
        check_vma=False,
    )
```

```python
import functools

import jax
import jax.numpy as jnp
import ml_dtypes
import numpy as np
from jax import lax
from jax.experimental import pallas as pl
from jax.experimental.pallas import tpu as pltpu
from jax.sharding import PartitionSpec as P

MESH = pl.DeviceIdType.MESH
SHIFT = 4.0
SIDES = ((1, 0), (-1, 0), (0, 1), (0, -1), (1, 1), (1, -1), (-1, 1), (-1, -1))
FAR = ((2, 0), (-2, 0), (2, 1), (2, -1), (-2, 1), (-2, -1))


def legendre_pair(order, nodes):
    p_prev = np.ones(nodes.shape)
    p_now = nodes * 1.0
    for k in range(2, order + 1):
        p_next = ((2 * k - 1) * nodes * p_now - (k - 1) * p_prev) / k
        p_prev = p_now
        p_now = p_next
    return (p_now, p_prev)


def spectral_tables():
    degree = 7
    points = degree + 1
    gll_nodes = np.cos(np.pi * np.arange(points) / degree)
    for sweep in range(100):
        p_now, p_prev = legendre_pair(degree, gll_nodes)
        gll_nodes = gll_nodes - (gll_nodes * p_now - p_prev) / ((degree + 1) * p_now)
    gll_nodes = np.sort(gll_nodes)
    legendre_vals, unused_prev = legendre_pair(degree, gll_nodes)
    gll_weights = 2.0 / (degree * (degree + 1) * legendre_vals**2)
    derivative = np.zeros((points, points))
    for row_index in range(points):
        for col_index in range(points):
            if row_index != col_index:
                derivative[row_index, col_index] = legendre_vals[row_index] / (
                    legendre_vals[col_index] * (gll_nodes[row_index] - gll_nodes[col_index])
                )
    derivative[0, 0] = -degree * (degree + 1) / 4.0
    derivative[-1, -1] = degree * (degree + 1) / 4.0
    gauss_nodes = np.cos(np.pi * (np.arange(12) + 0.75) / 12.5)
    for sweep in range(100):
        p_now, p_prev = legendre_pair(12, gauss_nodes)
        slope = 12 * (gauss_nodes * p_now - p_prev) / (gauss_nodes * gauss_nodes - 1.0)
        gauss_nodes = gauss_nodes - p_now / slope
    gauss_nodes = np.sort(gauss_nodes)
    p_now, p_prev = legendre_pair(12, gauss_nodes)
    slope = 12 * (gauss_nodes * p_now - p_prev) / (gauss_nodes * gauss_nodes - 1.0)
    gauss_weights = 2.0 / ((1.0 - gauss_nodes**2) * slope**2)
    interpolate = np.ones((12, points))
    for col_index in range(points):
        for other in range(points):
            if other != col_index:
                interpolate[:, col_index] *= (gauss_nodes - gll_nodes[other]) / (
                    gll_nodes[col_index] - gll_nodes[other]
                )
    return (gll_weights, derivative, gauss_weights, interpolate)


def halves(matrix):
    high = matrix.astype(ml_dtypes.bfloat16)
    low = (matrix - high.astype(np.float64)).astype(ml_dtypes.bfloat16)
    return high, low


def left_factor(matrix):
    high, low = halves(matrix)
    return np.concatenate([high, high, low], axis=1)


def right_factor(matrix):
    high, low = halves(matrix)
    return np.concatenate([high, high, low], axis=0)


def tables_for(len_z):
    weights, deriv, fine_weights, interp = spectral_tables()
    els_z = len_z // 8
    gradint = interp @ deriv
    stiff = deriv.T @ np.diag(weights) @ deriv
    eye2, eye_z = np.eye(2), np.eye(els_z)

    def shared(count):
        total = np.eye(8 * count)
        for k in range(count - 1):
            total[8 * k + 7, 8 * k + 8] = total[8 * k + 8, 8 * k + 7] = 1.0
        return total

    sum_y, sum_z = shared(2), shared(els_z)
    w_x, w_y, w_z = weights, np.tile(weights, 2), np.tile(weights, els_z)
    w_y2, w_z2 = sum_y @ w_y, sum_z @ w_z

    fine_z = np.zeros((len_z, 2 * 16 * els_z))
    back_z = np.zeros((16 * els_z, len_z))
    for e in range(els_z):
        fine_z[8 * e : 8 * e + 8, 16 * e : 16 * e + 12] = interp.T
        first = 16 * els_z + 16 * e
        fine_z[8 * e : 8 * e + 8, first : first + 12] = gradint.T
        back_z[16 * e : 16 * e + 12, 8 * e : 8 * e + 8] = fine_weights[:, None] * interp
    back_z = back_z @ sum_z
    fine_xy = np.concatenate(
        [np.kron(interp, interp), np.kron(gradint, interp), np.kron(interp, gradint)], axis=0
    )
    back = interp.T * fine_weights[None, :]
    back_xy = np.kron(back, back)

    op_xy = np.kron(stiff, np.diag(w_y2)) + np.kron(np.diag(w_x), sum_y @ np.kron(eye2, stiff))
    op_apart = np.concatenate(
        [np.kron(stiff, np.eye(16)), np.kron(np.eye(8), sum_y @ np.kron(eye2, stiff))], axis=0
    )
    op_z = np.kron(eye_z, stiff).T @ sum_z
    weak = np.diag(weights) @ deriv
    div_xy = np.concatenate(
        [np.kron(weak, np.diag(w_y)), np.kron(np.diag(w_x), np.kron(eye2, weak))], axis=1
    )
    div_x = np.kron(weak, np.eye(16))
    div_y = np.kron(np.eye(8), sum_y @ np.kron(eye2, weak))
    div_z = np.kron(eye_z, weak).T
    div_z2 = div_z @ sum_z

    w_xy, w_xy2 = np.kron(w_x, w_y), np.kron(w_x, w_y2)
    half_y = 1.0 / (sum_y @ np.ones(16))
    half_z = 1.0 / (sum_z @ np.ones(len_z))
    ones_x, ones_z = np.ones(8), np.ones(len_z)
    plain = np.stack(
        [
            np.outer(w_xy, w_z),
            np.outer(w_xy, ones_z),
            np.outer(w_xy2, ones_z),
            1.0 / np.outer(w_xy2, w_z2),
            np.outer(np.kron(ones_x, half_y), half_z),
            np.outer(np.ones(128), w_z),
            np.outer(np.ones(128), w_z2),
            np.outer(np.tile(np.concatenate([stiff[0], stiff[7]]), 8), ones_z),
            np.outer(np.kron(w_x, np.ones(16)), w_z2),
            np.outer(np.kron(ones_x, w_y2), w_z2),
            np.outer(np.tile(np.concatenate([weak[0], weak[7]]), 8) / np.kron(ones_x, w_y2), ones_z),
        ]
    ).astype(np.float32)
    from_right = np.concatenate(
        [right_factor(back_z), right_factor(op_z), right_factor(div_z), right_factor(div_z2)], axis=0
    )
    from_left = np.zeros((256, 2304), ml_dtypes.bfloat16)
    from_left[:128, :384] = left_factor(op_xy)
    from_left[:128, 384:1152] = left_factor(div_xy)
    from_left[:128, 1152:1536] = left_factor(div_x)
    from_left[:128, 1536:1920] = left_factor(div_y)
    from_left[:, 1920:] = left_factor(op_apart)
    shapes_xy = np.zeros((496, 432), ml_dtypes.bfloat16)
    shapes_xy[:432, :192] = left_factor(fine_xy)
    shapes_xy[432:] = left_factor(back_xy)
    return (
        right_factor(fine_z),
        shapes_xy,
        from_right,
        from_left,
        plain,
    )


def split(value):
    high = value.astype(jnp.bfloat16)
    low = (value - high.astype(jnp.float32)).astype(jnp.bfloat16)
    return high, low


def stacked(value):
    high, low = split(value)
    return jnp.concatenate([high, low, high], axis=0)


def joined(value):
    high, low = split(value)
    return jnp.concatenate([high, low, high], axis=1)


def mul(first, second):
    return jnp.dot(first, second, preferred_element_type=jnp.float32)


def kernel(
    sizes,
    vel_hbm,
    rea_hbm,
    fine_z_hbm,
    fine_xy_hbm,
    right_hbm,
    left_hbm,
    plain_hbm,
    adv_ref,
    pres_ref,
    resid_ref,
    vel_ref,
    rea_ref,
    fine_z_ref,
    fine_xy_ref,
    right_ref,
    left_ref,
    plain_ref,
    load_sem,
    adv_q,
    ops_q,
    sx3,
    sy3,
    sc3,
    rx3,
    ry3,
    rc3,
    sx1,
    sy1,
    sc1,
    rx1,
    ry1,
    rc1,
    part,
    got,
    send_sem,
    recv_sem,
    tree_send,
    tree_recv,
    word,
    mass_q,
    local_mass,
    lines_q,
    sums_x,
    sums_y,
    far_x,
    far_c,
    inverse_q,
):
    pairs = (
        (vel_hbm, vel_ref),
        (fine_z_hbm, fine_z_ref),
        (fine_xy_hbm, fine_xy_ref),
        (right_hbm, right_ref),
        (plain_hbm, plain_ref),
        (rea_hbm, rea_ref),
        (left_hbm, left_ref),
    )
    loads = [pltpu.make_async_copy(a, b, load_sem.at[k]) for k, (a, b) in enumerate(pairs)]
    for load in loads:
        load.start()

    count_x, count_y, low_count = sizes
    weights, deriv = spectral_tables()[:2]
    stiff = [[float(v) for v in row] for row in deriv.T @ np.diag(weights) @ deriv]
    slope = [[float(v) for v in row] for row in np.diag(weights) @ deriv @ np.diag(1.0 / weights)]
    thick = float(2.0 * weights[0])
    high_count = count_x // low_count
    me_x, me_y = lax.axis_index("wide"), lax.axis_index("narrow")
    me_low, me_high = lax.rem(me_x, low_count), me_x // low_count
    me_pair, me_core = me_y // 2, lax.rem(me_y, 2)

    def turn(place, step, count):
        moved = place + step % count
        return jnp.where(moved >= count, moved - count, moved)

    def at_side(side):
        return turn(me_x, side[0], count_x), turn(me_y, side[1], count_y)

    def far_first(count_a, count_b):
        hops = lambda step, count: min(step, count - step)
        steps = [(i, j) for i in range(count_a) for j in range(count_b) if (i, j) != (0, 0)]
        return sorted(steps, key=lambda s: -hops(s[0], count_a) - hops(s[1], count_b))

    def by_z(step):
        return me_high * low_count + turn(me_low, step, low_count), me_y

    def by_y(step):
        return turn(me_high, step, high_count) * low_count + me_low, me_y

    def by_pair(step):
        return me_x, turn(me_pair, step, count_y // 2) * 2 + me_core

    near = [by_z(1), by_z(-1), by_y(1), by_y(-1), by_pair(1), by_pair(-1)]
    rounds = (
        near[:4],
        [by_z(2), by_z(-2), by_y(2), by_y(-2)],
        [by_z(2), by_z(-2)] + near[4:],
        near[4:] + [(me_x, me_pair * 2 + 1 - me_core)],
    )
    partners = [at_side(side) for side in FAR + SIDES] + near

    barrier = pltpu.get_barrier_semaphore()
    for who in partners:
        pl.semaphore_signal(barrier, inc=1, device_id=who, device_id_type=MESH)

    def vouch(index):
        for who in rounds[index]:
            pl.semaphore_signal(word.at[index], inc=1, device_id=who, device_id_type=MESH)

    def hear(index):
        pl.semaphore_wait(word.at[index], len(rounds[index]))

    for load in loads[:3]:
        load.wait()
    parts = []
    for c in range(3):
        for e in range(2):
            parts.append(vel_ref[c, :, 8 * e : 8 * e + 8, :].reshape(64, 128))
    on_z = mul(joined(jnp.concatenate(parts, axis=0)), fine_z_ref[...])
    width = on_z.shape[1] // 2
    products = {}
    for e in range(2):
        fine = []
        for c in range(3):
            first = 64 * (2 * c + e)
            flat = mul(fine_xy_ref[:432, :192], stacked(on_z[first : first + 64, :width]))
            steep = mul(fine_xy_ref[:144, :192], stacked(on_z[first : first + 64, width:]))
            fine.append((flat[:144], flat[144:288], flat[288:], steep))
        for c in range(3):
            products[c, e] = (
                fine[0][0] * fine[c][1] + fine[1][0] * fine[c][2] + fine[2][0] * fine[c][3]
            )
    for load in loads[3:4]:
        load.wait()
    row8 = lax.broadcasted_iota(jnp.int32, (8, 8, 128), 1)
    back_rows = 3 * width
    for c in range(3):
        both = []
        for e in range(2):
            both.append(stacked(mul(joined(products[c, e]), right_ref[:back_rows, :])))
        weak = mul(fine_xy_ref[432:, :], jnp.concatenate(both, axis=1))
        first = weak[:, :128].reshape(8, 8, 128)
        second = weak[:, 128:].reshape(8, 8, 128)
        first, second = (
            first + jnp.where(row8 == 7, pltpu.roll(second, 7, 1), 0.0),
            second + jnp.where(row8 == 0, pltpu.roll(first, 1, 1), 0.0),
        )
        adv_q[c] = jnp.concatenate([first, second], axis=1).reshape(128, 128)

    pl.semaphore_wait(barrier, len(partners))

    has = {1: (me_x > 0, me_y > 0), -1: (me_x < count_x - 1, me_y < count_y - 1)}
    for load in loads[4:]:
        load.wait()

    rows = lax.broadcasted_iota(jnp.int32, (128, 128), 0)
    in_x, in_y = rows // 16, lax.rem(rows, 16)
    lane = lax.broadcasted_iota(jnp.int32, (128, 128), 1)
    in_z = lax.rem(lane, 8)
    cross_x = ((in_x == 0) & has[1][0]) | ((in_x == 7) & has[-1][0])
    cross_y = ((in_y == 0) & has[1][1]) | ((in_y == 15) & has[-1][1])
    cross = jnp.where(cross_x, 0.5, 1.0) * jnp.where(cross_y, 0.5, 1.0)
    twice_x, twice_y = jnp.where(cross_x, 2.0, 1.0), jnp.where(cross_y, 2.0, 1.0)
    scale_y = plain_ref[8] * twice_x
    scale_x = plain_ref[9] * twice_y
    scale_z = plain_ref[2] * twice_x * twice_y

    def pack(q, bufs, c):
        sx, sy, sc = bufs[:3]
        sx[0, c] = q[112:128, :]
        sx[1, c] = q[0:16, :]
        sy[0, c] = q[pl.ds(15, 8, stride=16), :]
        sy[1, c] = q[pl.ds(0, 8, stride=16), :]
        for k, row in enumerate((127, 112, 15, 0)):
            sc[k, c : c + 1, :] = q[row : row + 1, :]

    def attach(bufs, c, k, face):
        sx, sy, sc = bufs[:3]
        sx[k, c] = face
        sc[2 * k, c + 1 : c + 2, :] = face[15:16]
        sc[2 * k + 1, c + 1 : c + 2, :] = face[0:1]
        line = lines_q[pl.ds(1 - k, 8, stride=2), :]
        sy[k, c] = line
        sc[k, c : c + 1, :] = line[7:8]
        sc[2 + k, c : c + 1, :] = line[0:1]

    def launch(bufs, index, comps, far=None):
        sx, sy, sc, rx, ry, rc = bufs
        used = pl.ds(0, comps)
        moves = []
        if far is not None:
            for k in range(4):
                moves.append((FAR[2 + k], sc.at[k], far_c.at[far, k]))
        for k in range(4):
            moves.append((SIDES[4 + k], sc.at[k], rc.at[k]))
        if far is not None:
            for k in range(2):
                moves.append((FAR[k], sx.at[k, 0], far_x.at[far, k]))
        for k in range(2):
            moves.append((SIDES[k], sx.at[k, used], rx.at[k, used]))
        for k in range(2):
            moves.append((SIDES[2 + k], sy.at[k, used], ry.at[k, used]))
        copies = []
        for k, (side, source, target) in enumerate(moves):
            copy = pltpu.make_async_remote_copy(
                src_ref=source,
                dst_ref=target,
                send_sem=send_sem.at[index, k],
                recv_sem=recv_sem.at[index, k],
                device_id=at_side(side),
                device_id_type=MESH,
            )
            copy.start()
            copies.append(copy)
        return copies

    row_x = lax.broadcasted_iota(jnp.int32, (8, 128), 0)

    def side_line(bufs, k, c):
        ry, rc = bufs[4], bufs[5]
        low = jnp.where(has[1][0], rc[k, c : c + 1, :], 0.0)
        high = jnp.where(has[-1][0], rc[2 + k, c : c + 1, :], 0.0)
        return ry[k, c] + jnp.where(row_x == 0, low, 0.0) + jnp.where(row_x == 7, high, 0.0)

    ends_y = ((pl.ds(0, 8, stride=16), has[1][1]), (pl.ds(15, 8, stride=16), has[-1][1]))

    row_y = lax.broadcasted_iota(jnp.int32, (16, 128), 0)

    def side_face(face, corner, k, row):
        low = jnp.where(has[1][1], corner[2 * k, row : row + 1, :], 0.0)
        high = jnp.where(has[-1][1], corner[2 * k + 1, row : row + 1, :], 0.0)
        return face + jnp.where(row_y == 0, low, 0.0) + jnp.where(row_y == 15, high, 0.0)

    ends_x = ((slice(0, 16), has[1][0]), (slice(112, 128), has[-1][0]))

    def receive(fields, bufs, copies):
        rx = bufs[3]
        for copy in copies:
            copy.wait_recv()
        for c, q in enumerate(fields):
            for k, (rows, there) in enumerate(ends_x):
                q[rows, :] = q[rows, :] + jnp.where(there, rx[k, c], 0.0)
            for k, (rows, there) in enumerate(ends_y):
                q[rows, :] = q[rows, :] + jnp.where(there, side_line(bufs, k, c), 0.0)

    three = (sx3, sy3, sc3, rx3, ry3, rc3)
    ones = [tuple(buf.at[k] for buf in (sx1, sy1, sc1, rx1, ry1, rc1)) for k in range(3)]
    for c in range(3):
        pack(adv_q.at[c], three, c)
    lines_q[...] = jnp.sum(
        (adv_q[1] * plain_ref[10] * jnp.where(cross_y, 0.5, 1.0)).reshape(16, 8, 128), axis=1
    )
    outer = (jnp.where(has[1][0], 0.5, 1.0), jnp.where(has[-1][0], 0.5, 1.0))
    for k, end in ((0, 7), (1, 0)):
        face = (slope[end][0] * outer[0]) * adv_q[0, 0:16, :]
        face = face + (slope[end][7] * outer[1]) * adv_q[0, 112:128, :]
        for i in range(1, 7):
            face = face + slope[end][i] * adv_q[0, 16 * i : 16 * i + 16, :]
        attach(three, 3, k, face)
    copies = launch(three, 0, 4, far=0)
    vouch(0)
    flights = list(copies)

    local_half = plain_ref[4]
    inverse_mult = cross * local_half
    inverse_mass = plain_ref[3] * cross

    def sum_yz(value):
        up = pltpu.roll(value, 1, 1)
        down = pltpu.roll(value, 127, 1)
        value = value + jnp.where((in_z == 0) & (lane > 0), up, 0.0)
        value = value + jnp.where((in_z == 7) & (lane < 127), down, 0.0)
        up = pltpu.roll(value, 1, 0)
        down = pltpu.roll(value, 127, 0)
        return value + jnp.where(in_y == 8, up, 0.0) + jnp.where(in_y == 7, down, 0.0)

    mass_q[...] = sum_yz(plain_ref[0] * rea_ref[...].reshape(128, 128)) - SHIFT * cross
    vel = [vel_ref[c].reshape(128, 128) for c in range(3)]
    local_mass[...] = mass_q[...]
    op_xy, div_xy = slice(0, 384), slice(384, 1152)
    div_x, div_y = slice(1152, 1536), slice(1536, 1920)
    op_apart = slice(1920, 2304)
    op_z, div_z, div_z2 = (slice(back_rows + 384 * k, back_rows + 384 * k + 384) for k in range(3))

    def divergence(field, on_xy, on_z, scale_z, scale_xy):
        flat = mul(left_ref[:128, on_xy], stacked(jnp.concatenate(field[:2], axis=0)))
        return scale_z * flat + scale_xy * mul(joined(field[2]), right_ref[on_z, :])

    base = sum_yz(divergence(vel, div_xy, div_z, plain_ref[5], plain_ref[1]))

    def operate(value):
        flat = mul(left_ref[:128, op_xy], stacked(value))
        along = mul(joined(value), right_ref[op_z, :])
        return plain_ref[6] * flat + plain_ref[2] * along + local_mass[...] * value

    ops_q[0] = base
    pack(ops_q.at[0], ones[0], 0)
    pack(mass_q, ones[0], 1)
    later = launch(ones[0], 1, 2)
    flights += later
    hear(0)
    vouch(1)
    inverse_q[...] = inverse_mass
    two = (me_x > 1, me_x < count_x - 2)
    receive([adv_q.at[c] for c in range(3)], three, copies)
    adv = []
    for c in range(3):
        adv.append(adv_q[c] * inverse_mass)
    sums_x[...] = mul(left_ref[:128, div_x], stacked(adv[0]))
    sums_y[...] = mul(left_ref[:128, div_y], stacked(adv[1]))
    along = mul(joined(adv[2]), right_ref[div_z2, :])
    rx, ry, rc = three[3:]
    for k, (rows_k, there) in enumerate(ends_x):
        near_end, far_end = 7 - 7 * k, 7 * k
        mine = adv_q[0, rows_k, :] - side_face(rx[k, 0], rc, k, 0)
        other = jnp.where(two[k], side_face(far_x[0, k], far_c[0], k, 0), 0.0)
        face = side_face(rx[k, 3], rc, k, 4)
        face = face + (0.5 * slope[near_end][near_end]) * mine
        face = face + (0.5 * slope[near_end][far_end]) * other
        face = face * (thick * inverse_q[rows_k, :])
        sums_x[rows_k, :] = sums_x[rows_k, :] + jnp.where(there, face, 0.0)
    for k, (rows_k, there) in enumerate(ends_y):
        near_end = 7 - 7 * k
        mine = adv_q[1, rows_k, :] - side_line(three, k, 1)
        line = side_line(three, k, 3) + (0.5 * slope[near_end][near_end]) * mine
        line = line * (thick * inverse_q[rows_k, :])
        sums_y[rows_k, :] = sums_y[rows_k, :] + jnp.where(there, line, 0.0)
    receive([ops_q.at[0], mass_q], ones[0], later)
    hear(1)
    vouch(2)
    z0 = 0.05 * (scale_x * sums_x[...] + scale_y * sums_y[...] + scale_z * along) - ops_q[0]

    def dot(first, second, scale):
        return jnp.sum(first * second * scale, axis=0, keepdims=True)

    image = operate(z0)
    ops_q[1] = image
    pack(ops_q.at[1], ones[1], 0)
    lines_q[...] = jnp.sum((image * plain_ref[7]).reshape(16, 8, 128), axis=1)
    for k, end in ((0, 7), (1, 0)):
        face = stiff[end][0] * image[0:16]
        for i in range(1, 8):
            face = face + stiff[end][i] * image[16 * i : 16 * i + 16]
        attach(ones[1], 1, k, face)
    copies = launch(ones[1], 2, 2, far=1)
    stages = (
        [
            (me_high * low_count + turn(me_low, i, low_count), me_pair * 2 + turn(me_core, j, 2))
            for i, j in far_first(low_count, 2)
        ],
        [
            (
                turn(me_high, i, high_count) * low_count + me_low,
                turn(me_pair, j, count_y // 2) * 2 + me_core,
            )
            for i, j in far_first(high_count, count_y // 2)
        ],
    )
    flights += copies
    hear(2)
    vouch(3)
    for c in range(3):
        adv_ref[c] = adv[c].reshape(8, 16, 128)
    part[0, 0:1, :] = dot(z0, z0, inverse_mult)
    part[0, 6:8, :] = jnp.zeros((2, 128), jnp.float32)
    receive([ops_q.at[1]], ones[1], copies)
    hear(3)
    z1 = ops_q[1]
    rx, ry, rc = ones[1][3:]
    apart = mul(left_ref[:, op_apart], stacked(z1))
    along = mul(joined(z1), right_ref[op_z, :])
    sums_x[...] = apart[:128]
    sums_y[...] = apart[128:]
    for k, (rows_k, there) in enumerate(ends_x):
        mine = ops_q[1, rows_k, :] - side_face(rx[k, 0], rc, k, 0)
        other = jnp.where(two[k], side_face(far_x[1, k], far_c[1], k, 0), 0.0)
        face = side_face(rx[k, 1], rc, k, 2) + stiff[7][7] * mine + stiff[7][0] * other
        sums_x[rows_k, :] = sums_x[rows_k, :] + jnp.where(there, face, 0.0)
    for k, (rows_k, there) in enumerate(ends_y):
        mine = ops_q[1, rows_k, :] - side_line(ones[1], k, 0)
        line = side_line(ones[1], k, 1) + stiff[7][7] * mine
        sums_y[rows_k, :] = sums_y[rows_k, :] + jnp.where(there, line, 0.0)
    z2 = scale_x * sums_x[...] + scale_y * sums_y[...] + scale_z * along + mass_q[...] * z1
    ops_q[2] = z2
    part[0, 1:2, :] = dot(z0, z1, inverse_mult)
    part[0, 2:3, :] = dot(z1, z1, inverse_mult)
    last = operate(z2)
    part[0, 3:4, :] = dot(z1, z2, inverse_mult)
    part[0, 4:5, :] = dot(z2, z2, inverse_mult)
    part[0, 5:6, :] = dot(z2, last, local_half)

    slot = 0
    for index, stage in enumerate(stages):
        copies_in = []
        for k, who in enumerate(stage):
            copies_in.append(
                pltpu.make_async_remote_copy(
                    src_ref=part.at[index],
                    dst_ref=got.at[slot + k],
                    send_sem=tree_send.at[slot + k],
                    recv_sem=tree_recv.at[slot + k],
                    device_id=who,
                    device_id_type=MESH,
                )
            )
        for copy in copies_in:
            copy.start()
        if index == 0:
            ops_q[3] = last
            pack(ops_q.at[3], ones[2], 0)
            copies = launch(ones[2], 3, 1)
            flights += copies
        for copy in copies_in:
            copy.wait_recv()
        total = part[index]
        for k in range(len(stage)):
            total = total + got[slot + k]
        if index < 1:
            part[index + 1] = total
        flights += copies_in
        slot += len(stage)

    receive([ops_q.at[3]], ones[2], copies)
    sums = jnp.broadcast_to(jnp.sum(total, axis=1, keepdims=True), (8, 128))
    g00, g01, g11, g12, g22, g23 = (sums[k : k + 1, :] for k in range(6))
    h00 = g01 + SHIFT * g00
    h01 = g11 + SHIFT * g01
    h11 = g12 + SHIFT * g11
    h02 = g12 + SHIFT * g11
    h12 = g22 + SHIFT * g12
    h22 = g23 + SHIFT * g22
    over = 1.0 / h00
    l10, l20 = h01 * over, h02 * over
    d1 = h11 - l10 * h01
    e1 = h12 - l10 * h02
    over1 = 1.0 / d1
    l21 = e1 * over1
    d2 = h22 - l20 * h02 - l21 * e1
    b1 = g01 - l10 * g00
    b2 = g11 - l20 * g00 - l21 * b1
    c2 = b2 / d2
    c1 = b1 * over1 - l21 * c2
    c0 = g00 * over - l10 * c1 - l20 * c2
    z3 = ops_q[3]
    pres = c0 * z0 + c1 * z1 + c2 * z2
    pres_ref[...] = pres.reshape(8, 16, 128)
    resid = (
        (1.0 - SHIFT * c0) * z0 - (c0 + SHIFT * c1) * z1 - (c1 + SHIFT * c2) * z2 - c2 * z3
    )
    resid_ref[...] = resid.reshape(8, 16, 128)
    for copy in flights:
        copy.wait_send()


def store(*refs):
    sources, targets, sems = refs[:3], refs[3:6], refs[6]
    copies = [
        pltpu.make_async_copy(a, b, sems.at[k]) for k, (a, b) in enumerate(zip(sources, targets))
    ]
    for copy in copies:
        copy.start()
    for copy in copies:
        copy.wait()


def per_device(sizes, velocity, reaction):
    consts = [jnp.asarray(value) for value in tables_for(reaction.shape[2])]
    operands = [velocity, reaction] + consts
    shape_of = jax.ShapeDtypeStruct
    count_x, count_y, low_count = sizes
    trips = (2 * low_count - 1) + (count_x // low_count * count_y // 2 - 1)
    vmem, f32, dma = pltpu.VMEM, jnp.float32, pltpu.SemaphoreType.DMA
    results = pl.pallas_call(
        functools.partial(kernel, sizes),
        out_shape=(
            shape_of(velocity.shape, f32),
            shape_of(reaction.shape, f32),
            shape_of(reaction.shape, f32),
        ),
        in_specs=[pl.BlockSpec(memory_space=pltpu.HBM)] * 7,
        out_specs=(pl.BlockSpec(memory_space=vmem),) * 3,
        scratch_shapes=[vmem(value.shape, value.dtype) for value in operands]
        + [
            dma((7,)),
            vmem((3, 128, 128), f32),
            vmem((4, 128, 128), f32),
            vmem((2, 4, 16, 128), f32),
            vmem((2, 4, 8, 128), f32),
            vmem((4, 8, 128), f32),
            vmem((2, 4, 16, 128), f32),
            vmem((2, 4, 8, 128), f32),
            vmem((4, 8, 128), f32),
            vmem((3, 2, 2, 16, 128), f32),
            vmem((3, 2, 2, 8, 128), f32),
            vmem((3, 4, 8, 128), f32),
            vmem((3, 2, 2, 16, 128), f32),
            vmem((3, 2, 2, 8, 128), f32),
            vmem((3, 4, 8, 128), f32),
            vmem((2, 8, 128), f32),
            vmem((trips, 8, 128), f32),
            dma((4, 14)),
            dma((4, 14)),
            dma((trips,)),
            dma((trips,)),
            pltpu.SemaphoreType.REGULAR((4,)),
            vmem((128, 128), f32),
            vmem((128, 128), f32),
            vmem((16, 128), f32),
            vmem((128, 128), f32),
            vmem((128, 128), f32),
            vmem((2, 2, 16, 128), f32),
            vmem((2, 4, 8, 128), f32),
            vmem((128, 128), f32),
        ],
        compiler_params=pltpu.CompilerParams(
            collective_id=0, has_side_effects=True, vmem_limit_bytes=54700 * 1024
        ),
    )(*operands)
    return pl.pallas_call(
        store,
        out_shape=tuple(shape_of(value.shape, f32) for value in results),
        in_specs=[pl.BlockSpec(memory_space=vmem)] * 3,
        out_specs=(pl.BlockSpec(memory_space=pltpu.HBM),) * 3,
        scratch_shapes=[dma((3,))],
        compiler_params=pltpu.CompilerParams(vmem_limit_bytes=1024 * 1024),
    )(*results)


def solution(mesh):
    count_x, count_y = mesh.shape["wide"], mesh.shape["narrow"]
    low_count = 12 if count_x % 12 == 0 else 2
    return jax.shard_map(
        functools.partial(per_device, (count_x, count_y, low_count)),
        mesh=mesh,
        in_specs=(P(None, "wide", "narrow", None), P("wide", "narrow", None)),
        out_specs=(
            P(None, "wide", "narrow", None),
            P("wide", "narrow", None),
            P("wide", "narrow", None),
        ),
        check_vma=False,
    )
```
